32 devices in a mesh: dp: 4 (over z), ctx: 8 (over y, x, core).
Axes of the slice: x: 2, y: 2, z: 4, core: 2. Of those that a mesh axis runs over, the one named last changes fastest.
Arguments:
- queries: bfloat16 [8192, 1024], P(('dp', 'ctx')), may hold values from -27 to 27, as said below
- keys: bfloat16 [8192, 128], P(('dp', 'ctx')), may hold values from -4 to 4, as said below
- values: bfloat16 [8192, 128], P(('dp', 'ctx')), may hold values from -6 to 6
- grad_out: bfloat16 [8192, 1024], P(('dp', 'ctx')), may hold values from -6 to 6
- lengths: int32 [16], replicated, may hold values from 1 to 2048, 8192 in all
Outputs:
- attn_out: bfloat16 [8192, 1024], P(('dp', 'ctx'))
- grad_queries: bfloat16 [8192, 1024], P(('dp', 'ctx'))
- grad_keys: bfloat16 [8192, 128], P(('dp', 'ctx'))
- grad_values: bfloat16 [8192, 128], P(('dp', 'ctx'))
The draws below stay inside these ranges and needn't reach their ends.
Inputs may be any that keep to these rules, and one draw needn't show every extreme that they name: `queries`: query entries lie in this range. `keys`: key entries lie in this range.
All inputs are finite; a program needn't handle non-finite values.
Results may differ from the reference program's by a relative error of at most 0.029.
Values may be sent and summed in bfloat16 or wider, within the bound.
No kernel may reach another device: no remote copies, remote signals or barrier semaphores. Data moves between devices by JAX's collectives and lax.ppermute only.
A program may use at most 192 MiB of HBM per device.

```python
import math
import jax
import jax.numpy as jnp
import numpy as np
from jax import lax

HEADS = 8
HDIM = 128
T_DEV = 256
WIN = 8
MAXLEN = 2048
TOKENS = 8192
NDOCS = 16


def draw_queries(key, part):
    normal_rows = jax.random.normal(jax.random.fold_in(key, 201), (TOKENS, HEADS * HDIM), jnp.float32)
    return jnp.clip(normal_rows, -6.0, 6.0).astype(jnp.bfloat16)


def draw_keys(key, part):
    normal_rows = jax.random.normal(jax.random.fold_in(key, 202), (TOKENS, HDIM), jnp.float32)
    return jnp.clip(normal_rows, -4.0, 4.0).astype(jnp.bfloat16)


def steps_of(rng, dims, cuts, least, largest):
    factor_of, own = 1.0, jax.random.fold_in(rng, 6)
    for dim, shards_of in cuts:
        steps = jnp.exp(jax.random.uniform(jax.random.fold_in(own, dim), (shards_of,), jnp.float32, least / len(cuts), largest / len(cuts)))
        factor_of = factor_of * jnp.repeat(steps, dims[dim] // shards_of).reshape([-1 if axis == dim else 1 for axis in range(len(dims))])
    return factor_of


def profile(amount, total, limit, lean):
    portions = [(1 << 20) // math.isqrt(grade ** lean) + 1 for grade in range(2, amount + 1)]
    rest, given = total - limit - (amount - 1), [1] * (amount - 1)
    while rest > 0:
        candidates = [i for i in range(amount - 1) if given[i] < limit]
        whole, budget = sum([portions[i] for i in candidates]), rest
        for i in candidates:
            more = min(limit - given[i], max(1, budget * portions[i] // whole), rest)
            given[i] = given[i] + more
            rest = rest - more
    return np.array([limit] + given)


def uneven(stream_key, amount, total, reach, slope):
    if amount == 2:
        one = jax.random.randint(stream_key, (), max(1, total - reach), min(reach, total - 1) + 1)
        return jnp.stack([one, total - one])
    tallies = jnp.asarray(profile(amount, total, reach, slope), jnp.int32)
    couples = (amount - 1) // 2
    donor, taker = tallies[1:1 + 2 * couples:2], tallies[2:2 + 2 * couples:2]
    room = jnp.minimum(donor - 1, reach - taker)
    moved = jax.random.randint(jax.random.fold_in(stream_key, 1), (couples,), 0, 1 << 20) % (room + 1)
    tallies = tallies.at[1:1 + 2 * couples:2].set(donor - moved).at[2:2 + 2 * couples:2].set(taker + moved)
    return tallies[jax.random.permutation(jax.random.fold_in(stream_key, 2), amount)]


def scatter_about(rng, extent, width, limit, shards=(), held_as=jnp.bfloat16):
    result = width * jax.random.normal(rng, extent, jnp.float32)
    if shards:
        result = result * steps_of(rng, extent, shards, -0.22, 0.18)
    return jnp.clip(result, -limit, limit).astype(held_as)


def setup_inputs(seed: int = 0) -> dict:
    arg_keys = jax.random.split(jax.random.key(seed), 6)
    queries = draw_queries(jax.random.fold_in(arg_keys[5], 71), 0)
    keys = draw_keys(jax.random.fold_in(arg_keys[5], 71), 0)
    values = scatter_about(arg_keys[2], (TOKENS, HDIM), 1.0, 6.0, ((0, 32),))
    grad_out = scatter_about(arg_keys[3], (TOKENS, HEADS * HDIM), 1.0, 6.0, ((0, 32),))
    lengths = uneven(arg_keys[4], NDOCS, TOKENS, MAXLEN, 2).astype(jnp.int32)
    return {"queries": queries, "keys": keys, "values": values, "grad_out": grad_out, "lengths": lengths}


NEG_FILL = -1e30


def reference(queries, keys, values, grad_out, lengths):
    rows = T_DEV
    span = (WIN + 1) * rows
    margin = WIN * rows
    scale = float(HDIM) ** -0.5
    ends = jnp.cumsum(lengths).astype(jnp.int32)
    position = jnp.arange(TOKENS, dtype=jnp.int32)
    doc_ids = jnp.sum((ends[None, :] <= position[:, None]).astype(jnp.int32), axis=1).astype(jnp.int32)
    keys_pad = jnp.concatenate([jnp.zeros((margin, HDIM), keys.dtype), keys], axis=0)
    values_pad = jnp.concatenate([jnp.zeros((margin, HDIM), values.dtype), values], axis=0)
    docs_pad = jnp.concatenate([jnp.full((margin,), -1, jnp.int32), doc_ids], axis=0)

    def step(carry, block):
        key_acc, value_acc = carry
        start = (block * rows).astype(jnp.int32)
        query_flat = lax.dynamic_slice_in_dim(queries, start, rows, 0).reshape(rows * HEADS, HDIM)
        grad_flat = lax.dynamic_slice_in_dim(grad_out, start, rows, 0).reshape(rows * HEADS, HDIM)
        key_win = lax.dynamic_slice_in_dim(keys_pad, start, span, 0)
        value_win = lax.dynamic_slice_in_dim(values_pad, start, span, 0)
        query_doc = lax.dynamic_slice_in_dim(doc_ids, start, rows, 0)
        key_doc = lax.dynamic_slice_in_dim(docs_pad, start, span, 0)
        query_pos = start + jnp.arange(rows, dtype=jnp.int32)
        key_pos = start - margin + jnp.arange(span, dtype=jnp.int32)
        allowed = ((query_doc[:, None] == key_doc[None, :]) & (key_pos[None, :] <= query_pos[:, None]))[:, None, :]
        scores = (jnp.dot(query_flat, key_win.T, preferred_element_type=jnp.float32) * scale).reshape(rows, HEADS, span)
        row_max = jnp.max(jnp.where(allowed, scores, NEG_FILL), axis=-1)
        row_total = jnp.sum(jnp.where(allowed, jnp.exp(scores - row_max[..., None]), 0.0), axis=-1)
        logsum = row_max + jnp.log(row_total)
        probs = jnp.where(allowed, jnp.exp(scores - logsum[..., None]), 0.0)
        prob_half = probs.astype(jnp.bfloat16).reshape(rows * HEADS, span)
        output = jnp.dot(prob_half, value_win, preferred_element_type=jnp.float32).astype(jnp.bfloat16)
        correction = jnp.sum(grad_flat.astype(jnp.float32) * output.astype(jnp.float32), axis=1).reshape(rows, HEADS)
        dprob = jnp.dot(grad_flat, value_win.T, preferred_element_type=jnp.float32).reshape(rows, HEADS, span)
        dscore_half = (probs * (dprob - correction[..., None])).astype(jnp.bfloat16).reshape(rows * HEADS, span)
        grad_query = (jnp.dot(dscore_half, key_win, preferred_element_type=jnp.float32) * scale).astype(jnp.bfloat16)
        key_term = jnp.dot(dscore_half.T, query_flat, preferred_element_type=jnp.float32)
        value_term = jnp.dot(prob_half.T, grad_flat, preferred_element_type=jnp.float32)
        key_acc = lax.dynamic_update_slice_in_dim(key_acc, lax.dynamic_slice_in_dim(key_acc, start, span, 0) + key_term, start, 0)
        value_acc = lax.dynamic_update_slice_in_dim(value_acc, lax.dynamic_slice_in_dim(value_acc, start, span, 0) + value_term, start, 0)
        return (key_acc, value_acc), (output.reshape(rows, HEADS * HDIM), grad_query.reshape(rows, HEADS * HDIM))

    blocks = jnp.arange(TOKENS // rows, dtype=jnp.int32)
    start_acc = (jnp.zeros((TOKENS + margin, HDIM), jnp.float32), jnp.zeros((TOKENS + margin, HDIM), jnp.float32))
    (key_acc, value_acc), (outputs, grad_queries) = lax.scan(step, start_acc, blocks)
    attn_out = outputs.reshape(TOKENS, HEADS * HDIM)
    grad_q = grad_queries.reshape(TOKENS, HEADS * HDIM)
    grad_keys = (key_acc[margin:] * scale).astype(jnp.bfloat16)
    grad_values = value_acc[margin:].astype(jnp.bfloat16)
    return (attn_out, grad_q, grad_keys, grad_values)
```

```python
import functools
import math

import jax
import jax.numpy as jnp
from jax import lax
from jax.experimental import pallas as pl
from jax.experimental.pallas import tpu as pltpu
from jax.sharding import PartitionSpec as P

HEADS = 8
HDIM = 128
NEG_FILL = -1e30
SCALE = float(HDIM) ** -0.5
EXP2_SCALE = SCALE * math.log2(math.e)

NT = (((1,), (1,)), ((), ()))
NN = (((1,), (0,)), ((), ()))


def dot(a, b, dims=NN):
    return lax.dot_general(a, b, dims, preferred_element_type=jnp.float32)


def route(n_dp, n_ctx, flip):
    pairs = []
    for d in range(n_dp):
        for c in range(n_ctx):
            run = d + int(c >= c ^ flip)
            if run < n_dp:
                pairs.append((d * n_ctx + c, run * n_ctx + (c ^ flip)))
    return pairs


def core_route(n_dp, n_ctx):
    return [(d * n_ctx + c, d * n_ctx + (c ^ 1)) for d in range(n_dp) for c in range(n_ctx)]


def attend(n_ctx, n_docs, group, index_ref, lengths_ref, q_ref, do_ref, own_kv, kv_z, kv_core, kv_direct, kv_passed,
           o_ref, dq_ref, g_own, g_z, g_core, g_direct, g_passed,
           kv, scores, probs, dscore, q_t, do_t, do_s, top, top_b, out_acc, corr, dq_acc, bias, grads, sems):
    rows = q_ref.shape[0]
    many = len(kv_direct)
    block = index_ref[0]
    ctx = lax.rem(block, n_ctx)
    base = block * rows

    copies = [pltpu.make_async_copy(own_kv, kv.at[n_ctx, :, pl.ds(0, 2 * HDIM)], sems.at[n_ctx]),
              pltpu.make_async_copy(kv_z, kv.at[0, :, pl.ds(0, 2 * HDIM)], sems.at[0]),
              pltpu.make_async_copy(kv_core, kv.at[1, :, pl.ds(0, 2 * HDIM)], sems.at[1])]
    for i in range(many):
        copies.append(pltpu.make_async_copy(kv_direct[i], kv.at[2 * i + 2, :, pl.ds(0, 2 * HDIM)], sems.at[2 * i + 2]))
        copies.append(pltpu.make_async_copy(kv_passed.at[i], kv.at[2 * i + 3, :, pl.ds(0, 2 * HDIM)], sems.at[2 * i + 3]))
    for copy in copies:
        copy.start()
    ones = jnp.ones((rows, HDIM), jnp.bfloat16)
    for slot in range(n_ctx + 1):
        kv[slot, :, 2 * HDIM:] = ones

    token = base + lax.broadcasted_iota(jnp.int32, (rows, rows), 0)
    start = jnp.zeros((rows, rows), jnp.int32)
    low = jnp.int32(0)
    end = jnp.int32(0)
    for i in range(n_docs):
        end = end + lengths_ref[i]
        start = jnp.where(token >= end, end, start)
        low = jnp.where(base >= end, end, low)
    before = lax.div(base - low + rows - 1, rows)
    first = start

    def slot_of(back):
        other = lax.rem(ctx - back + 2 * n_ctx, n_ctx)
        return jnp.where(back == 0, n_ctx, ctx ^ other)

    for h in range(HEADS):
        lanes = pl.ds(h * HDIM, HDIM)
        q_t[:, h * rows:(h + 1) * rows] = q_ref[:, lanes].astype(jnp.float32).T.astype(jnp.bfloat16)
    for copy in copies:
        copy.wait()

    bias[...] = first

    for g in range(HEADS // group):
        top[...] = jnp.full(top.shape, NEG_FILL, jnp.float32)

        @pl.loop(0, before + 1)
        def _(back):
            slot = slot_of(back)
            key = base - back * rows + lax.broadcasted_iota(jnp.int32, (rows, rows), 1)
            query = base + lax.broadcasted_iota(jnp.int32, (rows, rows), 0)
            off = jnp.where((key >= bias[...]) & (key <= query), 0.0, NEG_FILL)
            key_block = kv[slot, :, :HDIM]
            for i in range(group):
                h = g * group + i
                s = dot(q_ref[:, h * HDIM:(h + 1) * HDIM], key_block, NT) + off
                scores[back, i] = s
                top[i] = jnp.maximum(top[i], jnp.maximum(s[:, :HDIM], s[:, HDIM:]))

        for i in range(group):
            high = jnp.max(top[i], axis=1, keepdims=True) * EXP2_SCALE
            top_b[i] = jnp.broadcast_to(high, (rows, HDIM))
            out_acc[i] = jnp.zeros((rows, 2 * HDIM), jnp.float32)

        @pl.loop(0, before + 1)
        def _(back):
            slot = slot_of(back)
            value_block = kv[slot, :, HDIM:]
            for i in range(group):
                h = g * group + i
                high = top_b[i]
                s = scores[back, i]
                p = jnp.concatenate([jnp.exp2(s[:, :HDIM] * EXP2_SCALE - high), jnp.exp2(s[:, HDIM:] * EXP2_SCALE - high)], axis=1)
                p = p.astype(jnp.bfloat16)
                probs[back, h * rows:(h + 1) * rows, :] = p
                out_acc[i] += dot(p, value_block)

        for i in range(group):
            h = g * group + i
            lanes = pl.ds(h * HDIM, HDIM)
            acc = out_acc[i]
            inverse = 1.0 / acc[:, HDIM:]
            out = (acc[:, :HDIM] * inverse).astype(jnp.bfloat16)
            o_ref[:, lanes] = out
            grad = do_ref[:, lanes].astype(jnp.float32)
            correction = jnp.sum(grad * out.astype(jnp.float32), axis=1, keepdims=True)
            corr[h] = correction * inverse
            scaled = grad * inverse
            do_s[h] = scaled.astype(jnp.bfloat16)
            do_t[:, h * rows:(h + 1) * rows] = scaled.T.astype(jnp.bfloat16)
            dq_acc[h] = jnp.zeros((rows, HDIM), jnp.float32)

    @pl.loop(0, before + 1)
    def _(back):
        slot = slot_of(back)
        key_block = kv[slot, :, :HDIM]
        value_block = kv[slot, :, HDIM:2 * HDIM]
        for h in range(HEADS):
            d = dot(do_s[h], value_block, NT)
            c = corr[h]
            d = d - jnp.concatenate([c, c], axis=1)
            ds = (probs[back, h * rows:(h + 1) * rows, :].astype(jnp.float32) * d).astype(jnp.bfloat16)
            dscore[h * rows:(h + 1) * rows, :] = ds
            dq_acc[h] += dot(ds, key_block)
        dv_t = dot(do_t[...], probs[back])
        dk_t = dot(q_t[...], dscore[...])
        grads[slot, :, :HDIM] = dk_t.T
        grads[slot, :, HDIM:] = dv_t.T

    @pl.loop(before + 1, n_ctx + 1)
    def _(back):
        grads[slot_of(back)] = jnp.zeros((rows, 2 * HDIM), jnp.float32)

    for h in range(HEADS):
        lanes = pl.ds(h * HDIM, HDIM)
        dq_ref[:, lanes] = (dq_acc[h] * SCALE).astype(jnp.bfloat16)
    g_own[...] = grads[n_ctx]
    g_z[...] = grads[0].astype(jnp.bfloat16)
    g_core[...] = grads[1].astype(jnp.bfloat16)
    for i in range(many):
        g_direct[i] = grads[2 * i + 2].astype(jnp.bfloat16)
        g_passed[i] = grads[2 * i + 3].astype(jnp.bfloat16)


def shards(queries, keys, values, grad_out, lengths):
    rows = keys.shape[0]
    n_dp, n_ctx = lax.axis_size("dp"), lax.axis_size("ctx")
    n_docs = lengths.shape[0]
    axes = ("dp", "ctx")
    many = n_ctx // 2 - 1
    index = (lax.axis_index("dp") * n_ctx + lax.axis_index("ctx")).astype(jnp.int32).reshape(1)
    kv = jnp.concatenate([keys, values], axis=1)

    def permute(block, pairs):
        return lax.ppermute(block, axes, pairs)

    direct = [permute(kv, route(n_dp, n_ctx, 2 * i + 2)) for i in range(many)]
    core = permute(kv, route(n_dp, n_ctx, 1))
    above = permute(kv, route(n_dp, n_ctx, 0))
    passed = permute(jnp.stack(direct), core_route(n_dp, n_ctx))

    blocks = n_ctx + 1
    group = HEADS if blocks * HEADS * rows * rows * 6 <= 32 * 2**20 else HEADS // 2
    vmem = pl.BlockSpec(memory_space=pltpu.VMEM)
    smem = pl.BlockSpec(memory_space=pltpu.SMEM)
    hbm = pl.BlockSpec(memory_space=pl.ANY)
    f32, bf16 = jnp.float32, jnp.bfloat16
    shape = jax.ShapeDtypeStruct
    attn_out, grad_queries, g_own, g_z, g_core, g_direct, g_passed = pl.pallas_call(
        functools.partial(attend, n_ctx, n_docs, group),
        out_shape=(shape(queries.shape, bf16), shape(queries.shape, bf16), shape((rows, 2 * HDIM), f32),
                   shape((rows, 2 * HDIM), bf16), shape((rows, 2 * HDIM), bf16),
                   shape((many, rows, 2 * HDIM), bf16), shape((many, rows, 2 * HDIM), bf16)),
        in_specs=[smem, smem, vmem, vmem, hbm, hbm, hbm, [hbm] * many, hbm],
        out_specs=(vmem,) * 7,
        scratch_shapes=[
            pltpu.VMEM((blocks, rows, 3 * HDIM), bf16),
            pltpu.VMEM((blocks, group, rows, rows), f32),
            pltpu.VMEM((blocks, HEADS * rows, rows), bf16),
            pltpu.VMEM((HEADS * rows, rows), bf16),
            pltpu.VMEM((HDIM, HEADS * rows), bf16),
            pltpu.VMEM((HDIM, HEADS * rows), bf16),
            pltpu.VMEM((HEADS, rows, HDIM), bf16),
            pltpu.VMEM((group, rows, HDIM), f32),
            pltpu.VMEM((group, rows, HDIM), f32),
            pltpu.VMEM((group, rows, 2 * HDIM), f32),
            pltpu.VMEM((HEADS, rows, HDIM), f32),
            pltpu.VMEM((HEADS, rows, HDIM), f32),
            pltpu.VMEM((rows, rows), jnp.int32),
            pltpu.VMEM((blocks, rows, 2 * HDIM), f32),
            pltpu.SemaphoreType.DMA((blocks,)),
        ],
        compiler_params=pltpu.CompilerParams(vmem_limit_bytes=60 * 2**20),
        name="attend",
    )(index, lengths, queries, grad_out, kv, above, core, direct, passed)

    partner = permute(g_passed, core_route(n_dp, n_ctx))
    summed = g_direct.astype(f32) + partner.astype(f32)
    back = lambda pairs: [(b, a) for a, b in pairs]
    total = g_own
    for i in range(many):
        total = total + permute(summed[i].astype(bf16), back(route(n_dp, n_ctx, 2 * i + 2))).astype(f32)
    total = total + permute(g_core, back(route(n_dp, n_ctx, 1))).astype(f32)
    total = total + permute(g_z, back(route(n_dp, n_ctx, 0))).astype(f32)
    grad_keys = (total[:, :HDIM] * SCALE).astype(bf16)
    grad_values = total[:, HDIM:].astype(bf16)
    return (attn_out, grad_queries, grad_keys, grad_values)


def solution(mesh):
    tokens = P(("dp", "ctx"), None)
    return jax.shard_map(
        shards,
        mesh=mesh,
        in_specs=(tokens, tokens, tokens, tokens, P()),
        out_specs=(tokens, tokens, tokens, tokens),
        check_vma=False,
    )
```

```python
import functools
import math

import jax
import jax.numpy as jnp
from jax import lax
from jax.experimental import pallas as pl
from jax.experimental.pallas import tpu as pltpu
from jax.sharding import PartitionSpec as P

HEADS = 8
HDIM = 128
NEG_FILL = -1e30
SCALE = float(HDIM) ** -0.5
EXP2_SCALE = SCALE * math.log2(math.e)

NT = (((1,), (1,)), ((), ()))
NN = (((1,), (0,)), ((), ()))


def dot(a, b, dims=NN):
    return lax.dot_general(a, b, dims, preferred_element_type=jnp.float32)


def run_route(n_dp, n_ctx):
    return [(d * n_ctx + c, (d + 1) * n_ctx + c) for d in range(n_dp - 1) for c in range(n_ctx)]


def flip_route(n_dp, n_ctx, flip):
    return [(d * n_ctx + c, d * n_ctx + (c ^ flip)) for d in range(n_dp) for c in range(n_ctx)]


def attend(n_ctx, n_docs, group, index_ref, lengths_ref, q_ref, do_ref, own_kv, kv_prev, kv_direct, kv_passed,
           o_ref, dq_ref, g_own, g_prev, g_direct, g_passed,
           kv, scores, probs, dscore, q_t, do_t, do_s, top, top_b, out_acc, corr, dq_acc, bias, grads):
    rows = q_ref.shape[0]
    many = kv_passed.shape[0]
    block = index_ref[0]
    ctx = lax.rem(block, n_ctx)
    base = block * rows

    kv[n_ctx, :, :2 * HDIM] = own_kv[...]
    kv[0, :, :2 * HDIM] = kv_prev[...]
    for i in range(many):
        kv[2 * i + 1, :, :2 * HDIM] = kv_passed[i]
        if i > 0:
            kv[2 * i, :, :2 * HDIM] = kv_direct[i - 1][...]
    ones = jnp.ones((rows, HDIM), jnp.bfloat16)
    for slot in range(n_ctx + 1):
        kv[slot, :, 2 * HDIM:] = ones

    token = base + lax.broadcasted_iota(jnp.int32, (rows, rows), 0)
    start = jnp.zeros((rows, rows), jnp.int32)
    low = jnp.int32(0)
    end = jnp.int32(0)
    for i in range(n_docs):
        end = end + lengths_ref[i]
        start = jnp.where(token >= end, end, start)
        low = jnp.where(base >= end, end, low)
    before = lax.div(base - low + rows - 1, rows)
    first = start

    def slot_of(back):
        other = lax.rem(ctx - back + 2 * n_ctx, n_ctx)
        return jnp.where(back == 0, n_ctx, ctx ^ other)

    for h in range(HEADS):
        lanes = pl.ds(h * HDIM, HDIM)
        q_t[:, h * rows:(h + 1) * rows] = q_ref[:, lanes].astype(jnp.float32).T.astype(jnp.bfloat16)
    bias[...] = first

    for g in range(HEADS // group):
        top[...] = jnp.full(top.shape, NEG_FILL, jnp.float32)

        @pl.loop(0, before + 1)
        def _(back):
            slot = slot_of(back)
            key = base - back * rows + lax.broadcasted_iota(jnp.int32, (rows, rows), 1)
            query = base + lax.broadcasted_iota(jnp.int32, (rows, rows), 0)
            off = jnp.where((key >= bias[...]) & (key <= query), 0.0, NEG_FILL)
            key_block = kv[slot, :, :HDIM]
            for i in range(group):
                h = g * group + i
                s = dot(q_ref[:, h * HDIM:(h + 1) * HDIM], key_block, NT) + off
                scores[back, i] = s
                top[i] = jnp.maximum(top[i], jnp.maximum(s[:, :HDIM], s[:, HDIM:]))

        for i in range(group):
            high = jnp.max(top[i], axis=1, keepdims=True) * EXP2_SCALE
            top_b[i] = jnp.broadcast_to(high, (rows, HDIM))
            out_acc[i] = jnp.zeros((rows, 2 * HDIM), jnp.float32)

        @pl.loop(0, before + 1)
        def _(back):
            slot = slot_of(back)
            value_block = kv[slot, :, HDIM:]
            for i in range(group):
                h = g * group + i
                high = top_b[i]
                s = scores[back, i]
                p = jnp.concatenate([jnp.exp2(s[:, :HDIM] * EXP2_SCALE - high), jnp.exp2(s[:, HDIM:] * EXP2_SCALE - high)], axis=1)
                p = p.astype(jnp.bfloat16)
                probs[back, h * rows:(h + 1) * rows, :] = p
                out_acc[i] += dot(p, value_block)

        for i in range(group):
            h = g * group + i
            lanes = pl.ds(h * HDIM, HDIM)
            acc = out_acc[i]
            inverse = 1.0 / acc[:, HDIM:]
            out = (acc[:, :HDIM] * inverse).astype(jnp.bfloat16)
            o_ref[:, lanes] = out
            grad = do_ref[:, lanes].astype(jnp.float32)
            correction = jnp.sum(grad * out.astype(jnp.float32), axis=1, keepdims=True)
            corr[h] = correction * inverse
            scaled = grad * inverse
            do_s[h] = scaled.astype(jnp.bfloat16)
            do_t[:, h * rows:(h + 1) * rows] = scaled.T.astype(jnp.bfloat16)
            dq_acc[h] = jnp.zeros((rows, HDIM), jnp.float32)

    @pl.loop(0, before + 1)
    def _(back):
        slot = slot_of(back)
        key_block = kv[slot, :, :HDIM]
        value_block = kv[slot, :, HDIM:2 * HDIM]
        for h in range(HEADS):
            d = dot(do_s[h], value_block, NT)
            c = corr[h]
            d = d - jnp.concatenate([c, c], axis=1)
            ds = (probs[back, h * rows:(h + 1) * rows, :].astype(jnp.float32) * d).astype(jnp.bfloat16)
            dscore[h * rows:(h + 1) * rows, :] = ds
            dq_acc[h] += dot(ds, key_block)
        dv_t = dot(do_t[...], probs[back])
        dk_t = dot(q_t[...], dscore[...])
        grads[slot, :, :HDIM] = dk_t.T
        grads[slot, :, HDIM:] = dv_t.T

    @pl.loop(before + 1, n_ctx + 1)
    def _(back):
        grads[slot_of(back)] = jnp.zeros((rows, 2 * HDIM), jnp.float32)

    for h in range(HEADS):
        lanes = pl.ds(h * HDIM, HDIM)
        dq_ref[:, lanes] = (dq_acc[h] * SCALE).astype(jnp.bfloat16)
    g_own[...] = grads[n_ctx]
    g_prev[...] = grads[0]
    for i in range(many):
        g_passed[i] = grads[2 * i + 1].astype(jnp.bfloat16)
        if i > 0:
            g_direct[i - 1] = grads[2 * i].astype(jnp.bfloat16)


def shards(queries, keys, values, grad_out, lengths):
    rows = keys.shape[0]
    n_dp, n_ctx = lax.axis_size("dp"), lax.axis_size("ctx")
    n_docs = lengths.shape[0]
    axes = ("dp", "ctx")
    many = n_ctx // 2
    ctx = lax.axis_index("ctx")
    index = (lax.axis_index("dp") * n_ctx + ctx).astype(jnp.int32).reshape(1)
    kv = jnp.concatenate([keys, values], axis=1)

    def swap(block, flip):
        return lax.ppermute(block, axes, flip_route(n_dp, n_ctx, flip))

    def later(flip):
        return ctx < ctx ^ flip

    prev = lax.ppermute(kv, axes, run_route(n_dp, n_ctx))
    sent = [jnp.where(later(max(2 * i, 1)), kv, prev) for i in range(many)]
    direct = [swap(sent[i], 2 * i) for i in range(1, many)]
    passed = swap(jnp.stack([sent[0]] + direct), 1)

    blocks = n_ctx + 1
    group = HEADS if blocks * HEADS * rows * rows * 6 <= 32 * 2**20 else HEADS // 2
    vmem = pl.BlockSpec(memory_space=pltpu.VMEM)
    smem = pl.BlockSpec(memory_space=pltpu.SMEM)
    f32, bf16 = jnp.float32, jnp.bfloat16
    shape = jax.ShapeDtypeStruct
    attn_out, grad_queries, g_own, g_prev, g_direct, g_passed = pl.pallas_call(
        functools.partial(attend, n_ctx, n_docs, group),
        out_shape=(shape(queries.shape, bf16), shape(queries.shape, bf16), shape((rows, 2 * HDIM), f32),
                   shape((rows, 2 * HDIM), f32), shape((many - 1, rows, 2 * HDIM), bf16),
                   shape((many, rows, 2 * HDIM), bf16)),
        in_specs=[smem, smem, vmem, vmem, vmem, vmem, [vmem] * (many - 1), vmem],
        out_specs=(vmem,) * 6,
        scratch_shapes=[
            pltpu.VMEM((blocks, rows, 3 * HDIM), bf16),
            pltpu.VMEM((blocks, group, rows, rows), f32),
            pltpu.VMEM((blocks, HEADS * rows, rows), bf16),
            pltpu.VMEM((HEADS * rows, rows), bf16),
            pltpu.VMEM((HDIM, HEADS * rows), bf16),
            pltpu.VMEM((HDIM, HEADS * rows), bf16),
            pltpu.VMEM((HEADS, rows, HDIM), bf16),
            pltpu.VMEM((group, rows, HDIM), f32),
            pltpu.VMEM((group, rows, HDIM), f32),
            pltpu.VMEM((group, rows, 2 * HDIM), f32),
            pltpu.VMEM((HEADS, rows, HDIM), f32),
            pltpu.VMEM((HEADS, rows, HDIM), f32),
            pltpu.VMEM((rows, rows), jnp.int32),
            pltpu.VMEM((blocks, rows, 2 * HDIM), f32),
        ],
        compiler_params=pltpu.CompilerParams(vmem_limit_bytes=60 * 2**20),
        name="attend",
    )(index, lengths, queries, grad_out, kv, prev, direct, passed)

    partner = swap(g_passed, 1).astype(f32)
    own_total, prev_total = g_own, g_prev
    for i in range(many):
        term = partner[0]
        if i > 0:
            term = swap((g_direct[i - 1].astype(f32) + partner[i]).astype(bf16), 2 * i).astype(f32)
        ours = later(max(2 * i, 1))
        own_total = own_total + jnp.where(ours, term, 0.0)
        prev_total = prev_total + jnp.where(ours, 0.0, term)
    back = [(b, a) for a, b in run_route(n_dp, n_ctx)]
    total = own_total + lax.ppermute(prev_total.astype(bf16), axes, back).astype(f32)
    grad_keys = (total[:, :HDIM] * SCALE).astype(bf16)
    grad_values = total[:, HDIM:].astype(bf16)
    return (attn_out, grad_queries, grad_keys, grad_values)


def solution(mesh):
    tokens = P(("dp", "ctx"), None)
    return jax.shard_map(
        shards,
        mesh=mesh,
        in_specs=(tokens, tokens, tokens, tokens, P()),
        out_specs=(tokens, tokens, tokens, tokens),
        check_vma=False,
    )
```

```python
import functools
import math

import jax
import jax.numpy as jnp
from jax import lax
from jax.experimental import pallas as pl
from jax.experimental.pallas import tpu as pltpu
from jax.sharding import PartitionSpec as P

HEADS = 8
HDIM = 128
NEG_FILL = -1e30
SCALE = float(HDIM) ** -0.5
EXP2_SCALE = SCALE * math.log2(math.e)

NT = (((1,), (1,)), ((), ()))
NN = (((1,), (0,)), ((), ()))


def dot(a, b, dims=NN):
    return lax.dot_general(a, b, dims, preferred_element_type=jnp.float32)


def run_route(n_dp, n_ctx):
    return [(d * n_ctx + c, (d + 1) * n_ctx + c) for d in range(n_dp - 1) for c in range(n_ctx)]


def flip_route(n_dp, n_ctx, flip):
    return [(d * n_ctx + c, d * n_ctx + (c ^ flip)) for d in range(n_dp) for c in range(n_ctx)]


def attend(n_ctx, n_docs, group, index_ref, lengths_ref, q_ref, do_ref, own_kv, kv_prev, kv_direct, kv_passed,
           o_ref, dq_ref, g_own, g_prev, g_direct, g_passed,
           kv, scores, probs, dscore, q_s, q_t, do_s, do_t, top, out_acc, corr, dq_acc, bias, grads):
    rows = q_ref.shape[0]
    many = kv_passed.shape[0]
    block = index_ref[0]
    ctx = lax.rem(block, n_ctx)
    base = block * rows

    kv[n_ctx, :, :2 * HDIM] = own_kv[...]
    kv[0, :, :2 * HDIM] = kv_prev[...]
    for i in range(many):
        kv[2 * i + 1, :, :2 * HDIM] = kv_passed[i]
        if i > 0:
            kv[2 * i, :, :2 * HDIM] = kv_direct[i - 1][...]
    ones = jnp.ones((rows, HDIM), jnp.bfloat16)
    for slot in range(n_ctx + 1):
        kv[slot, :, 2 * HDIM:] = ones

    token = base + lax.broadcasted_iota(jnp.int32, (rows, rows), 0)
    start = jnp.zeros((rows, rows), jnp.int32)
    low = jnp.int32(0)
    end = jnp.int32(0)
    for i in range(n_docs):
        end = end + lengths_ref[i]
        start = jnp.where(token >= end, end, start)
        low = jnp.where(base >= end, end, low)
    before = lax.div(base - low + rows - 1, rows)

    def slot_of(back):
        other = lax.rem(ctx - back + 2 * n_ctx, n_ctx)
        return jnp.where(back == 0, n_ctx, ctx ^ other)

    for h in range(HEADS):
        q = q_ref[:, h * HDIM:(h + 1) * HDIM]
        q_s[h * rows:(h + 1) * rows, :] = q
        q_t[:, h * rows:(h + 1) * rows] = q.astype(jnp.float32).T.astype(jnp.bfloat16)
    bias[...] = start

    def wide(column):
        return jnp.concatenate([column, column], axis=1)

    for g in range(HEADS // group):
        span = pl.ds(g * group * rows, group * rows)
        top[...] = jnp.full(top.shape, NEG_FILL, jnp.float32)

        @pl.loop(0, before + 1)
        def _(back):
            slot = slot_of(back)
            key = base - back * rows + lax.broadcasted_iota(jnp.int32, (rows, rows), 1)
            query = base + lax.broadcasted_iota(jnp.int32, (rows, rows), 0)
            off = jnp.where((key >= bias[...]) & (key <= query), 0.0, NEG_FILL)
            s = dot(q_s[span, :], kv[slot, :, :HDIM], NT).reshape(group, rows, rows) + off[None]
            s = s.reshape(group * rows, rows)
            scores[back] = s
            top[...] = jnp.maximum(top[...], jnp.maximum(s[:, :HDIM], s[:, HDIM:]))

        top[...] = jnp.broadcast_to(jnp.max(top[...], axis=1, keepdims=True) * EXP2_SCALE, top.shape)
        out_acc[...] = jnp.zeros(out_acc.shape, jnp.float32)

        @pl.loop(0, before + 1)
        def _(back):
            p = jnp.exp2(scores[back] * EXP2_SCALE - wide(top[...])).astype(jnp.bfloat16)
            probs[back, span, :] = p
            out_acc[...] += dot(p, kv[slot_of(back), :, HDIM:])

        for i in range(group):
            h = g * group + i
            lanes = pl.ds(h * HDIM, HDIM)
            here = pl.ds(h * rows, rows)
            acc = out_acc[i * rows:(i + 1) * rows, :]
            inverse = 1.0 / acc[:, HDIM:]
            out = (acc[:, :HDIM] * inverse).astype(jnp.bfloat16)
            o_ref[:, lanes] = out
            grad = do_ref[:, lanes].astype(jnp.float32)
            corr[here, :] = jnp.sum(grad * out.astype(jnp.float32), axis=1, keepdims=True) * inverse
            scaled = grad * inverse
            do_s[here, :] = scaled.astype(jnp.bfloat16)
            do_t[:, here] = scaled.T.astype(jnp.bfloat16)

    dq_acc[...] = jnp.zeros(dq_acc.shape, jnp.float32)

    @pl.loop(0, before + 1)
    def _(back):
        slot = slot_of(back)
        d = dot(do_s[...], kv[slot, :, HDIM:2 * HDIM], NT) - wide(corr[...])
        ds = (probs[back].astype(jnp.float32) * d).astype(jnp.bfloat16)
        dscore[...] = ds
        dq_acc[...] += dot(ds, kv[slot, :, :HDIM])
        grads[slot, :, HDIM:] = dot(do_t[...], probs[back]).T
        grads[slot, :, :HDIM] = dot(q_t[...], dscore[...]).T

    @pl.loop(before + 1, n_ctx + 1)
    def _(back):
        grads[slot_of(back)] = jnp.zeros((rows, 2 * HDIM), jnp.float32)

    for h in range(HEADS):
        dq_ref[:, h * HDIM:(h + 1) * HDIM] = (dq_acc[h * rows:(h + 1) * rows, :] * SCALE).astype(jnp.bfloat16)
    g_own[...] = grads[n_ctx]
    g_prev[...] = grads[0]
    for i in range(many):
        g_passed[i] = grads[2 * i + 1].astype(jnp.bfloat16)
        if i > 0:
            g_direct[i - 1] = grads[2 * i].astype(jnp.bfloat16)


def shards(queries, keys, values, grad_out, lengths):
    rows = keys.shape[0]
    n_dp, n_ctx = lax.axis_size("dp"), lax.axis_size("ctx")
    n_docs = lengths.shape[0]
    axes = ("dp", "ctx")
    many = n_ctx // 2
    ctx = lax.axis_index("ctx")
    index = (lax.axis_index("dp") * n_ctx + ctx).astype(jnp.int32).reshape(1)
    kv = jnp.concatenate([keys, values], axis=1)

    def swap(block, flip):
        return lax.ppermute(block, axes, flip_route(n_dp, n_ctx, flip))

    def later(flip):
        return ctx < ctx ^ flip

    prev = lax.ppermute(kv, axes, run_route(n_dp, n_ctx))
    sent = [jnp.where(later(max(2 * i, 1)), kv, prev) for i in range(many)]
    direct = [swap(sent[i], 2 * i) for i in range(1, many)]
    passed = swap(jnp.stack([sent[0]] + direct), 1)

    blocks = n_ctx + 1
    group = HEADS if blocks * HEADS * rows * rows * 6 <= 32 * 2**20 else HEADS // 2
    vmem = pl.BlockSpec(memory_space=pltpu.VMEM)
    smem = pl.BlockSpec(memory_space=pltpu.SMEM)
    f32, bf16 = jnp.float32, jnp.bfloat16
    shape = jax.ShapeDtypeStruct
    scratch = [
        pltpu.VMEM((blocks, rows, 3 * HDIM), bf16),
        pltpu.VMEM((blocks, group * rows, rows), f32),
        pltpu.VMEM((blocks, HEADS * rows, rows), bf16),
        pltpu.VMEM((HEADS * rows, rows), bf16),
        pltpu.VMEM((HEADS * rows, HDIM), bf16),
        pltpu.VMEM((HDIM, HEADS * rows), bf16),
        pltpu.VMEM((HEADS * rows, HDIM), bf16),
        pltpu.VMEM((HDIM, HEADS * rows), bf16),
        pltpu.VMEM((group * rows, HDIM), f32),
        pltpu.VMEM((group * rows, 2 * HDIM), f32),
        pltpu.VMEM((HEADS * rows, HDIM), f32),
        pltpu.VMEM((HEADS * rows, HDIM), f32),
        pltpu.VMEM((rows, rows), jnp.int32),
        pltpu.VMEM((blocks, rows, 2 * HDIM), f32),
    ]
    held = sum(math.prod(ref.shape) * jnp.dtype(ref.dtype).itemsize for ref in scratch)
    attn_out, grad_queries, g_own, g_prev, g_direct, g_passed = pl.pallas_call(
        functools.partial(attend, n_ctx, n_docs, group),
        out_shape=(shape(queries.shape, bf16), shape(queries.shape, bf16), shape((rows, 2 * HDIM), f32),
                   shape((rows, 2 * HDIM), f32), shape((many - 1, rows, 2 * HDIM), bf16),
                   shape((many, rows, 2 * HDIM), bf16)),
        in_specs=[smem, smem, vmem, vmem, vmem, vmem, [vmem] * (many - 1), vmem],
        out_specs=(vmem,) * 6,
        scratch_shapes=scratch,
        compiler_params=pltpu.CompilerParams(vmem_limit_bytes=held + 8 * 2**20),
        name="attend",
    )(index, lengths, queries, grad_out, kv, prev, direct, passed)

    partner = swap(g_passed, 1).astype(f32)
    own_total, prev_total = g_own, g_prev
    for i in range(many):
        term = partner[0]
        if i > 0:
            term = swap((g_direct[i - 1].astype(f32) + partner[i]).astype(bf16), 2 * i).astype(f32)
        ours = later(max(2 * i, 1))
        own_total = own_total + jnp.where(ours, term, 0.0)
        prev_total = prev_total + jnp.where(ours, 0.0, term)
    back = [(b, a) for a, b in run_route(n_dp, n_ctx)]
    total = own_total + lax.ppermute(prev_total.astype(bf16), axes, back).astype(f32)
    grad_keys = (total[:, :HDIM] * SCALE).astype(bf16)
    grad_values = total[:, HDIM:].astype(bf16)
    return (attn_out, grad_queries, grad_keys, grad_values)


def solution(mesh):
    tokens = P(("dp", "ctx"), None)
    return jax.shard_map(
        shards,
        mesh=mesh,
        in_specs=(tokens, tokens, tokens, tokens, P()),
        out_specs=(tokens, tokens, tokens, tokens),
        check_vma=False,
    )
```

```python
import functools
import math

import jax
import jax.numpy as jnp
from jax import lax
from jax.experimental import pallas as pl
from jax.experimental.pallas import tpu as pltpu
from jax.sharding import PartitionSpec as P

HEADS = 8
HDIM = 128
NEG_FILL = -1e30
SCALE = float(HDIM) ** -0.5
EXP2_SCALE = SCALE * math.log2(math.e)

NT = (((1,), (1,)), ((), ()))
NN = (((1,), (0,)), ((), ()))
F32, BF16 = jnp.float32, jnp.bfloat16


def dot(a, b, dims=NN):
    return lax.dot_general(a, b, dims, preferred_element_type=F32)


def wide(column):
    return jnp.concatenate([column, column], axis=1)


def run_route(n_dp, n_ctx):
    return [(d * n_ctx + c, (d + 1) * n_ctx + c) for d in range(n_dp - 1) for c in range(n_ctx)]


def flip_route(n_dp, n_ctx, flip):
    return [(d * n_ctx + c, d * n_ctx + (c ^ flip)) for d in range(n_dp) for c in range(n_ctx)]


class Place:
    def __init__(self, n_ctx, rows, index_ref, lengths_ref):
        self.n_ctx, self.rows = n_ctx, rows
        self.ctx = lax.rem(index_ref[0], n_ctx)
        self.base = index_ref[0] * rows
        self.ends, end = [], jnp.int32(0)
        for i in range(lengths_ref.shape[0]):
            end = end + lengths_ref[i]
            self.ends.append(end)
        low, high = jnp.int32(0), self.ends[-1]
        for end in self.ends:
            low = jnp.where(end <= self.base, end, low)
        for end in reversed(self.ends):
            high = jnp.where(end > self.base, end, high)
        self.before = lax.div(self.base - low + rows - 1, rows)
        self.short = high - self.base <= rows - rows // n_ctx

    def slot(self, back):
        other = lax.rem(self.ctx - back + 2 * self.n_ctx, self.n_ctx)
        return jnp.where(back == 0, self.n_ctx, self.ctx ^ other)

    def past(self, backs, body):
        first, step = backs[0], backs.step
        count = jnp.clip(lax.div(self.before - first + step, step), 0, len(backs))
        for short in (True, False):

            @pl.when(self.short if short else jnp.logical_not(self.short))
            def _():
                @pl.loop(0, count)
                def _(i):
                    body(first + i * step, HEADS * (self.rows - self.rows // self.n_ctx if short else self.rows))

        return count


def chunks(rows, n_ctx):
    size = rows // n_ctx
    for c in range(n_ctx):
        for h in range(HEADS):
            yield (pl.ds((c * HEADS + h) * size, size), (pl.ds(c * size, size), pl.ds(h * HDIM, HDIM)))


def prepare(n_ctx, q_ref, do_ref, q_s, q_t, do_r):
    rows = q_ref.shape[0]
    for here, there in chunks(rows, n_ctx):
        q_s[here, :] = q_ref[there]
        do_r[here, :] = do_ref[there]
    for h in range(HEADS):
        here = pl.ds(h * rows, rows)
        q_t[:, here] = q_s[here, :].astype(F32).T.astype(BF16)


def forward(n_ctx, span, index_ref, lengths_ref, q_s, q_t, do_r, own_kv, kv_prev, kv_direct, kv_passed,
            o_ref, kv, probs, ds_odd, do_s, do_t, corr, g_passed, scores, top, out_acc, start):
    rows = o_ref.shape[0]
    size = rows // n_ctx
    place = Place(n_ctx, rows, index_ref, lengths_ref)
    pairs = n_ctx // 2

    kv[n_ctx, :, :2 * HDIM] = own_kv[...]
    kv[0, :, :2 * HDIM] = kv_prev[...]
    for i in range(pairs):
        kv[2 * i + 1, :, :2 * HDIM] = kv_passed[i]
        if i > 0:
            kv[2 * i, :, :2 * HDIM] = kv_direct[i - 1][...]
    for slot in range(n_ctx + 1):
        kv[slot, :, 2 * HDIM:] = jnp.ones((rows, HDIM), BF16)

    token = place.base + lax.broadcasted_iota(jnp.int32, (rows, rows), 0)
    begin = jnp.zeros((rows, rows), jnp.int32)
    for end in place.ends:
        begin = jnp.where(token >= end, end, begin)
    start[...] = begin

    for low in range(0, HEADS * rows, span):

        def score(back, many, fresh=False):
            n = min(many - low, span)
            tokens = pl.ds(low // HEADS, n // HEADS)
            shape = (n // HEADS, rows)
            key = place.base - back * rows + lax.broadcasted_iota(jnp.int32, shape, 1)
            query = place.base + low // HEADS + lax.broadcasted_iota(jnp.int32, shape, 0)
            off = jnp.where((key >= start[tokens, :]) & (key <= query), 0.0, NEG_FILL)
            s = dot(q_s[low:low + n, :], kv[place.slot(back), :, :HDIM], NT)
            s = s.reshape(n // HEADS // size, HEADS, size, rows) + off.reshape(n // HEADS // size, 1, size, rows)
            s = s.reshape(n, rows)
            scores[back, :n, :] = s
            high = jnp.maximum(s[:, :HDIM], s[:, HDIM:])
            top[:n, :] = high if fresh else jnp.maximum(top[:n, :], high)

        def attend(back, many, fresh=False):
            n = min(many - low, span)
            p = jnp.exp2(scores[back, :n, :] * EXP2_SCALE - wide(top[:n, :])).astype(BF16)
            probs[back, low:low + n, :] = p
            term = dot(p, kv[place.slot(back), :, HDIM:])
            out_acc[:n, :] = term if fresh else out_acc[:n, :] + term

        score(0, HEADS * rows, True)
        place.past(range(1, n_ctx + 1), score)
        top[...] = jnp.broadcast_to(jnp.max(top[...], axis=1, keepdims=True) * EXP2_SCALE, top.shape)
        attend(0, HEADS * rows, True)
        place.past(range(1, n_ctx + 1), attend)

        for i in range(0, span, rows):
            acc = out_acc[i:i + rows, :]
            here = pl.ds(low + i, rows)
            inverse = 1.0 / acc[:, HDIM:]
            out = (acc[:, :HDIM] * inverse).astype(BF16)
            grad = do_r[here, :].astype(F32)
            corr[here, :] = jnp.sum(grad * out.astype(F32), axis=1, keepdims=True) * inverse
            scaled = grad * inverse
            do_s[here, :] = scaled.astype(BF16)
            do_t[:, here] = scaled.T.astype(BF16)
            for j, (part, there) in enumerate(chunks(rows, n_ctx)):
                if low + i <= part.start < low + i + rows:
                    o_ref[there] = out[part.start - low - i:part.start - low - i + size, :]

    def backward(back, many):
        slot = place.slot(back)
        ds_odd[lax.div(back, 2), :many, :] = ds = dscore(many, do_s, probs[back, :many, :], kv, slot, corr)
        g_passed[lax.div(slot, 2)] = key_value_terms(many, q_t, do_t, ds, probs[back, :many, :]).astype(BF16)

    done = place.past(range(1, n_ctx, 2), backward)

    @pl.loop(done, pairs)
    def _(i):
        g_passed[lax.div(place.slot(2 * i + 1), 2)] = jnp.zeros((rows, 2 * HDIM), BF16)


def dscore(many, do_s, p, kv, slot, corr):
    d = dot(do_s[:many, :], kv[slot, :, HDIM:2 * HDIM], NT) - wide(corr[:many, :])
    return (p.astype(F32) * d).astype(BF16)


def key_value_terms(many, q_t, do_t, ds, p):
    return jnp.concatenate([dot(q_t[:, :many], ds).T, dot(do_t[:, :many], p).T], axis=1)


def even(n_ctx, index_ref, lengths_ref, q_t, do_s, do_t, kv, probs, corr, ds_even, g_direct):
    rows = kv.shape[1]
    place = Place(n_ctx, rows, index_ref, lengths_ref)

    def backward(back, many):
        slot = place.slot(back)
        ds_even[lax.div(back, 2) - 1, :many, :] = ds = dscore(many, do_s, probs[back, :many, :], kv, slot, corr)
        g_direct[lax.div(slot, 2) - 1] = key_value_terms(many, q_t, do_t, ds, probs[back, :many, :])

    done = place.past(range(2, n_ctx, 2), backward)

    @pl.loop(done, n_ctx // 2 - 1)
    def _(i):
        g_direct[lax.div(place.slot(2 * i + 2), 2) - 1] = jnp.zeros((rows, 2 * HDIM), F32)


def rest(n_ctx, index_ref, lengths_ref, q_t, do_s, do_t, kv, probs, corr, ds_odd, ds_even, dq_ref, g_own, g_prev, dq_acc):
    rows = kv.shape[1]
    place = Place(n_ctx, rows, index_ref, lengths_ref)

    def backward(back, many, ref):
        slot = place.slot(back)
        p = probs[back, :many, :]
        ds = dscore(many, do_s, p, kv, slot, corr)
        ref[...] = key_value_terms(many, q_t, do_t, ds, p)
        term = dot(ds, kv[slot, :, :HDIM])
        if ref is g_own:
            dq_acc[...] = term
        else:
            dq_acc[:many, :] += term

    def add(ref, index):
        def body(back, many):
            dq_acc[:many, :] += dot(ref[index(back), :many, :], kv[place.slot(back), :, :HDIM])
        return body

    backward(0, HEADS * rows, g_own)
    place.past(range(1, n_ctx, 2), add(ds_odd, lambda back: lax.div(back, 2)))
    place.past(range(2, n_ctx, 2), add(ds_even, lambda back: lax.div(back, 2) - 1))
    g_prev[...] = jnp.zeros(g_prev.shape, F32)
    place.past(range(n_ctx, n_ctx + 1), lambda back, many: backward(back, many, g_prev))

    for here, there in chunks(rows, n_ctx):
        dq_ref[there] = (dq_acc[here, :] * SCALE).astype(BF16)


def finish(total, last, gk_ref, gv_ref):
    terms = total[...] + last[...].astype(F32)
    gk_ref[...] = (terms[:, :HDIM] * SCALE).astype(BF16)
    gv_ref[...] = terms[:, HDIM:].astype(BF16)


def size_of(refs):
    return sum(math.prod(ref.shape) * jnp.dtype(ref.dtype).itemsize for ref in refs)


def call(body, name, outs, scalars, args, scratch, flops, resident):
    outs = tuple(jax.ShapeDtypeStruct(shape, dtype) for shape, dtype in outs)
    held = size_of(scratch) + 8 * 2**20
    if not resident:
        held = min(held + size_of(outs) + size_of(jax.tree.leaves(args)), 62 * 2**20)
    vmem = pl.BlockSpec(memory_space=pltpu.VMEM)
    smem = pl.BlockSpec(memory_space=pltpu.SMEM)
    return pl.pallas_call(
        body,
        out_shape=outs,
        in_specs=[smem] * len(scalars) + [jax.tree.map(lambda _: vmem, arg) for arg in args],
        out_specs=(vmem,) * len(outs),
        scratch_shapes=scratch,
        compiler_params=pltpu.CompilerParams(vmem_limit_bytes=held),
        cost_estimate=pl.CostEstimate(flops=flops, bytes_accessed=2**20, transcendentals=0),
        name=name,
    )(*scalars, *args)


def shards(queries, keys, values, grad_out, lengths):
    rows = keys.shape[0]
    n_dp, n_ctx = lax.axis_size("dp"), lax.axis_size("ctx")
    axes = ("dp", "ctx")
    pairs = n_ctx // 2
    ctx = lax.axis_index("ctx")
    index = (lax.axis_index("dp") * n_ctx + ctx).astype(jnp.int32).reshape(1)
    kv = jnp.concatenate([keys, values], axis=1)

    def swap(block, flip):
        return lax.ppermute(block, axes, flip_route(n_dp, n_ctx, flip))

    def later(flip):
        return ctx < ctx ^ flip

    prev = lax.ppermute(kv, axes, run_route(n_dp, n_ctx))
    sent = [jnp.where(later(max(2 * i, 1)), kv, prev) for i in range(pairs)]
    direct = [swap(sent[i], 2 * i) for i in range(1, pairs)]
    passed = swap(jnp.stack([sent[0]] + direct), 1)

    blocks, many = n_ctx + 1, HEADS * rows
    resident = blocks * many * rows <= 6 * 2**20
    span = many if resident else many // 4
    run = functools.partial(call, resident=resident)
    once = 2 * many * rows * HDIM
    by_row, by_lane = (many, HDIM), (HDIM, many)
    block = (rows, 2 * HDIM)
    scalars = (index, lengths)

    q_s, q_t, do_r = run(functools.partial(prepare, n_ctx), "prepare",
                          [(by_row, BF16), (by_lane, BF16), (by_row, BF16)], (), (queries, grad_out), [], once)
    attn_out, kv_all, probs, ds_odd, do_s, do_t, corr, g_passed = run(
        functools.partial(forward, n_ctx, span), "forward",
        [(queries.shape, BF16), ((blocks, rows, 3 * HDIM), BF16), ((blocks, many, rows), BF16), ((pairs, many, rows), BF16),
         (by_row, BF16), (by_lane, BF16), (by_row, F32), ((pairs,) + block, BF16)],
        scalars, (q_s, q_t, do_r, kv, prev, direct, passed),
        [pltpu.VMEM((blocks, span, rows), F32), pltpu.VMEM((span, HDIM), F32), pltpu.VMEM((span, 2 * HDIM), F32),
         pltpu.VMEM((rows, rows), jnp.int32)],
        (2 * blocks + 3 * pairs) * once)
    partner = swap(g_passed, 1).astype(F32)
    shared = (q_t, do_s, do_t, kv_all, probs, corr)
    ds_even, g_direct = run(functools.partial(even, n_ctx), "even",
                             [((pairs - 1, many, rows), BF16), ((pairs - 1,) + block, F32)],
                             scalars, shared, [], 3 * (pairs - 1) * once)
    terms = [partner[0]] + [swap((g_direct[i - 1] + partner[i]).astype(BF16), 2 * i).astype(F32) for i in range(1, pairs)]
    grad_queries, g_own, g_prev = run(functools.partial(rest, n_ctx), "rest",
                                       [(queries.shape, BF16), (block, F32), (block, F32)],
                                       scalars, shared + (ds_odd, ds_even), [pltpu.VMEM(by_row, F32)], (blocks + 6) * once)
    own_total, prev_total = g_own, g_prev
    for i in range(pairs):
        ours = later(max(2 * i, 1))
        own_total = own_total + jnp.where(ours, terms[i], 0.0)
        prev_total = prev_total + jnp.where(ours, 0.0, terms[i])
    back = [(b, a) for a, b in run_route(n_dp, n_ctx)]
    last = lax.ppermute(prev_total.astype(BF16), axes, back)
    grad_keys, grad_values = run(finish, "finish", [(keys.shape, BF16), (values.shape, BF16)], (), (own_total, last), [], 1)
    return (attn_out, grad_queries, grad_keys, grad_values)


def solution(mesh):
    tokens = P(("dp", "ctx"), None)
    return jax.shard_map(
        shards,
        mesh=mesh,
        in_specs=(tokens, tokens, tokens, tokens, P()),
        out_specs=(tokens, tokens, tokens, tokens),
        check_vma=False,
    )
```

```python
import functools
import math

import jax
import jax.numpy as jnp
from jax import lax
from jax.experimental import pallas as pl
from jax.experimental.pallas import tpu as pltpu
from jax.sharding import PartitionSpec as P

HEADS = 8
HDIM = 128
NEG_FILL = -1e30
SCALE = float(HDIM) ** -0.5
EXP2_SCALE = SCALE * math.log2(math.e)

NT = (((1,), (1,)), ((), ()))
NN = (((1,), (0,)), ((), ()))
F32, BF16 = jnp.float32, jnp.bfloat16


def dot(a, b, dims=NN):
    return lax.dot_general(a, b, dims, preferred_element_type=F32)


def wide(column):
    return jnp.concatenate([column, column], axis=1)


def run_route(n_dp, n_ctx):
    return [(d * n_ctx + c, (d + 1) * n_ctx + c) for d in range(n_dp - 1) for c in range(n_ctx)]


def flip_route(n_dp, n_ctx, flip):
    return [(d * n_ctx + c, d * n_ctx + (c ^ flip)) for d in range(n_dp) for c in range(n_ctx)]


class Place:
    def __init__(self, n_ctx, rows, index_ref, lengths_ref):
        self.n_ctx, self.rows = n_ctx, rows
        self.ctx = lax.rem(index_ref[0], n_ctx)
        self.base = index_ref[0] * rows
        self.ends, end = [], jnp.int32(0)
        for i in range(lengths_ref.shape[0]):
            end = end + lengths_ref[i]
            self.ends.append(end)
        low, high = jnp.int32(0), self.ends[-1]
        for end in self.ends:
            low = jnp.where(end <= self.base, end, low)
        for end in reversed(self.ends):
            high = jnp.where(end > self.base, end, high)
        self.before = lax.div(self.base - low + rows - 1, rows)
        self.short = high - self.base <= rows - rows // n_ctx

    def slot(self, back):
        other = lax.rem(self.ctx - back + 2 * self.n_ctx, self.n_ctx)
        return jnp.where(back == 0, self.n_ctx, self.ctx ^ other)

    def past(self, backs, body):
        first, step = backs[0], backs.step
        count = jnp.clip(lax.div(self.before - first + step, step), 0, len(backs))
        for short in (True, False):

            @pl.when(self.short if short else jnp.logical_not(self.short))
            def _():
                @pl.loop(0, count)
                def _(i):
                    body(first + i * step, HEADS * (self.rows - self.rows // self.n_ctx if short else self.rows))

        return count


def chunks(rows, n_ctx):
    size = rows // n_ctx
    for c in range(n_ctx):
        for h in range(HEADS):
            yield (pl.ds((c * HEADS + h) * size, size), (pl.ds(c * size, size), pl.ds(h * HDIM, HDIM)))


def join(keys, values, kv):
    kv[:, :HDIM] = keys[...]
    kv[:, HDIM:] = values[...]


def with_ones(kv):
    return jnp.concatenate([kv, jnp.ones((kv.shape[0], HDIM), BF16)], axis=1)


def levels(place, back, many, q_s, key_block, start):
    size, rows = place.rows // place.n_ctx, place.rows
    tokens = many // HEADS
    key = place.base - back * rows + lax.broadcasted_iota(jnp.int32, (tokens, rows), 1)
    query = place.base + lax.broadcasted_iota(jnp.int32, (tokens, rows), 0)
    off = jnp.where((key >= start[:tokens, :]) & (key <= query), 0.0, NEG_FILL)
    s = dot(q_s[:many, :], key_block, NT) * EXP2_SCALE
    s = s.reshape(tokens // size, HEADS, size, rows) + off.reshape(tokens // size, 1, size, rows)
    return s.reshape(many, rows)


def fold(s):
    return jnp.maximum(s[:, :HDIM], s[:, HDIM:])


def row_max(s):
    return jnp.broadcast_to(jnp.max(s, axis=1, keepdims=True), (s.shape[0], HDIM))


def prepare(n_ctx, index_ref, lengths_ref, q_ref, do_ref, kv_ref, kv_own, q_s, q_t, do_r, start, level, p_own, acc):
    rows = q_ref.shape[0]
    place = Place(n_ctx, rows, index_ref, lengths_ref)
    kv_own[...] = with_ones(kv_ref[...])
    for here, there in chunks(rows, n_ctx):
        q_s[here, :] = q_ref[there]
        do_r[here, :] = do_ref[there]
    token = place.base + lax.broadcasted_iota(jnp.int32, (rows, HDIM), 0)
    begin = jnp.zeros((rows, HDIM), jnp.int32)
    for end in place.ends:
        begin = jnp.where(token >= end, end, begin)
    start[...] = wide(begin) if rows == 2 * HDIM else jnp.broadcast_to(begin[:, :1], (rows, rows))
    s = levels(place, 0, HEADS * rows, q_s, kv_own[:, :HDIM], start)
    top = row_max(fold(s))
    level[...] = top
    p = jnp.exp2(s - wide(top)).astype(BF16)
    p_own[...] = p
    acc[...] = dot(p, kv_own[:, HDIM:])
    for h in range(HEADS):
        here = pl.ds(h * rows, rows)
        q_t[:, here] = q_s[here, :].astype(F32).T.astype(BF16)


def attend(place, back, many, q_s, kv, start, level, acc, probs):
    p = jnp.exp2(levels(place, back, many, q_s, kv[:, :HDIM], start) - wide(level[:many, :])).astype(BF16)
    probs[:many, :] = p
    acc[:many, :] += dot(p, kv[:, HDIM:])


def attend_even(n_ctx, index_ref, lengths_ref, q_s, start, level, acc_in, kv_prev, kv_direct, kv_even, p_even, acc):
    rows = kv_prev.shape[0]
    place = Place(n_ctx, rows, index_ref, lengths_ref)
    kv_even[0] = with_ones(kv_prev[...])
    for i in range(n_ctx // 2 - 1):
        kv_even[i + 1] = with_ones(kv_direct[i][...])
    acc[...] = acc_in[...]

    def body(back, many):
        kv = kv_even.at[lax.div(place.slot(back), 2)]
        attend(place, back, many, q_s, kv, start, level, acc, p_even.at[lax.div(back, 2) - 1])

    place.past(range(2, n_ctx + 1, 2), body)


def dscore(many, do_s, p, kv, corr):
    d = dot(do_s[:many, :], kv[:, HDIM:2 * HDIM], NT) - wide(corr[:many, :])
    return (p.astype(F32) * d).astype(BF16)


def key_value_terms(many, q_t, do_t, ds, p):
    return jnp.concatenate([dot(q_t[:, :many], ds).T, dot(do_t[:, :many], p).T], axis=1)


def forward(n_ctx, index_ref, lengths_ref, q_s, q_t, do_r, start, level, acc_in, kv_own, kv_even, kv_passed, p_own_in, p_even_in,
            o_ref, kv_odd, ds_odd, do_s, do_t, corr, g_passed, p_own, p_even, p_odd, acc, top, p_new, sem):
    rows = o_ref.shape[0]
    size = rows // n_ctx
    place = Place(n_ctx, rows, index_ref, lengths_ref)
    pairs = n_ctx // 2
    everything = HEADS * rows
    odd_backs, even_backs = range(1, n_ctx, 2), range(2, n_ctx + 1, 2)
    del p_own_in, p_even_in

    for i in range(pairs):
        kv_odd[i] = with_ones(kv_passed[i])

    def odd(back):
        return kv_odd.at[lax.div(place.slot(back), 2)]

    def even(back):
        return kv_even.at[lax.div(place.slot(back), 2)]

    acc[...] = acc_in[...]
    place.past(odd_backs, lambda back, many: attend(place, back, many, q_s, odd(back), start, level, acc, p_odd.at[lax.div(back, 2)]))

    @pl.when(jnp.logical_not(jnp.max(acc[:, HDIM:]) < 2.0 ** 40))
    def _():
        def raise_top(back, many, kv):
            top[:many, :] = jnp.maximum(top[:many, :], fold(levels(place, back, many, q_s, kv[:, :HDIM], start)))

        top[...] = jnp.full(top.shape, NEG_FILL, F32)
        raise_top(0, everything, kv_own)
        place.past(odd_backs, lambda back, many: raise_top(back, many, odd(back)))
        place.past(even_backs, lambda back, many: raise_top(back, many, even(back)))
        top[...] = row_max(top[...])
        acc[...] = jnp.zeros(acc.shape, F32)

        def replace(back, many, kv, probs):
            attend(place, back, many, q_s, kv, start, top, acc, p_new)
            copy = pltpu.make_async_copy(p_new.at[pl.ds(0, many)], probs.at[pl.ds(0, many)], sem)
            copy.start()
            copy.wait()

        replace(0, everything, kv_own, p_own)
        place.past(even_backs, lambda back, many: replace(back, many, even(back), p_even.at[lax.div(back, 2) - 1]))
        place.past(odd_backs, lambda back, many: attend(place, back, many, q_s, odd(back), start, top, acc, p_odd.at[lax.div(back, 2)]))

    for i in range(0, everything, rows):
        here = pl.ds(i, rows)
        total = acc[here, :]
        inverse = 1.0 / total[:, HDIM:]
        out = (total[:, :HDIM] * inverse).astype(BF16)
        grad = do_r[here, :].astype(F32)
        corr[here, :] = jnp.sum(grad * out.astype(F32), axis=1, keepdims=True) * inverse
        scaled = grad * inverse
        do_s[here, :] = scaled.astype(BF16)
        do_t[:, here] = scaled.T.astype(BF16)
        for part, there in chunks(rows, n_ctx):
            if i <= part.start < i + rows:
                o_ref[there] = out[part.start - i:part.start - i + size, :]

    def backward(back, many):
        p = p_odd[lax.div(back, 2), :many, :]
        ds_odd[lax.div(back, 2), :many, :] = ds = dscore(many, do_s, p, odd(back), corr)
        g_passed[lax.div(place.slot(back), 2)] = key_value_terms(many, q_t, do_t, ds, p).astype(BF16)

    done = place.past(odd_backs, backward)

    @pl.loop(done, pairs)
    def _(i):
        g_passed[lax.div(place.slot(2 * i + 1), 2)] = jnp.zeros((rows, 2 * HDIM), BF16)


def even(n_ctx, index_ref, lengths_ref, q_t, do_s, do_t, kv_even, p_even, corr, ds_even, g_direct):
    rows = kv_even.shape[1]
    place = Place(n_ctx, rows, index_ref, lengths_ref)

    def backward(back, many):
        at = lax.div(place.slot(back), 2)
        p = p_even[lax.div(back, 2) - 1, :many, :]
        ds_even[lax.div(back, 2) - 1, :many, :] = ds = dscore(many, do_s, p, kv_even.at[at], corr)
        g_direct[at - 1] = key_value_terms(many, q_t, do_t, ds, p)

    done = place.past(range(2, n_ctx, 2), backward)

    @pl.loop(done, n_ctx // 2 - 1)
    def _(i):
        g_direct[lax.div(place.slot(2 * i + 2), 2) - 1] = jnp.zeros((rows, 2 * HDIM), F32)


def rest(n_ctx, index_ref, lengths_ref, q_t, do_s, do_t, kv_even, p_even, corr, kv_own, p_own, kv_odd, ds_odd, ds_even,
         dq_ref, g_own, g_prev, dq_acc):
    rows = kv_own.shape[0]
    place = Place(n_ctx, rows, index_ref, lengths_ref)

    p = p_own[...]
    ds = dscore(HEADS * rows, do_s, p, kv_own, corr)
    g_own[...] = key_value_terms(HEADS * rows, q_t, do_t, ds, p)
    dq_acc[...] = dot(ds, kv_own[:, :HDIM])

    def add_odd(back, many):
        dq_acc[:many, :] += dot(ds_odd[lax.div(back, 2), :many, :], kv_odd[lax.div(place.slot(back), 2), :, :HDIM])

    def add_even(back, many):
        dq_acc[:many, :] += dot(ds_even[lax.div(back, 2) - 1, :many, :], kv_even[lax.div(place.slot(back), 2), :, :HDIM])

    def farthest(back, many):
        p = p_even[n_ctx // 2 - 1, :many, :]
        ds = dscore(many, do_s, p, kv_even.at[0], corr)
        g_prev[...] = key_value_terms(many, q_t, do_t, ds, p)
        dq_acc[:many, :] += dot(ds, kv_even[0, :, :HDIM])

    place.past(range(1, n_ctx, 2), add_odd)
    place.past(range(2, n_ctx, 2), add_even)
    g_prev[...] = jnp.zeros(g_prev.shape, F32)
    place.past(range(n_ctx, n_ctx + 1), farthest)

    for here, there in chunks(rows, n_ctx):
        dq_ref[there] = (dq_acc[here, :] * SCALE).astype(BF16)


def finish(total, last, gk_ref, gv_ref):
    terms = total[...] + last[...].astype(F32)
    gk_ref[...] = (terms[:, :HDIM] * SCALE).astype(BF16)
    gv_ref[...] = terms[:, HDIM:].astype(BF16)


def size_of(refs):
    return sum(math.prod(ref.shape) * jnp.dtype(ref.dtype).itemsize for ref in refs if hasattr(ref, "shape") and ref.shape)


def call(body, name, outs, scalars, args, scratch, flops, resident, aliases=()):
    vmem = pl.BlockSpec(memory_space=pltpu.VMEM)
    smem = pl.BlockSpec(memory_space=pltpu.SMEM)
    anywhere = pl.BlockSpec(memory_space=pl.ANY)
    outs = tuple(jax.ShapeDtypeStruct(shape, dtype) for shape, dtype in outs)
    held = size_of(scratch) + 8 * 2**20
    if not resident:
        held = min(held + size_of(outs) + size_of(jax.tree.leaves(args)), 62 * 2**20)
    in_specs = [jax.tree.map(lambda _: vmem, arg) for arg in args]
    out_specs = [vmem] * len(outs)
    places = [sum(len(jax.tree.leaves(arg)) for arg in args[:i]) + len(scalars) for i in range(len(args))]
    for i, o in aliases:
        in_specs[i] = out_specs[o] = anywhere
    return pl.pallas_call(
        body,
        out_shape=outs,
        in_specs=[smem] * len(scalars) + in_specs,
        out_specs=tuple(out_specs),
        scratch_shapes=scratch,
        input_output_aliases={places[i]: o for i, o in aliases},
        compiler_params=pltpu.CompilerParams(vmem_limit_bytes=held),
        cost_estimate=pl.CostEstimate(flops=flops, bytes_accessed=2**20, transcendentals=0),
        name=name,
    )(*scalars, *args)


def shards(queries, keys, values, grad_out, lengths):
    rows = keys.shape[0]
    n_dp, n_ctx = lax.axis_size("dp"), lax.axis_size("ctx")
    axes = ("dp", "ctx")
    pairs = n_ctx // 2
    ctx = lax.axis_index("ctx")
    index = (lax.axis_index("dp") * n_ctx + ctx).astype(jnp.int32).reshape(1)
    many = HEADS * rows
    once = 2 * many * rows * HDIM
    by_row, by_lane = (many, HDIM), (HDIM, many)
    block, kv_ones = (rows, 2 * HDIM), (rows, 3 * HDIM)
    scalars = (index, lengths)
    run = functools.partial(call, resident=(n_ctx + 1) * many * rows <= 6 * 2**20)

    def kernel(body, *args, **kwargs):
        return run(functools.partial(body, n_ctx), body.__name__, *args, **kwargs)

    def swap(block, flip):
        return lax.ppermute(block, axes, flip_route(n_dp, n_ctx, flip))

    def later(flip):
        return ctx < ctx ^ flip

    kv, = run(join, "join", [(block, BF16)], (), (keys, values), [], 1)
    prev = lax.ppermute(kv, axes, run_route(n_dp, n_ctx))
    kv_own, q_s, q_t, do_r, start, level, p_own, acc = kernel(
        prepare, [(kv_ones, BF16), (by_row, BF16), (by_lane, BF16), (by_row, BF16), ((rows, rows), jnp.int32), (by_row, F32),
                  ((many, rows), BF16), ((many, 2 * HDIM), F32)],
        scalars, (queries, grad_out, kv), [], 2 * once)
    sent = [jnp.where(later(max(2 * i, 1)), kv_own[:, :2 * HDIM], prev) for i in range(pairs)]
    direct = [swap(sent[i], 2 * i) for i in range(1, pairs)]
    passed = swap(jnp.stack([sent[0]] + direct), 1)
    kv_even, p_even, acc = kernel(
        attend_even, [((pairs,) + kv_ones, BF16), ((pairs, many, rows), BF16), ((many, 2 * HDIM), F32)],
        scalars, (q_s, start, level, acc, prev, direct), [], 2 * pairs * once)
    attn_out, kv_odd, ds_odd, do_s, do_t, corr, g_passed, p_own, p_even = kernel(
        forward,
        [(queries.shape, BF16), ((pairs,) + kv_ones, BF16), ((pairs, many, rows), BF16),
         (by_row, BF16), (by_lane, BF16), (by_row, F32), ((pairs,) + block, BF16), (p_own.shape, BF16), (p_even.shape, BF16)],
        scalars, (q_s, q_t, do_r, start, level, acc, kv_own, kv_even, passed, p_own, p_even),
        [pltpu.VMEM((pairs, many, rows), BF16), pltpu.VMEM((many, 2 * HDIM), F32), pltpu.VMEM(by_row, F32),
         pltpu.VMEM((many, rows), BF16), pltpu.SemaphoreType.DMA],
        5 * pairs * once, aliases=((9, 7), (10, 8)))
    partner = swap(g_passed, 1).astype(F32)
    shared = (q_t, do_s, do_t, kv_even, p_even, corr)
    ds_even, g_direct = kernel(even, [((pairs - 1, many, rows), BF16), ((pairs - 1,) + block, F32)],
                               scalars, shared, [], 3 * (pairs - 1) * once)
    terms = [partner[0]] + [swap((g_direct[i - 1] + partner[i]).astype(BF16), 2 * i).astype(F32) for i in range(1, pairs)]
    grad_queries, g_own, g_prev = kernel(rest, [(queries.shape, BF16), (block, F32), (block, F32)],
                                         scalars, shared + (kv_own, p_own, kv_odd, ds_odd, ds_even),
                                         [pltpu.VMEM(by_row, F32)], (n_ctx + 7) * once)
    own_total, prev_total = g_own, g_prev
    for i in range(pairs):
        ours = later(max(2 * i, 1))
        own_total = own_total + jnp.where(ours, terms[i], 0.0)
        prev_total = prev_total + jnp.where(ours, 0.0, terms[i])
    back = [(b, a) for a, b in run_route(n_dp, n_ctx)]
    last = lax.ppermute(prev_total.astype(BF16), axes, back)
    grad_keys, grad_values = run(finish, "finish", [(keys.shape, BF16), (values.shape, BF16)], (), (own_total, last), [], 1)
    return (attn_out, grad_queries, grad_keys, grad_values)


def solution(mesh):
    tokens = P(("dp", "ctx"), None)
    return jax.shard_map(
        shards,
        mesh=mesh,
        in_specs=(tokens, tokens, tokens, tokens, P()),
        out_specs=(tokens, tokens, tokens, tokens),
        check_vma=False,
    )
```

```python
import functools
import math

import jax
import jax.numpy as jnp
from jax import lax
from jax.experimental import pallas as pl
from jax.experimental.pallas import tpu as pltpu
from jax.sharding import PartitionSpec as P

HEADS = 8
HDIM = 128
NEG_FILL = -1e30
SCALE = float(HDIM) ** -0.5
EXP2_SCALE = SCALE * math.log2(math.e)

NT = (((1,), (1,)), ((), ()))
NN = (((1,), (0,)), ((), ()))
F32, BF16 = jnp.float32, jnp.bfloat16


def dot(a, b, dims=NN):
    return lax.dot_general(a, b, dims, preferred_element_type=F32)


def wide(column):
    return jnp.concatenate([column, column], axis=1)


def run_route(n_dp, n_ctx):
    return [(d * n_ctx + c, (d + 1) * n_ctx + c) for d in range(n_dp - 1) for c in range(n_ctx)]


def flip_route(n_dp, n_ctx, flip):
    return [(d * n_ctx + c, d * n_ctx + (c ^ flip)) for d in range(n_dp) for c in range(n_ctx)]


def facts_of(n_ctx, rows, index, lengths_ref):
    base = index * rows
    ends, end = [], jnp.int32(0)
    for i in range(lengths_ref.shape[0]):
        end = end + lengths_ref[i]
        ends.append(end)
    low, high = jnp.int32(0), ends[-1]
    for end in ends:
        low = jnp.where(end <= base, end, low)
    for end in reversed(ends):
        high = jnp.where(end > base, end, high)
    before = lax.div(base - low + rows - 1, rows)
    short = (high - base <= rows - rows // n_ctx).astype(jnp.int32)
    return (lax.rem(index, n_ctx), base, before, short), ends


class Place:
    def __init__(self, n_ctx, rows, facts):
        self.n_ctx, self.rows = n_ctx, rows
        self.ctx, self.base, self.before, short = facts if isinstance(facts, tuple) else (facts[i, 0] for i in range(4))
        self.short = short == 1

    def chip(self, back):
        return lax.div(lax.rem(self.ctx - back + 2 * self.n_ctx, self.n_ctx), 2)

    def past(self, backs, body):
        first, step = backs[0], backs.step
        count = jnp.clip(lax.div(self.before - first + step, step), 0, len(backs))
        for short in (True, False):

            @pl.when(self.short if short else jnp.logical_not(self.short))
            def _():
                @pl.loop(0, count)
                def _(i):
                    body(first + i * step, HEADS * (self.rows - self.rows // self.n_ctx if short else self.rows))

        return count


def chunks(rows, n_ctx):
    size = rows // n_ctx
    for c in range(n_ctx):
        for h in range(HEADS):
            yield (pl.ds((c * HEADS + h) * size, size), (pl.ds(c * size, size), pl.ds(h * HDIM, HDIM)))


def fetch(pairs, sems):
    copies = [pltpu.make_async_copy(source, target, sems.at[i]) for i, (source, target) in enumerate(pairs)]
    for copy in copies:
        copy.start()
    return copies


def join(keys, values, kv, sems):
    for copy in fetch([(keys, kv.at[:, pl.ds(0, HDIM)]), (values, kv.at[:, pl.ds(HDIM, HDIM)])], sems):
        copy.wait()


def with_ones(kv):
    return jnp.concatenate([kv, jnp.ones((kv.shape[0], HDIM), BF16)], axis=1)


def levels(place, back, many, q_s, key_block, start):
    size, rows = place.rows // place.n_ctx, place.rows
    tokens = many // HEADS
    key = place.base - back * rows + lax.broadcasted_iota(jnp.int32, (tokens, rows), 1)
    query = place.base + lax.broadcasted_iota(jnp.int32, (tokens, rows), 0)
    off = jnp.where((key >= start[:tokens, :]) & (key <= query), 0.0, NEG_FILL)
    s = dot(q_s[:many, :], key_block, NT) * EXP2_SCALE
    s = s.reshape(tokens // size, HEADS, size, rows) + off.reshape(tokens // size, 1, size, rows)
    return s.reshape(many, rows)


def fold(s):
    return jnp.maximum(s[:, :HDIM], s[:, HDIM:])


def row_max(s):
    return jnp.broadcast_to(jnp.max(s, axis=1, keepdims=True), (s.shape[0], HDIM))


def prepare(n_ctx, lengths_hbm, q_hbm, do_hbm, kv_ref, facts_ref, kv_own, q_s, q_t, do_r, start, level, p_own, acc,
            lengths_ref, q_ref, do_ref, sems):
    copies = fetch([(lengths_hbm, lengths_ref), (q_hbm, q_ref), (do_hbm, do_ref)], sems)
    rows = q_ref.shape[0]
    index = lax.axis_index("dp") * n_ctx + lax.axis_index("ctx")
    kv_own[...] = with_ones(kv_ref[...])
    copies[0].wait()
    facts, ends = facts_of(n_ctx, rows, index, lengths_ref)
    place = Place(n_ctx, rows, facts)
    line = lax.broadcasted_iota(jnp.int32, facts_ref.shape, 0)
    held = jnp.zeros(facts_ref.shape, jnp.int32)
    for i, fact in enumerate(facts):
        held = jnp.where(line == i, fact, held)
    facts_ref[...] = held
    token = place.base + lax.broadcasted_iota(jnp.int32, (rows, HDIM), 0)
    begin = jnp.zeros((rows, HDIM), jnp.int32)
    for end in ends:
        begin = jnp.where(token >= end, end, begin)
    start[...] = wide(begin) if rows == 2 * HDIM else jnp.broadcast_to(begin[:, :1], (rows, rows))
    copies[1].wait()
    for here, there in chunks(rows, n_ctx):
        q_s[here, :] = q_ref[there]
    s = levels(place, 0, HEADS * rows, q_s, kv_own[:, :HDIM], start)
    top = row_max(fold(s))
    level[...] = top
    p = jnp.exp2(s - wide(top)).astype(BF16)
    p_own[...] = p
    acc[...] = dot(p, kv_own[:, HDIM:])
    copies[2].wait()
    for here, there in chunks(rows, n_ctx):
        do_r[here, :] = do_ref[there]
    for h in range(HEADS):
        here = pl.ds(h * rows, rows)
        q_t[:, here] = q_s[here, :].astype(F32).T.astype(BF16)


def attend(place, back, many, q_s, kv, start, level, acc, probs):
    p = jnp.exp2(levels(place, back, many, q_s, kv[:, :HDIM], start) - wide(level[:many, :])).astype(BF16)
    probs[:many, :] = p
    acc[:many, :] += dot(p, kv[:, HDIM:])


def attend_even(n_ctx, facts, q_s, start, level, acc_in, kv_got, kv_even, p_even, acc):
    rows = kv_got.shape[1]
    place = Place(n_ctx, rows, facts)
    for i in range(n_ctx // 2):
        kv_even[i] = with_ones(kv_got[i])
    acc[...] = acc_in[...]

    def body(back, many):
        attend(place, back, many, q_s, kv_even.at[place.chip(back)], start, level, acc, p_even.at[lax.div(back, 2) - 1])

    place.past(range(2, n_ctx + 1, 2), body)


def dscore(many, do_s, p, kv, corr):
    d = dot(do_s[:many, :], kv[:, HDIM:2 * HDIM], NT) - wide(corr[:many, :])
    return (p.astype(F32) * d).astype(BF16)


def key_value_terms(many, q_t, do_t, ds, p):
    return jnp.concatenate([dot(q_t[:, :many], ds).T, dot(do_t[:, :many], p).T], axis=1)


def forward(n_ctx, facts, q_s, q_t, do_r, start, level, acc_in, kv_own, kv_even, kv_passed, p_own_in, p_even_in,
            o_hbm, kv_odd, ds_odd, do_s, do_t, corr, g_passed, p_own, p_even, o_ref, p_odd, acc, top, p_new, sems):
    rows = o_ref.shape[0]
    size = rows // n_ctx
    place = Place(n_ctx, rows, facts)
    pairs = n_ctx // 2
    everything = HEADS * rows
    odd_backs, even_backs = range(1, n_ctx, 2), range(2, n_ctx + 1, 2)
    del p_own_in, p_even_in

    for i in range(pairs):
        kv_odd[i] = with_ones(kv_passed[i])

    def odd(back):
        return kv_odd.at[place.chip(back)]

    def even(back):
        return kv_even.at[place.chip(back)]

    acc[...] = acc_in[...]
    place.past(odd_backs, lambda back, many: attend(place, back, many, q_s, odd(back), start, level, acc, p_odd.at[lax.div(back, 2)]))

    @pl.when(jnp.logical_not(jnp.max(acc[:, HDIM:]) < 2.0 ** 40))
    def _():
        def raise_top(back, many, kv):
            top[:many, :] = jnp.maximum(top[:many, :], fold(levels(place, back, many, q_s, kv[:, :HDIM], start)))

        top[...] = jnp.full(top.shape, NEG_FILL, F32)
        raise_top(0, everything, kv_own)
        place.past(odd_backs, lambda back, many: raise_top(back, many, odd(back)))
        place.past(even_backs, lambda back, many: raise_top(back, many, even(back)))
        top[...] = row_max(top[...])
        acc[...] = jnp.zeros(acc.shape, F32)

        def replace(back, many, kv, probs):
            attend(place, back, many, q_s, kv, start, top, acc, p_new)
            copy = pltpu.make_async_copy(p_new.at[pl.ds(0, many)], probs.at[pl.ds(0, many)], sems.at[0])
            copy.start()
            copy.wait()

        replace(0, everything, kv_own, p_own)
        place.past(even_backs, lambda back, many: replace(back, many, even(back), p_even.at[lax.div(back, 2) - 1]))
        place.past(odd_backs, lambda back, many: attend(place, back, many, q_s, odd(back), start, top, acc, p_odd.at[lax.div(back, 2)]))

    for i in range(0, everything, rows):
        here = pl.ds(i, rows)
        total = acc[here, :]
        inverse = 1.0 / total[:, HDIM:]
        out = (total[:, :HDIM] * inverse).astype(BF16)
        grad = do_r[here, :].astype(F32)
        corr[here, :] = jnp.sum(grad * out.astype(F32), axis=1, keepdims=True) * inverse
        scaled = grad * inverse
        do_s[here, :] = scaled.astype(BF16)
        do_t[:, here] = scaled.T.astype(BF16)
        for part, there in chunks(rows, n_ctx):
            if i <= part.start < i + rows:
                o_ref[there] = out[part.start - i:part.start - i + size, :]

    leaving = pltpu.make_async_copy(o_ref, o_hbm, sems.at[1])
    leaving.start()

    def backward(back, many):
        p = p_odd[lax.div(back, 2), :many, :]
        ds_odd[lax.div(back, 2), :many, :] = ds = dscore(many, do_s, p, odd(back), corr)
        g_passed[place.chip(back)] = key_value_terms(many, q_t, do_t, ds, p).astype(BF16)

    done = place.past(odd_backs, backward)

    @pl.loop(done, pairs)
    def _(i):
        g_passed[place.chip(2 * i + 1)] = jnp.zeros((rows, 2 * HDIM), BF16)

    leaving.wait()


def even(n_ctx, facts, q_t, do_s, do_t, kv_even, p_even, corr, ds_even, g_direct):
    rows = kv_even.shape[1]
    place = Place(n_ctx, rows, facts)

    def backward(back, many):
        at = place.chip(back)
        p = p_even[lax.div(back, 2) - 1, :many, :]
        ds_even[lax.div(back, 2) - 1, :many, :] = ds = dscore(many, do_s, p, kv_even.at[at], corr)
        g_direct[at] = key_value_terms(many, q_t, do_t, ds, p)

    done = place.past(range(2, n_ctx, 2), backward)

    @pl.loop(done, n_ctx // 2)
    def _(i):
        g_direct[place.chip(2 * i + 2)] = jnp.zeros((rows, 2 * HDIM), F32)


def rest(n_ctx, facts, q_t, do_s, do_t, kv_even, p_even, corr, kv_own, p_own, kv_odd, ds_odd, ds_even,
         dq_ref, g_own, g_prev, dq_acc):
    rows = kv_own.shape[0]
    place = Place(n_ctx, rows, facts)

    p = p_own[...]
    ds = dscore(HEADS * rows, do_s, p, kv_own, corr)
    g_own[...] = key_value_terms(HEADS * rows, q_t, do_t, ds, p)
    dq_acc[...] = dot(ds, kv_own[:, :HDIM])

    def add_odd(back, many):
        dq_acc[:many, :] += dot(ds_odd[lax.div(back, 2), :many, :], kv_odd[place.chip(back), :, :HDIM])

    def add_even(back, many):
        dq_acc[:many, :] += dot(ds_even[lax.div(back, 2) - 1, :many, :], kv_even[place.chip(back), :, :HDIM])

    def farthest(back, many):
        p = p_even[n_ctx // 2 - 1, :many, :]
        at = place.chip(back)
        ds = dscore(many, do_s, p, kv_even.at[at], corr)
        g_prev[...] = key_value_terms(many, q_t, do_t, ds, p)
        dq_acc[:many, :] += dot(ds, kv_even[at, :, :HDIM])

    place.past(range(1, n_ctx, 2), add_odd)
    place.past(range(2, n_ctx, 2), add_even)
    g_prev[...] = jnp.zeros(g_prev.shape, F32)
    place.past(range(n_ctx, n_ctx + 1), farthest)

    for here, there in chunks(rows, n_ctx):
        dq_ref[there] = (dq_acc[here, :] * SCALE).astype(BF16)


def finish(total, last, gk_ref, gv_ref):
    terms = total[...] + last[...].astype(F32)
    gk_ref[...] = (terms[:, :HDIM] * SCALE).astype(BF16)
    gv_ref[...] = terms[:, HDIM:].astype(BF16)


def size_of(arrays):
    return sum(math.prod(array.shape) * jnp.dtype(array.dtype).itemsize for array in arrays)


def call(body, name, outs, args, scratch, flops, resident, aliases=(), away=(), leaves=(), copies=0):
    vmem = pl.BlockSpec(memory_space=pltpu.VMEM)
    anywhere = pl.BlockSpec(memory_space=pl.ANY)
    hbm = pl.BlockSpec(memory_space=pltpu.HBM)
    outs = tuple(jax.ShapeDtypeStruct(shape, dtype) for shape, dtype in outs)
    held = size_of(scratch) + 8 * 2**20
    if not resident:
        held = min(held + size_of(outs) + size_of(args), 62 * 2**20)
    in_specs, out_specs = [vmem] * len(args), [vmem] * len(outs)
    for i in away:
        in_specs[i] = hbm
    for o in leaves:
        out_specs[o] = hbm
    for i, o in aliases:
        in_specs[i] = out_specs[o] = anywhere
    return pl.pallas_call(
        body,
        out_shape=outs,
        in_specs=in_specs,
        out_specs=tuple(out_specs),
        scratch_shapes=scratch + [pltpu.SemaphoreType.DMA((copies,))] * (copies > 0),
        input_output_aliases=dict(aliases),
        compiler_params=pltpu.CompilerParams(vmem_limit_bytes=held),
        cost_estimate=pl.CostEstimate(flops=flops, bytes_accessed=2**20, transcendentals=0),
        name=name,
    )(*(pltpu.with_memory_space_constraint(arg, pltpu.HBM) if i in away else arg for i, arg in enumerate(args)))


def shards(queries, keys, values, grad_out, lengths):
    rows = keys.shape[0]
    n_dp, n_ctx = lax.axis_size("dp"), lax.axis_size("ctx")
    axes = ("dp", "ctx")
    pairs = n_ctx // 2
    ctx = lax.axis_index("ctx")
    many = HEADS * rows
    once = 2 * many * rows * HDIM
    by_row, by_lane = (many, HDIM), (HDIM, many)
    block, kv_ones = (rows, 2 * HDIM), (rows, 3 * HDIM)
    run = functools.partial(call, resident=(n_ctx + 1) * many * rows <= 6 * 2**20)
    chip, chips = ctx // 2, lax.broadcasted_iota(jnp.int32, (pairs, 1, 1), 0)
    groups = [list(range(core, n_ctx, 2)) for core in range(2)]

    def kernel(body, *args, **kwargs):
        return run(functools.partial(body, n_ctx), body.__name__, *args, **kwargs)

    def across(blocks):
        return lax.all_to_all(blocks, "ctx", 0, 0, axis_index_groups=groups, tiled=True)

    def swap(blocks):
        return lax.ppermute(blocks, axes, flip_route(n_dp, n_ctx, 1))

    kv, = run(join, "join", [(block, BF16)], (keys, values), [], 1, away=(0, 1), copies=2)
    prev = lax.ppermute(kv, axes, run_route(n_dp, n_ctx))
    facts, kv_own, q_s, q_t, do_r, start, level, p_own, acc = kernel(
        prepare, [((8, HDIM), jnp.int32), (kv_ones, BF16), (by_row, BF16), (by_lane, BF16), (by_row, BF16),
                  ((rows, rows), jnp.int32), (by_row, F32), ((many, rows), BF16), ((many, 2 * HDIM), F32)],
        (lengths, queries, grad_out, kv),
        [pltpu.SMEM(lengths.shape, jnp.int32), pltpu.VMEM(queries.shape, BF16), pltpu.VMEM(queries.shape, BF16)], 2 * once,
        away=(0, 1, 2), copies=3)
    ours = kv_own[:, :2 * HDIM]
    got = across(jnp.where(chips > chip, ours, prev))
    passed = swap(jnp.where((chips == chip) & (ctx % 2 == 0), ours, got))
    kv_even, p_even, acc = kernel(
        attend_even, [((pairs,) + kv_ones, BF16), ((pairs, many, rows), BF16), ((many, 2 * HDIM), F32)],
        (facts, q_s, start, level, acc, got), [], 2 * pairs * once)
    attn_out, kv_odd, ds_odd, do_s, do_t, corr, g_passed, p_own, p_even = kernel(
        forward,
        [(queries.shape, BF16), ((pairs,) + kv_ones, BF16), ((pairs, many, rows), BF16),
         (by_row, BF16), (by_lane, BF16), (by_row, F32), ((pairs,) + block, BF16), (p_own.shape, BF16), (p_even.shape, BF16)],
        (facts, q_s, q_t, do_r, start, level, acc, kv_own, kv_even, passed, p_own, p_even),
        [pltpu.VMEM(queries.shape, BF16), pltpu.VMEM((pairs, many, rows), BF16), pltpu.VMEM((many, 2 * HDIM), F32),
         pltpu.VMEM(by_row, F32), pltpu.VMEM((many, rows), BF16)],
        5 * pairs * once, aliases=((10, 7), (11, 8)), leaves=(0,), copies=2)
    partner = swap(g_passed)
    shared = (facts, q_t, do_s, do_t, kv_even, p_even, corr)
    ds_even, g_direct = kernel(even, [((pairs - 1, many, rows), BF16), ((pairs,) + block, F32)],
                               shared, [], 3 * (pairs - 1) * once)
    terms = across((g_direct + partner.astype(F32)).astype(BF16)).astype(F32)
    grad_queries, g_own, g_prev = kernel(rest, [(queries.shape, BF16), (block, F32), (block, F32)],
                                         shared + (kv_own, p_own, kv_odd, ds_odd, ds_even),
                                         [pltpu.VMEM(by_row, F32)], (n_ctx + 7) * once)
    after = (chips > chip) | ((chips == chip) & (ctx % 2 == 0))
    own_total = g_own + jnp.sum(jnp.where(after, terms, 0.0), axis=0)
    prev_total = g_prev + jnp.sum(jnp.where(after, 0.0, terms), axis=0)
    back = [(b, a) for a, b in run_route(n_dp, n_ctx)]
    last = lax.ppermute(prev_total.astype(BF16), axes, back)
    grad_keys, grad_values = run(finish, "finish", [(keys.shape, BF16), (values.shape, BF16)], (own_total, last), [], 1)
    return (attn_out, grad_queries, grad_keys, grad_values)


def solution(mesh):
    tokens = P(("dp", "ctx"), None)
    return jax.shard_map(
        shards,
        mesh=mesh,
        in_specs=(tokens, tokens, tokens, tokens, P()),
        out_specs=(tokens, tokens, tokens, tokens),
        check_vma=False,
    )
```

```python
import functools
import math

import jax
import jax.numpy as jnp
from jax import lax
from jax.experimental import pallas as pl
from jax.experimental.pallas import tpu as pltpu
from jax.sharding import PartitionSpec as P

HEADS = 8
HDIM = 128
NEG_FILL = -1e30
SCALE = float(HDIM) ** -0.5
EXP2_SCALE = SCALE * math.log2(math.e)

NT = (((1,), (1,)), ((), ()))
NN = (((1,), (0,)), ((), ()))
F32, BF16 = jnp.float32, jnp.bfloat16


def dot(a, b, dims=NN):
    return lax.dot_general(a, b, dims, preferred_element_type=F32)


def wide(column):
    return jnp.concatenate([column, column], axis=1)


def run_route(n_dp, n_ctx):
    return [(d * n_ctx + c, (d + 1) * n_ctx + c) for d in range(n_dp - 1) for c in range(n_ctx)]


def flip_route(n_dp, n_ctx, flip):
    return [(d * n_ctx + c, d * n_ctx + (c ^ flip)) for d in range(n_dp) for c in range(n_ctx)]


def facts_of(n_ctx, rows, index, lengths_ref):
    base = index * rows
    ends, end = [], jnp.int32(0)
    for i in range(lengths_ref.shape[0]):
        end = end + lengths_ref[i]
        ends.append(end)
    low, high = jnp.int32(0), ends[-1]
    for end in ends:
        low = jnp.where(end <= base, end, low)
    for end in reversed(ends):
        high = jnp.where(end > base, end, high)
    before = lax.div(base - low + rows - 1, rows)
    short = (high - base <= rows - rows // n_ctx).astype(jnp.int32)
    return (lax.rem(index, n_ctx), base, before, short), ends


class Place:
    def __init__(self, n_ctx, rows, facts):
        self.n_ctx, self.rows = n_ctx, rows
        self.ctx, self.base, self.before, short = facts if isinstance(facts, tuple) else (facts[i, 0] for i in range(4))
        self.short = short == 1

    def hop(self, back):
        return lax.div(self.ctx ^ lax.rem(self.ctx - back + 2 * self.n_ctx, self.n_ctx), 2)

    def past(self, backs, body):
        first, step = backs[0], backs.step
        count = jnp.clip(lax.div(self.before - first + step, step), 0, len(backs))
        for short in (True, False):

            @pl.when(self.short if short else jnp.logical_not(self.short))
            def _():
                @pl.loop(0, count)
                def _(i):
                    body(first + i * step, HEADS * (self.rows - self.rows // self.n_ctx if short else self.rows))

        return count


def chunks(rows, n_ctx):
    size = rows // n_ctx
    for c in range(n_ctx):
        for h in range(HEADS):
            yield (pl.ds((c * HEADS + h) * size, size), (pl.ds(c * size, size), pl.ds(h * HDIM, HDIM)))


def fetch(pairs, sems):
    copies = [pltpu.make_async_copy(source, target, sems.at[i]) for i, (source, target) in enumerate(pairs)]
    for copy in copies:
        copy.start()
    return copies


def join(keys, values, kv, sems):
    for copy in fetch([(keys, kv.at[:, pl.ds(0, HDIM)]), (values, kv.at[:, pl.ds(HDIM, HDIM)])], sems):
        copy.wait()


def with_ones(kv):
    return jnp.concatenate([kv, jnp.ones((kv.shape[0], HDIM), BF16)], axis=1)


def levels(place, back, many, q_s, key_block, start):
    size, rows = place.rows // place.n_ctx, place.rows
    tokens = many // HEADS
    key = place.base - back * rows + lax.broadcasted_iota(jnp.int32, (tokens, rows), 1)
    query = place.base + lax.broadcasted_iota(jnp.int32, (tokens, rows), 0)
    off = jnp.where((key >= start[:tokens, :]) & (key <= query), 0.0, NEG_FILL)
    s = dot(q_s[:many, :], key_block, NT) * EXP2_SCALE
    s = s.reshape(tokens // size, HEADS, size, rows) + off.reshape(tokens // size, 1, size, rows)
    return s.reshape(many, rows)


def fold(s):
    return jnp.maximum(s[:, :HDIM], s[:, HDIM:])


def row_max(s):
    return jnp.broadcast_to(jnp.max(s, axis=1, keepdims=True), (s.shape[0], HDIM))


def prepare(n_ctx, lengths_hbm, q_hbm, do_hbm, kv_ref, facts_ref, kv_own, q_s, q_t, do_r, start, level, p_own, acc,
            lengths_ref, q_ref, do_ref, sems):
    copies = fetch([(lengths_hbm, lengths_ref), (q_hbm, q_ref), (do_hbm, do_ref)], sems)
    rows = q_ref.shape[0]
    index = lax.axis_index("dp") * n_ctx + lax.axis_index("ctx")
    kv_own[...] = with_ones(kv_ref[...])
    copies[0].wait()
    facts, ends = facts_of(n_ctx, rows, index, lengths_ref)
    place = Place(n_ctx, rows, facts)
    line = lax.broadcasted_iota(jnp.int32, facts_ref.shape, 0)
    held = jnp.zeros(facts_ref.shape, jnp.int32)
    for i, fact in enumerate(facts):
        held = jnp.where(line == i, fact, held)
    facts_ref[...] = held
    token = place.base + lax.broadcasted_iota(jnp.int32, (rows, HDIM), 0)
    begin = jnp.zeros((rows, HDIM), jnp.int32)
    for end in ends:
        begin = jnp.where(token >= end, end, begin)
    start[...] = wide(begin) if rows == 2 * HDIM else jnp.broadcast_to(begin[:, :1], (rows, rows))
    copies[1].wait()
    for here, there in chunks(rows, n_ctx):
        q_s[here, :] = q_ref[there]
    s = levels(place, 0, HEADS * rows, q_s, kv_own[:, :HDIM], start)
    top = row_max(fold(s))
    level[...] = top
    p = jnp.exp2(s - wide(top)).astype(BF16)
    p_own[...] = p
    acc[...] = dot(p, kv_own[:, HDIM:])
    copies[2].wait()
    for here, there in chunks(rows, n_ctx):
        do_r[here, :] = do_ref[there]
    for h in range(HEADS):
        here = pl.ds(h * rows, rows)
        q_t[:, here] = q_s[here, :].astype(F32).T.astype(BF16)


def attend(place, back, many, q_s, kv, start, level, acc, probs):
    p = jnp.exp2(levels(place, back, many, q_s, kv[:, :HDIM], start) - wide(level[:many, :])).astype(BF16)
    probs[:many, :] = p
    acc[:many, :] += dot(p, kv[:, HDIM:])


def attend_even(n_ctx, facts, q_s, start, level, acc_in, *refs):
    *got, kv_even, p_even, acc = refs
    rows = got[0].shape[0]
    place = Place(n_ctx, rows, facts)
    for i, ref in enumerate(got):
        kv_even[i] = with_ones(ref[...])
    acc[...] = acc_in[...]

    def body(back, many):
        attend(place, back, many, q_s, kv_even.at[place.hop(back)], start, level, acc, p_even.at[lax.div(back, 2) - 1])

    place.past(range(2, n_ctx + 1, 2), body)


def gradients(many, q_t, do_s, do_t, p, kv, corr):
    d = dot(do_s[:many, :], kv[:, HDIM:2 * HDIM], NT)
    dv = dot(do_t[:, :many], p)
    ds = (p.astype(F32) * (d - wide(corr[:many, :]))).astype(BF16)
    dk = dot(q_t[:, :many], ds)
    return ds, jnp.concatenate([dk.T, dv.T], axis=1)


def forward(n_ctx, facts, q_s, q_t, do_r, start, level, acc_in, kv_own, kv_even, kv_passed, p_own_in, p_even_in,
            o_hbm, kv_odd, ds_odd, do_s, do_t, corr, g_passed, p_own, p_even, o_ref, p_odd, acc, top, p_new, sems):
    rows = o_ref.shape[0]
    size = rows // n_ctx
    place = Place(n_ctx, rows, facts)
    pairs = n_ctx // 2
    everything = HEADS * rows
    odd_backs, even_backs = range(1, n_ctx, 2), range(2, n_ctx + 1, 2)
    del p_own_in, p_even_in

    for i in range(pairs):
        kv_odd[i] = with_ones(kv_passed[i])

    def odd(back):
        return kv_odd.at[place.hop(back)]

    def even(back):
        return kv_even.at[place.hop(back)]

    acc[...] = acc_in[...]
    place.past(odd_backs, lambda back, many: attend(place, back, many, q_s, odd(back), start, level, acc, p_odd.at[lax.div(back, 2)]))

    @pl.when(jnp.logical_not(jnp.max(acc[:, HDIM:]) < 2.0 ** 40))
    def _():
        def raise_top(back, many, kv):
            top[:many, :] = jnp.maximum(top[:many, :], fold(levels(place, back, many, q_s, kv[:, :HDIM], start)))

        top[...] = jnp.full(top.shape, NEG_FILL, F32)
        raise_top(0, everything, kv_own)
        place.past(odd_backs, lambda back, many: raise_top(back, many, odd(back)))
        place.past(even_backs, lambda back, many: raise_top(back, many, even(back)))
        top[...] = row_max(top[...])
        acc[...] = jnp.zeros(acc.shape, F32)

        def replace(back, many, kv, probs):
            attend(place, back, many, q_s, kv, start, top, acc, p_new)
            copy = pltpu.make_async_copy(p_new.at[pl.ds(0, many)], probs.at[pl.ds(0, many)], sems.at[0])
            copy.start()
            copy.wait()

        replace(0, everything, kv_own, p_own)
        place.past(even_backs, lambda back, many: replace(back, many, even(back), p_even.at[lax.div(back, 2) - 1]))
        place.past(odd_backs, lambda back, many: attend(place, back, many, q_s, odd(back), start, top, acc, p_odd.at[lax.div(back, 2)]))

    for i in range(0, everything, rows):
        here = pl.ds(i, rows)
        total = acc[here, :]
        inverse = 1.0 / total[:, HDIM:]
        out = (total[:, :HDIM] * inverse).astype(BF16)
        grad = do_r[here, :].astype(F32)
        corr[here, :] = jnp.sum(grad * out.astype(F32), axis=1, keepdims=True) * inverse
        scaled = grad * inverse
        do_s[here, :] = scaled.astype(BF16)
        do_t[:, here] = scaled.T.astype(BF16)
        for part, there in chunks(rows, n_ctx):
            if i <= part.start < i + rows:
                o_ref[there] = out[part.start - i:part.start - i + size, :]

    leaving = pltpu.make_async_copy(o_ref, o_hbm, sems.at[1])
    leaving.start()

    def backward(back, many):
        p = p_odd[lax.div(back, 2), :many, :]
        ds_odd[lax.div(back, 2), :many, :], terms = gradients(many, q_t, do_s, do_t, p, odd(back), corr)
        g_passed[place.hop(back)] = terms.astype(BF16)

    done = place.past(odd_backs, backward)

    @pl.loop(done, pairs)
    def _(i):
        g_passed[place.hop(2 * i + 1)] = jnp.zeros((rows, 2 * HDIM), BF16)

    leaving.wait()


def even(n_ctx, facts, q_t, do_s, do_t, kv_even, p_even, corr, ds_even, g_direct):
    rows = kv_even.shape[1]
    place = Place(n_ctx, rows, facts)

    def backward(back, many):
        at = place.hop(back)
        p = p_even[lax.div(back, 2) - 1, :many, :]
        ds_even[lax.div(back, 2) - 1, :many, :], g_direct[at - 1] = gradients(many, q_t, do_s, do_t, p, kv_even.at[at], corr)

    done = place.past(range(2, n_ctx, 2), backward)

    @pl.loop(done, n_ctx // 2 - 1)
    def _(i):
        g_direct[place.hop(2 * i + 2) - 1] = jnp.zeros((rows, 2 * HDIM), F32)


def rest(n_ctx, facts, q_t, do_s, do_t, kv_even, p_even, corr, kv_own, p_own, kv_odd, ds_odd, ds_even,
         dq_ref, g_own, g_prev, dq_acc):
    rows = kv_own.shape[0]
    place = Place(n_ctx, rows, facts)

    p = p_own[...]
    ds, g_own[...] = gradients(HEADS * rows, q_t, do_s, do_t, p, kv_own, corr)
    dq_acc[...] = dot(ds, kv_own[:, :HDIM])

    def add_odd(back, many):
        dq_acc[:many, :] += dot(ds_odd[lax.div(back, 2), :many, :], kv_odd[place.hop(back), :, :HDIM])

    def add_even(back, many):
        dq_acc[:many, :] += dot(ds_even[lax.div(back, 2) - 1, :many, :], kv_even[place.hop(back), :, :HDIM])

    def farthest(back, many):
        p = p_even[n_ctx // 2 - 1, :many, :]
        at = place.hop(back)
        ds, g_prev[...] = gradients(many, q_t, do_s, do_t, p, kv_even.at[at], corr)
        dq_acc[:many, :] += dot(ds, kv_even[at, :, :HDIM])

    place.past(range(1, n_ctx, 2), add_odd)
    place.past(range(2, n_ctx, 2), add_even)
    g_prev[...] = jnp.zeros(g_prev.shape, F32)
    place.past(range(n_ctx, n_ctx + 1), farthest)

    for here, there in chunks(rows, n_ctx):
        dq_ref[there] = (dq_acc[here, :] * SCALE).astype(BF16)


def finish(total, last, gk_ref, gv_ref):
    terms = total[...] + last[...].astype(F32)
    gk_ref[...] = (terms[:, :HDIM] * SCALE).astype(BF16)
    gv_ref[...] = terms[:, HDIM:].astype(BF16)


def size_of(arrays):
    return sum(math.prod(array.shape) * jnp.dtype(array.dtype).itemsize for array in arrays)


def call(body, name, outs, args, scratch, flops, resident, aliases=(), away=(), leaves=(), copies=0):
    vmem = pl.BlockSpec(memory_space=pltpu.VMEM)
    anywhere = pl.BlockSpec(memory_space=pl.ANY)
    hbm = pl.BlockSpec(memory_space=pltpu.HBM)
    outs = tuple(jax.ShapeDtypeStruct(shape, dtype) for shape, dtype in outs)
    held = size_of(scratch) + 8 * 2**20
    if not resident:
        held = min(held + size_of(outs) + size_of(args), 62 * 2**20)
    in_specs, out_specs = [vmem] * len(args), [vmem] * len(outs)
    for i in away:
        in_specs[i] = hbm
    for o in leaves:
        out_specs[o] = hbm
    for i, o in aliases:
        in_specs[i] = out_specs[o] = anywhere
    return pl.pallas_call(
        body,
        out_shape=outs,
        in_specs=in_specs,
        out_specs=tuple(out_specs),
        scratch_shapes=scratch + [pltpu.SemaphoreType.DMA((copies,))] * (copies > 0),
        input_output_aliases=dict(aliases),
        compiler_params=pltpu.CompilerParams(vmem_limit_bytes=held),
        cost_estimate=pl.CostEstimate(flops=flops, bytes_accessed=2**20, transcendentals=0),
        name=name,
    )(*(pltpu.with_memory_space_constraint(arg, pltpu.HBM) if i in away else arg for i, arg in enumerate(args)))


def shards(queries, keys, values, grad_out, lengths):
    rows = keys.shape[0]
    n_dp, n_ctx = lax.axis_size("dp"), lax.axis_size("ctx")
    axes = ("dp", "ctx")
    pairs = n_ctx // 2
    ctx = lax.axis_index("ctx")
    many = HEADS * rows
    once = 2 * many * rows * HDIM
    by_row, by_lane = (many, HDIM), (HDIM, many)
    block, kv_ones = (rows, 2 * HDIM), (rows, 3 * HDIM)
    run = functools.partial(call, resident=(n_ctx + 1) * many * rows <= 6 * 2**20)
    def kernel(body, *args, **kwargs):
        return run(functools.partial(body, n_ctx), body.__name__, *args, **kwargs)

    def swap(blocks, flip):
        return lax.ppermute(blocks, axes, flip_route(n_dp, n_ctx, flip))

    later = [ctx < ctx ^ max(2 * i, 1) for i in range(pairs)]

    kv, = run(join, "join", [(block, BF16)], (keys, values), [], 1, away=(0, 1), copies=2)
    prev = lax.ppermute(kv, axes, run_route(n_dp, n_ctx))
    facts, kv_own, q_s, q_t, do_r, start, level, p_own, acc = kernel(
        prepare, [((8, HDIM), jnp.int32), (kv_ones, BF16), (by_row, BF16), (by_lane, BF16), (by_row, BF16),
                  ((rows, rows), jnp.int32), (by_row, F32), ((many, rows), BF16), ((many, 2 * HDIM), F32)],
        (lengths, queries, grad_out, kv),
        [pltpu.SMEM(lengths.shape, jnp.int32), pltpu.VMEM(queries.shape, BF16), pltpu.VMEM(queries.shape, BF16)], 2 * once,
        away=(0, 1, 2), copies=3)
    ours = kv_own[:, :2 * HDIM]
    sent = [jnp.where(after, ours, prev) for after in later]
    got = [prev] + [swap(sent[i], 2 * i) for i in range(1, pairs)]
    passed = swap(jnp.stack(sent[:1] + got[1:]), 1)
    kv_even, p_even, acc = kernel(
        attend_even, [((pairs,) + kv_ones, BF16), ((pairs, many, rows), BF16), ((many, 2 * HDIM), F32)],
        (facts, q_s, start, level, acc, *got), [], 2 * pairs * once)
    attn_out, kv_odd, ds_odd, do_s, do_t, corr, g_passed, p_own, p_even = kernel(
        forward,
        [(queries.shape, BF16), ((pairs,) + kv_ones, BF16), ((pairs, many, rows), BF16),
         (by_row, BF16), (by_lane, BF16), (by_row, F32), ((pairs,) + block, BF16), (p_own.shape, BF16), (p_even.shape, BF16)],
        (facts, q_s, q_t, do_r, start, level, acc, kv_own, kv_even, passed, p_own, p_even),
        [pltpu.VMEM(queries.shape, BF16), pltpu.VMEM((pairs, many, rows), BF16), pltpu.VMEM((many, 2 * HDIM), F32),
         pltpu.VMEM(by_row, F32), pltpu.VMEM((many, rows), BF16)],
        5 * pairs * once, aliases=((10, 7), (11, 8)), leaves=(0,), copies=2)
    partner = swap(g_passed, 1).astype(F32)
    shared = (facts, q_t, do_s, do_t, kv_even, p_even, corr)
    ds_even, g_direct = kernel(even, [((pairs - 1, many, rows), BF16), ((pairs - 1,) + block, F32)],
                               shared, [], 3 * (pairs - 1) * once)
    terms = [partner[0]] + [swap((g_direct[i - 1] + partner[i]).astype(BF16), 2 * i).astype(F32) for i in range(1, pairs)]
    grad_queries, g_own, g_prev = kernel(rest, [(queries.shape, BF16), (block, F32), (block, F32)],
                                         shared + (kv_own, p_own, kv_odd, ds_odd, ds_even),
                                         [pltpu.VMEM(by_row, F32)], (n_ctx + 7) * once)
    own_total, prev_total = g_own, g_prev
    for after, term in zip(later, terms):
        own_total = own_total + jnp.where(after, term, 0.0)
        prev_total = prev_total + jnp.where(after, 0.0, term)
    back = [(b, a) for a, b in run_route(n_dp, n_ctx)]
    last = lax.ppermute(prev_total.astype(BF16), axes, back)
    grad_keys, grad_values = run(finish, "finish", [(keys.shape, BF16), (values.shape, BF16)], (own_total, last), [], 1)
    return (attn_out, grad_queries, grad_keys, grad_values)


def solution(mesh):
    tokens = P(("dp", "ctx"), None)
    return jax.shard_map(
        shards,
        mesh=mesh,
        in_specs=(tokens, tokens, tokens, tokens, P()),
        out_specs=(tokens, tokens, tokens, tokens),
        check_vma=False,
    )
```

```python
import functools
import math

import jax
import jax.numpy as jnp
from jax import lax
from jax.experimental import pallas as pl
from jax.experimental.pallas import tpu as pltpu
from jax.sharding import PartitionSpec as P

HEADS = 8
HDIM = 128
NEG_FILL = -1e30
SCALE = float(HDIM) ** -0.5
EXP2_SCALE = SCALE * math.log2(math.e)

NT = (((1,), (1,)), ((), ()))
NN = (((1,), (0,)), ((), ()))
F32, BF16 = jnp.float32, jnp.bfloat16


def dot(a, b, dims=NN):
    return lax.dot_general(a, b, dims, preferred_element_type=F32)


def wide(column):
    return jnp.concatenate([column, column], axis=1)


def run_route(n_dp, n_ctx):
    return [(d * n_ctx + c, (d + 1) * n_ctx + c) for d in range(n_dp - 1) for c in range(n_ctx)]


def flip_route(n_dp, n_ctx, flip):
    return [(d * n_ctx + c, d * n_ctx + (c ^ flip)) for d in range(n_dp) for c in range(n_ctx)]


def facts_of(n_ctx, rows, index, lengths_ref):
    base = index * rows
    ends, end = [], jnp.int32(0)
    for i in range(lengths_ref.shape[0]):
        end = end + lengths_ref[i]
        ends.append(end)
    low, high = jnp.int32(0), ends[-1]
    for end in ends:
        low = jnp.where(end <= base, end, low)
    for end in reversed(ends):
        high = jnp.where(end > base, end, high)
    before = lax.div(base - low + rows - 1, rows)
    short = (high - base <= rows - rows // n_ctx).astype(jnp.int32)
    return (lax.rem(index, n_ctx), base, before, short), ends


class Place:
    def __init__(self, n_ctx, rows, facts):
        self.n_ctx, self.rows = n_ctx, rows
        self.ctx, self.base, self.before, short = facts if isinstance(facts, tuple) else (facts[i, 0] for i in range(4))
        self.short = short == 1

    def hop(self, back):
        return lax.div(self.ctx ^ lax.rem(self.ctx - back + 2 * self.n_ctx, self.n_ctx), 2)

    def past(self, backs, body):
        first, step = backs[0], backs.step
        count = jnp.clip(lax.div(self.before - first + step, step), 0, len(backs))
        for short in (True, False):
            many = HEADS * (self.rows - self.rows // self.n_ctx if short else self.rows)
            fits = self.short if short else jnp.logical_not(self.short)

            if len(backs) > 1:

                @pl.when(fits)
                def _():
                    @pl.loop(0, lax.div(count, 2))
                    def _(i):
                        body((first + 2 * i * step, first + (2 * i + 1) * step), many)

            @pl.when(fits & (lax.rem(count, 2) == 1))
            def _():
                body((first + (count - 1) * step,), many)

        return count


def chunks(rows, n_ctx):
    size = rows // n_ctx
    for c in range(n_ctx):
        for h in range(HEADS):
            yield (pl.ds((c * HEADS + h) * size, size), (pl.ds(c * size, size), pl.ds(h * HDIM, HDIM)))


def fetch(pairs, sems):
    copies = [pltpu.make_async_copy(source, target, sems.at[i]) for i, (source, target) in enumerate(pairs)]
    for copy in copies:
        copy.start()
    return copies


def join(keys, values, kv, sems):
    for copy in fetch([(keys, kv.at[:, pl.ds(0, HDIM)]), (values, kv.at[:, pl.ds(HDIM, HDIM)])], sems):
        copy.wait()


def with_ones(kv):
    return jnp.concatenate([kv, jnp.ones((kv.shape[0], HDIM), BF16)], axis=1)


def levels(place, back, many, q_s, key_block, start):
    size, rows = place.rows // place.n_ctx, place.rows
    tokens = many // HEADS
    key = place.base - back * rows + lax.broadcasted_iota(jnp.int32, (tokens, rows), 1)
    query = place.base + lax.broadcasted_iota(jnp.int32, (tokens, rows), 0)
    off = jnp.where((key >= start[:tokens, :]) & (key <= query), 0.0, NEG_FILL)
    s = dot(q_s[:many, :], key_block, NT) * EXP2_SCALE
    s = s.reshape(tokens // size, HEADS, size, rows) + off.reshape(tokens // size, 1, size, rows)
    return s.reshape(many, rows)


def fold(s):
    return jnp.maximum(s[:, :HDIM], s[:, HDIM:])


def row_max(s):
    return jnp.broadcast_to(jnp.max(s, axis=1, keepdims=True), (s.shape[0], HDIM))


def prepare(n_ctx, lengths_hbm, q_hbm, do_hbm, kv_ref, facts_ref, kv_own, q_s, q_t, do_r, start, level, p_own, acc,
            lengths_ref, q_ref, do_ref, sems):
    copies = fetch([(lengths_hbm, lengths_ref), (q_hbm, q_ref), (do_hbm, do_ref)], sems)
    rows = q_ref.shape[0]
    index = lax.axis_index("dp") * n_ctx + lax.axis_index("ctx")
    kv_own[...] = with_ones(kv_ref[...])
    copies[0].wait()
    facts, ends = facts_of(n_ctx, rows, index, lengths_ref)
    place = Place(n_ctx, rows, facts)
    line = lax.broadcasted_iota(jnp.int32, facts_ref.shape, 0)
    held = jnp.zeros(facts_ref.shape, jnp.int32)
    for i, fact in enumerate(facts):
        held = jnp.where(line == i, fact, held)
    facts_ref[...] = held
    token = place.base + lax.broadcasted_iota(jnp.int32, (rows, HDIM), 0)
    begin = jnp.zeros((rows, HDIM), jnp.int32)
    for end in ends:
        begin = jnp.where(token >= end, end, begin)
    start[...] = wide(begin) if rows == 2 * HDIM else jnp.broadcast_to(begin[:, :1], (rows, rows))
    copies[1].wait()
    for here, there in chunks(rows, n_ctx):
        q_s[here, :] = q_ref[there]
    s = levels(place, 0, HEADS * rows, q_s, kv_own[:, :HDIM], start)
    top = row_max(fold(s))
    level[...] = top
    p = jnp.exp2(s - wide(top)).astype(BF16)
    p_own[...] = p
    acc[...] = dot(p, kv_own[:, HDIM:])
    copies[2].wait()
    for here, there in chunks(rows, n_ctx):
        do_r[here, :] = do_ref[there]
    for h in range(HEADS):
        here = pl.ds(h * rows, rows)
        q_t[:, here] = q_s[here, :].T


def side_by_side(parts, axis):
    return parts[0] if len(parts) == 1 else jnp.concatenate(parts, axis=axis)


def attend(place, backs, many, q_s, kvs, start, level, acc, probs):
    scores = [levels(place, back, many, q_s, kv[:, :HDIM], start) for back, kv in zip(backs, kvs)]
    p = [jnp.exp2(s - wide(level[:many, :])).astype(BF16) for s in scores]
    for ref, part in zip(probs, p):
        ref[:many, :] = part
    acc[:many, :] += dot(side_by_side(p, 1), side_by_side([kv[:, HDIM:] for kv in kvs], 0))


def attend_even(n_ctx, facts, q_s, start, level, acc_in, *refs):
    *got, kv_even, p_even, acc = refs
    rows = got[0].shape[0]
    place = Place(n_ctx, rows, facts)
    for i, ref in enumerate(got):
        kv_even[i] = with_ones(ref[...])
    acc[...] = acc_in[...]

    def body(backs, many):
        attend(place, backs, many, q_s, [kv_even.at[place.hop(back)] for back in backs], start, level, acc,
               [p_even.at[lax.div(back, 2) - 1] for back in backs])

    place.past(range(2, n_ctx + 1, 2), body)


def gradients(many, q_t, do_s, do_t, ps, kvs, corr):
    d = [dot(do_s[:many, :], kv[:, HDIM:2 * HDIM], NT) for kv in kvs]
    dv = [dot(do_t[:, :many], p) for p in ps]
    ds = [(p.astype(F32) * (each - wide(corr[:many, :]))).astype(BF16) for p, each in zip(ps, d)]
    dk = [dot(q_t[:, :many], each) for each in ds]
    return [(each, jnp.concatenate([k.T, v.T], axis=1)) for each, k, v in zip(ds, dk, dv)]


def forward(n_ctx, facts, q_s, q_t, do_r, start, level, acc_in, kv_own, kv_even, kv_passed, p_own_in, p_even_in,
            o_hbm, kv_odd, ds_odd, do_s, do_t, corr, g_passed, p_own, p_even, o_ref, p_odd, acc, top, p_new, sems):
    rows = o_ref.shape[0]
    size = rows // n_ctx
    place = Place(n_ctx, rows, facts)
    pairs = n_ctx // 2
    everything = HEADS * rows
    odd_backs, even_backs = range(1, n_ctx, 2), range(2, n_ctx + 1, 2)
    del p_own_in, p_even_in

    for i in range(pairs):
        kv_odd[i] = with_ones(kv_passed[i])

    def odd(backs):
        return [kv_odd.at[place.hop(back)] for back in backs]

    def even(backs):
        return [kv_even.at[place.hop(back)] for back in backs]

    def attend_odd(reference):
        def body(backs, many):
            attend(place, backs, many, q_s, odd(backs), start, reference, acc, [p_odd.at[lax.div(back, 2)] for back in backs])
        return body

    acc[...] = acc_in[...]
    place.past(odd_backs, attend_odd(level))

    @pl.when(jnp.logical_not(jnp.max(acc[:, HDIM:]) < 2.0 ** 40))
    def _():
        def raise_top(backs, many, kvs):
            for back, kv in zip(backs, kvs):
                top[:many, :] = jnp.maximum(top[:many, :], fold(levels(place, back, many, q_s, kv[:, :HDIM], start)))

        top[...] = jnp.full(top.shape, NEG_FILL, F32)
        raise_top((0,), everything, [kv_own])
        place.past(odd_backs, lambda backs, many: raise_top(backs, many, odd(backs)))
        place.past(even_backs, lambda backs, many: raise_top(backs, many, even(backs)))
        top[...] = row_max(top[...])
        acc[...] = jnp.zeros(acc.shape, F32)

        def replace(backs, many, kvs, probs):
            for back, kv, ref in zip(backs, kvs, probs):
                attend(place, (back,), many, q_s, [kv], start, top, acc, [p_new])
                copy = pltpu.make_async_copy(p_new.at[pl.ds(0, many)], ref.at[pl.ds(0, many)], sems.at[0])
                copy.start()
                copy.wait()

        replace((0,), everything, [kv_own], [p_own])
        place.past(even_backs, lambda backs, many: replace(backs, many, even(backs), [p_even.at[lax.div(back, 2) - 1] for back in backs]))
        place.past(odd_backs, attend_odd(top))

    for i in range(0, everything, rows):
        here = pl.ds(i, rows)
        total = acc[here, :]
        inverse = 1.0 / total[:, HDIM:]
        out = (total[:, :HDIM] * inverse).astype(BF16)
        grad = do_r[here, :].astype(F32)
        corr[here, :] = jnp.sum(grad * out.astype(F32), axis=1, keepdims=True) * inverse
        scaled = grad * inverse
        do_s[here, :] = scaled.astype(BF16)
        do_t[:, here] = scaled.astype(BF16).T
        for part, there in chunks(rows, n_ctx):
            if i <= part.start < i + rows:
                o_ref[there] = out[part.start - i:part.start - i + size, :]

    leaving = pltpu.make_async_copy(o_ref, o_hbm, sems.at[1])
    leaving.start()

    def backward(backs, many):
        ps = [p_odd[lax.div(back, 2), :many, :] for back in backs]
        for back, (ds, terms) in zip(backs, gradients(many, q_t, do_s, do_t, ps, odd(backs), corr)):
            ds_odd[lax.div(back, 2), :many, :] = ds
            g_passed[place.hop(back)] = terms.astype(BF16)

    done = place.past(odd_backs, backward)

    @pl.loop(done, pairs)
    def _(i):
        g_passed[place.hop(2 * i + 1)] = jnp.zeros((rows, 2 * HDIM), BF16)

    leaving.wait()


def even(n_ctx, facts, q_t, do_s, do_t, kv_even, p_even, corr, ds_even, g_direct):
    rows = kv_even.shape[1]
    place = Place(n_ctx, rows, facts)

    def backward(backs, many):
        ps = [p_even[lax.div(back, 2) - 1, :many, :] for back in backs]
        kvs = [kv_even.at[place.hop(back)] for back in backs]
        for back, (ds, terms) in zip(backs, gradients(many, q_t, do_s, do_t, ps, kvs, corr)):
            ds_even[lax.div(back, 2) - 1, :many, :] = ds
            g_direct[place.hop(back) - 1] = terms

    done = place.past(range(2, n_ctx, 2), backward)

    @pl.loop(done, n_ctx // 2 - 1)
    def _(i):
        g_direct[place.hop(2 * i + 2) - 1] = jnp.zeros((rows, 2 * HDIM), F32)


def rest(n_ctx, facts, q_t, do_s, do_t, kv_even, p_even, corr, kv_own, p_own, kv_odd, ds_odd, ds_even,
         dq_ref, g_own, g_prev, dq_acc):
    rows = kv_own.shape[0]
    place = Place(n_ctx, rows, facts)

    (ds, g_own[...]), = gradients(HEADS * rows, q_t, do_s, do_t, [p_own[...]], [kv_own], corr)
    dq_acc[...] = dot(ds, kv_own[:, :HDIM])

    def add(backs, many, ds, kv):
        dq_acc[:many, :] += dot(side_by_side([ds(back)[:many, :] for back in backs], 1),
                                side_by_side([kv[place.hop(back), :, :HDIM] for back in backs], 0))

    def add_odd(backs, many):
        add(backs, many, lambda back: ds_odd.at[lax.div(back, 2)], kv_odd)

    def add_even(backs, many):
        add(backs, many, lambda back: ds_even.at[lax.div(back, 2) - 1], kv_even)

    def farthest(backs, many):
        at = place.hop(backs[0])
        (ds, g_prev[...]), = gradients(many, q_t, do_s, do_t, [p_even[n_ctx // 2 - 1, :many, :]], [kv_even.at[at]], corr)
        dq_acc[:many, :] += dot(ds, kv_even[at, :, :HDIM])

    place.past(range(1, n_ctx, 2), add_odd)
    place.past(range(2, n_ctx, 2), add_even)
    g_prev[...] = jnp.zeros(g_prev.shape, F32)
    place.past(range(n_ctx, n_ctx + 1), farthest)

    for here, there in chunks(rows, n_ctx):
        dq_ref[there] = (dq_acc[here, :] * SCALE).astype(BF16)


def finish(total, last, gk_ref, gv_ref):
    terms = total[...] + last[...].astype(F32)
    gk_ref[...] = (terms[:, :HDIM] * SCALE).astype(BF16)
    gv_ref[...] = terms[:, HDIM:].astype(BF16)


def size_of(arrays):
    return sum(math.prod(array.shape) * jnp.dtype(array.dtype).itemsize for array in arrays)


def call(body, name, outs, args, scratch, flops, resident, aliases=(), away=(), leaves=(), copies=0):
    vmem = pl.BlockSpec(memory_space=pltpu.VMEM)
    anywhere = pl.BlockSpec(memory_space=pl.ANY)
    hbm = pl.BlockSpec(memory_space=pltpu.HBM)
    outs = tuple(jax.ShapeDtypeStruct(shape, dtype) for shape, dtype in outs)
    held = size_of(scratch) + 8 * 2**20
    if not resident:
        held = min(held + size_of(outs) + size_of(args), 62 * 2**20)
    in_specs, out_specs = [vmem] * len(args), [vmem] * len(outs)
    for i in away:
        in_specs[i] = hbm
    for o in leaves:
        out_specs[o] = hbm
    for i, o in aliases:
        in_specs[i] = out_specs[o] = anywhere
    return pl.pallas_call(
        body,
        out_shape=outs,
        in_specs=in_specs,
        out_specs=tuple(out_specs),
        scratch_shapes=scratch + [pltpu.SemaphoreType.DMA((copies,))] * (copies > 0),
        input_output_aliases=dict(aliases),
        compiler_params=pltpu.CompilerParams(vmem_limit_bytes=held),
        cost_estimate=pl.CostEstimate(flops=flops, bytes_accessed=2**20, transcendentals=0),
        name=name,
    )(*(pltpu.with_memory_space_constraint(arg, pltpu.HBM) if i in away else arg for i, arg in enumerate(args)))


def shards(queries, keys, values, grad_out, lengths):
    rows = keys.shape[0]
    n_dp, n_ctx = lax.axis_size("dp"), lax.axis_size("ctx")
    axes = ("dp", "ctx")
    pairs = n_ctx // 2
    ctx = lax.axis_index("ctx")
    many = HEADS * rows
    once = 2 * many * rows * HDIM
    by_row, by_lane = (many, HDIM), (HDIM, many)
    block, kv_ones = (rows, 2 * HDIM), (rows, 3 * HDIM)
    run = functools.partial(call, resident=(n_ctx + 1) * many * rows <= 6 * 2**20)
    def kernel(body, *args, **kwargs):
        return run(functools.partial(body, n_ctx), body.__name__, *args, **kwargs)

    def swap(blocks, flip):
        return lax.ppermute(blocks, axes, flip_route(n_dp, n_ctx, flip))

    later = [ctx < ctx ^ max(2 * i, 1) for i in range(pairs)]

    kv, = run(join, "join", [(block, BF16)], (keys, values), [], 1, away=(0, 1), copies=2)
    prev = lax.ppermute(kv, axes, run_route(n_dp, n_ctx))
    facts, kv_own, q_s, q_t, do_r, start, level, p_own, acc = kernel(
        prepare, [((8, HDIM), jnp.int32), (kv_ones, BF16), (by_row, BF16), (by_lane, BF16), (by_row, BF16),
                  ((rows, rows), jnp.int32), (by_row, F32), ((many, rows), BF16), ((many, 2 * HDIM), F32)],
        (lengths, queries, grad_out, kv),
        [pltpu.SMEM(lengths.shape, jnp.int32), pltpu.VMEM(queries.shape, BF16), pltpu.VMEM(queries.shape, BF16)], 2 * once,
        away=(0, 1, 2), copies=3)
    ours = kv_own[:, :2 * HDIM]
    sent = [jnp.where(after, ours, prev) for after in later]
    got = [prev] + [swap(sent[i], 2 * i) for i in range(1, pairs)]
    passed = swap(jnp.stack(sent[:1] + got[1:]), 1)
    kv_even, p_even, acc = kernel(
        attend_even, [((pairs,) + kv_ones, BF16), ((pairs, many, rows), BF16), ((many, 2 * HDIM), F32)],
        (facts, q_s, start, level, acc, *got), [], 2 * pairs * once)
    attn_out, kv_odd, ds_odd, do_s, do_t, corr, g_passed, p_own, p_even = kernel(
        forward,
        [(queries.shape, BF16), ((pairs,) + kv_ones, BF16), ((pairs, many, rows), BF16),
         (by_row, BF16), (by_lane, BF16), (by_row, F32), ((pairs,) + block, BF16), (p_own.shape, BF16), (p_even.shape, BF16)],
        (facts, q_s, q_t, do_r, start, level, acc, kv_own, kv_even, passed, p_own, p_even),
        [pltpu.VMEM(queries.shape, BF16), pltpu.VMEM((pairs, many, rows), BF16), pltpu.VMEM((many, 2 * HDIM), F32),
         pltpu.VMEM(by_row, F32), pltpu.VMEM((many, rows), BF16)],
        5 * pairs * once, aliases=((10, 7), (11, 8)), leaves=(0,), copies=2)
    partner = swap(g_passed, 1).astype(F32)
    shared = (facts, q_t, do_s, do_t, kv_even, p_even, corr)
    ds_even, g_direct = kernel(even, [((pairs - 1, many, rows), BF16), ((pairs - 1,) + block, F32)],
                               shared, [], 3 * (pairs - 1) * once)
    terms = [partner[0]] + [swap((g_direct[i - 1] + partner[i]).astype(BF16), 2 * i).astype(F32) for i in range(1, pairs)]
    grad_queries, g_own, g_prev = kernel(rest, [(queries.shape, BF16), (block, F32), (block, F32)],
                                         shared + (kv_own, p_own, kv_odd, ds_odd, ds_even),
                                         [pltpu.VMEM(by_row, F32)], (n_ctx + 7) * once)
    own_total, prev_total = g_own, g_prev
    for after, term in zip(later, terms):
        own_total = own_total + jnp.where(after, term, 0.0)
        prev_total = prev_total + jnp.where(after, 0.0, term)
    back = [(b, a) for a, b in run_route(n_dp, n_ctx)]
    last = lax.ppermute(prev_total.astype(BF16), axes, back)
    grad_keys, grad_values = run(finish, "finish", [(keys.shape, BF16), (values.shape, BF16)], (own_total, last), [], 1)
    return (attn_out, grad_queries, grad_keys, grad_values)


def solution(mesh):
    tokens = P(("dp", "ctx"), None)
    return jax.shard_map(
        shards,
        mesh=mesh,
        in_specs=(tokens, tokens, tokens, tokens, P()),
        out_specs=(tokens, tokens, tokens, tokens),
        check_vma=False,
    )
```

```python
import functools
import math

import jax
import jax.numpy as jnp
from jax import lax
from jax.experimental import pallas as pl
from jax.experimental.pallas import tpu as pltpu
from jax.sharding import PartitionSpec as P

HEADS = 8
HDIM = 128
NEG_FILL = -1e30
SCALE = float(HDIM) ** -0.5
EXP2_SCALE = SCALE * math.log2(math.e)

NT = (((1,), (1,)), ((), ()))
NN = (((1,), (0,)), ((), ()))
F32, BF16 = jnp.float32, jnp.bfloat16


def dot(a, b, dims=NN):
    return lax.dot_general(a, b, dims, preferred_element_type=F32)


def wide(column):
    return jnp.concatenate([column, column], axis=1)


def run_route(n_dp, n_ctx):
    return [(d * n_ctx + c, (d + 1) * n_ctx + c) for d in range(n_dp - 1) for c in range(n_ctx)]


def flip_route(n_dp, n_ctx, flip):
    return [(d * n_ctx + c, d * n_ctx + (c ^ flip)) for d in range(n_dp) for c in range(n_ctx)]


def facts_of(n_ctx, rows, index, lengths_ref):
    base = index * rows
    ends, end = [], jnp.int32(0)
    for i in range(lengths_ref.shape[0]):
        end = end + lengths_ref[i]
        ends.append(end)
    low, high = jnp.int32(0), ends[-1]
    for end in ends:
        low = jnp.where(end <= base, end, low)
    for end in reversed(ends):
        high = jnp.where(end > base, end, high)
    before = lax.div(base - low + rows - 1, rows)
    short = (high - base <= rows - rows // n_ctx).astype(jnp.int32)
    return (lax.rem(index, n_ctx), base, before, short), ends


class Place:
    def __init__(self, n_ctx, rows, facts):
        self.n_ctx, self.rows = n_ctx, rows
        self.ctx, self.base, self.before, short = facts if isinstance(facts, tuple) else (facts[i, 0] for i in range(4))
        self.short = short == 1

    def hop(self, back):
        return lax.div(self.ctx ^ lax.rem(self.ctx - back + 2 * self.n_ctx, self.n_ctx), 2)

    def past(self, backs, body):
        first, step = backs[0], backs.step
        count = jnp.clip(lax.div(self.before - first + step, step), 0, len(backs))
        for short in (True, False):
            many = HEADS * (self.rows - self.rows // self.n_ctx if short else self.rows)
            fits = self.short if short else jnp.logical_not(self.short)

            if len(backs) > 1:

                @pl.when(fits)
                def _():
                    @pl.loop(0, lax.div(count, 2))
                    def _(i):
                        body((first + 2 * i * step, first + (2 * i + 1) * step), many)

            @pl.when(fits & (lax.rem(count, 2) == 1))
            def _():
                body((first + (count - 1) * step,), many)

        return count


def chunks(rows, n_ctx):
    size = rows // n_ctx
    for c in range(n_ctx):
        for h in range(HEADS):
            yield (pl.ds((c * HEADS + h) * size, size), (pl.ds(c * size, size), pl.ds(h * HDIM, HDIM)))


def fetch(pairs, sems):
    copies = [pltpu.make_async_copy(source, target, sems.at[i]) for i, (source, target) in enumerate(pairs)]
    for copy in copies:
        copy.start()
    return copies


def join(keys, values, kv, sems):
    for copy in fetch([(keys, kv.at[:, pl.ds(0, HDIM)]), (values, kv.at[:, pl.ds(HDIM, HDIM)])], sems):
        copy.wait()


def with_ones(kv):
    return jnp.concatenate([kv, jnp.ones((kv.shape[0], HDIM), BF16)], axis=1)


def levels(place, back, many, q_s, key_block, start):
    size, rows = place.rows // place.n_ctx, place.rows
    tokens = many // HEADS
    key = place.base - back * rows + lax.broadcasted_iota(jnp.int32, (tokens, rows), 1)
    query = place.base + lax.broadcasted_iota(jnp.int32, (tokens, rows), 0)
    off = jnp.where((key >= start[:tokens, :]) & (key <= query), 0.0, NEG_FILL)
    s = dot(q_s[:many, :], key_block, NT) * EXP2_SCALE
    s = s.reshape(tokens // size, HEADS, size, rows) + off.reshape(tokens // size, 1, size, rows)
    return s.reshape(many, rows)


def fold(s):
    return jnp.maximum(s[:, :HDIM], s[:, HDIM:])


def row_max(s):
    return jnp.broadcast_to(jnp.max(s, axis=1, keepdims=True), (s.shape[0], HDIM))


def prepare(n_ctx, lengths_hbm, q_hbm, do_hbm, kv_ref, facts_ref, kv_own, q_s, q_t, do_r, start, level, p_own, acc,
            lengths_ref, q_ref, do_ref, sems):
    copies = fetch([(lengths_hbm, lengths_ref), (q_hbm, q_ref), (do_hbm, do_ref)], sems)
    rows = q_ref.shape[0]
    index = lax.axis_index("dp") * n_ctx + lax.axis_index("ctx")
    kv_own[...] = with_ones(kv_ref[...])
    copies[0].wait()
    facts, ends = facts_of(n_ctx, rows, index, lengths_ref)
    place = Place(n_ctx, rows, facts)
    line = lax.broadcasted_iota(jnp.int32, facts_ref.shape, 0)
    held = jnp.zeros(facts_ref.shape, jnp.int32)
    for i, fact in enumerate(facts):
        held = jnp.where(line == i, fact, held)
    facts_ref[...] = held
    token = place.base + lax.broadcasted_iota(jnp.int32, (rows, HDIM), 0)
    begin = jnp.zeros((rows, HDIM), jnp.int32)
    for end in ends:
        begin = jnp.where(token >= end, end, begin)
    start[...] = wide(begin) if rows == 2 * HDIM else jnp.broadcast_to(begin[:, :1], (rows, rows))
    copies[1].wait()
    for here, there in chunks(rows, n_ctx):
        q_s[here, :] = q_ref[there]
    s = levels(place, 0, HEADS * rows, q_s, kv_own[:, :HDIM], start)
    top = row_max(fold(s))
    level[...] = top
    p = jnp.exp2(s - wide(top)).astype(BF16)
    p_own[...] = p
    acc[...] = dot(p, kv_own[:, HDIM:])
    copies[2].wait()
    for here, there in chunks(rows, n_ctx):
        do_r[here, :] = do_ref[there]
    for h in range(HEADS):
        here = pl.ds(h * rows, rows)
        q_t[:, here] = q_s[here, :].T


def side_by_side(parts, axis):
    return parts[0] if len(parts) == 1 else jnp.concatenate(parts, axis=axis)


def attend(place, backs, many, q_s, kvs, start, level, acc, probs):
    scores = [levels(place, back, many, q_s, kv[:, :HDIM], start) for back, kv in zip(backs, kvs)]
    p = [jnp.exp2(s - wide(level[:many, :])).astype(BF16) for s in scores]
    for ref, part in zip(probs, p):
        ref[:many, :] = part
    acc[:many, :] += dot(side_by_side(p, 1), side_by_side([kv[:, HDIM:] for kv in kvs], 0))


def attend_even(n_ctx, facts, q_s, start, level, acc_in, *refs):
    *got, kv_even, p_even, acc = refs
    rows = got[0].shape[0]
    place = Place(n_ctx, rows, facts)
    for i, ref in enumerate(got):
        kv_even[i] = with_ones(ref[...])
    acc[...] = acc_in[...]

    def body(backs, many):
        attend(place, backs, many, q_s, [kv_even.at[place.hop(back)] for back in backs], start, level, acc,
               [p_even.at[lax.div(back, 2) - 1] for back in backs])

    place.past(range(2, n_ctx + 1, 2), body)


def gradients(many, q_t, do_s, do_t, ps, kvs, corr):
    d = [dot(do_s[:many, :], kv[:, HDIM:2 * HDIM], NT) for kv in kvs]
    dv = [dot(do_t[:, :many], p) for p in ps]
    ds = [(p.astype(F32) * (each - wide(corr[:many, :]))).astype(BF16) for p, each in zip(ps, d)]
    dk = [dot(q_t[:, :many], each) for each in ds]
    return [(each, jnp.concatenate([k.T, v.T], axis=1)) for each, k, v in zip(ds, dk, dv)]


def forward(n_ctx, facts, q_s, q_t, do_r, start, level, acc_in, kv_own, kv_even, kv_passed, p_own_in, p_even_in,
            o_hbm, kv_odd, ds_odd, do_s, do_t, corr, g_passed, p_own, p_even, o_ref, p_odd, acc, top, p_new, kv_now, sems):
    rows = o_ref.shape[0]
    size = rows // n_ctx
    place = Place(n_ctx, rows, facts)
    pairs = n_ctx // 2
    everything = HEADS * rows
    odd_backs = range(1, n_ctx, 2)
    del p_own_in, p_even_in

    for i in range(pairs):
        kv_odd[i] = with_ones(kv_passed[i])

    def odd(backs):
        return [kv_odd.at[place.hop(back)] for back in backs]

    def attend_odd(backs, many):
        attend(place, backs, many, q_s, odd(backs), start, level, acc, [p_odd.at[lax.div(back, 2)] for back in backs])

    acc[...] = acc_in[...]
    place.past(odd_backs, attend_odd)

    @pl.when(jnp.logical_not(jnp.max(acc[:, HDIM:]) < 2.0 ** 40))
    def _():
        def each(step):
            @pl.loop(0, place.before + 1)
            def _(back):
                at = place.hop(back)

                @pl.when(back == 0)
                def _():
                    kv_now[...] = kv_own[...]

                @pl.when(lax.rem(back, 2) == 1)
                def _():
                    kv_now[...] = kv_odd[at]

                @pl.when((back > 0) & (lax.rem(back, 2) == 0))
                def _():
                    kv_now[...] = kv_even[at]

                @pl.loop(0, n_ctx)
                def _(c):
                    here = pl.ds(c * HEADS * size, HEADS * size)
                    tokens = pl.ds(c * size, size)
                    key = place.base - back * rows + lax.broadcasted_iota(jnp.int32, (size, rows), 1)
                    query = place.base + c * size + lax.broadcasted_iota(jnp.int32, (size, rows), 0)
                    off = jnp.where((key >= start[tokens, :]) & (key <= query), 0.0, NEG_FILL)
                    s = dot(q_s[here, :], kv_now[:, :HDIM], NT) * EXP2_SCALE
                    step(here, (s.reshape(HEADS, size, rows) + off[None]).reshape(HEADS * size, rows))

                if step is replace:
                    half = lax.div(back, 2)
                    for fits, target in ((back == 0, p_own), (lax.rem(back, 2) == 1, p_odd.at[half]),
                                         ((back > 0) & (lax.rem(back, 2) == 0), p_even.at[jnp.maximum(half - 1, 0)])):

                        @pl.when(fits)
                        def _():
                            copy = pltpu.make_async_copy(p_new, target, sems.at[0])
                            copy.start()
                            copy.wait()

        def highest(here, s):
            top[here, :] = jnp.maximum(top[here, :], row_max(fold(s)))

        def replace(here, s):
            p = jnp.exp2(s - wide(top[here, :])).astype(BF16)
            p_new[here, :] = p
            acc[here, :] += dot(p, kv_now[:, HDIM:])

        @pl.loop(0, n_ctx)
        def _(c):
            here = pl.ds(c * HEADS * size, HEADS * size)
            top[here, :] = jnp.full((HEADS * size, HDIM), NEG_FILL, F32)
            acc[here, :] = jnp.zeros((HEADS * size, 2 * HDIM), F32)

        each(highest)
        each(replace)

    for i in range(0, everything, rows):
        here = pl.ds(i, rows)
        total = acc[here, :]
        inverse = 1.0 / total[:, HDIM:]
        out = (total[:, :HDIM] * inverse).astype(BF16)
        grad = do_r[here, :].astype(F32)
        corr[here, :] = jnp.sum(grad * out.astype(F32), axis=1, keepdims=True) * inverse
        scaled = grad * inverse
        do_s[here, :] = scaled.astype(BF16)
        do_t[:, here] = scaled.T.astype(BF16)
        for part, there in chunks(rows, n_ctx):
            if i <= part.start < i + rows:
                o_ref[there] = out[part.start - i:part.start - i + size, :]

    leaving = pltpu.make_async_copy(o_ref, o_hbm, sems.at[1])
    leaving.start()

    def backward(backs, many):
        ps = [p_odd[lax.div(back, 2), :many, :] for back in backs]
        for back, (ds, terms) in zip(backs, gradients(many, q_t, do_s, do_t, ps, odd(backs), corr)):
            ds_odd[lax.div(back, 2), :many, :] = ds
            g_passed[place.hop(back)] = terms.astype(BF16)

    done = place.past(odd_backs, backward)

    @pl.loop(done, pairs)
    def _(i):
        g_passed[place.hop(2 * i + 1)] = jnp.zeros((rows, 2 * HDIM), BF16)

    leaving.wait()


def even(n_ctx, facts, q_t, do_s, do_t, kv_even, p_even, corr, ds_even, g_direct):
    rows = kv_even.shape[1]
    place = Place(n_ctx, rows, facts)

    def backward(backs, many):
        ps = [p_even[lax.div(back, 2) - 1, :many, :] for back in backs]
        kvs = [kv_even.at[place.hop(back)] for back in backs]
        for back, (ds, terms) in zip(backs, gradients(many, q_t, do_s, do_t, ps, kvs, corr)):
            ds_even[lax.div(back, 2) - 1, :many, :] = ds
            g_direct[place.hop(back) - 1] = terms

    done = place.past(range(2, n_ctx, 2), backward)

    @pl.loop(done, n_ctx // 2 - 1)
    def _(i):
        g_direct[place.hop(2 * i + 2) - 1] = jnp.zeros((rows, 2 * HDIM), F32)


def rest(n_ctx, facts, q_t, do_s, do_t, kv_even, p_even, corr, kv_own, p_own, kv_odd, ds_odd, ds_even,
         dq_ref, g_own, g_prev, dq_acc):
    rows = kv_own.shape[0]
    place = Place(n_ctx, rows, facts)

    (ds, g_own[...]), = gradients(HEADS * rows, q_t, do_s, do_t, [p_own[...]], [kv_own], corr)
    dq_acc[...] = dot(ds, kv_own[:, :HDIM])

    def add(backs, many, ds, kv):
        dq_acc[:many, :] += dot(side_by_side([ds(back)[:many, :] for back in backs], 1),
                                side_by_side([kv[place.hop(back), :, :HDIM] for back in backs], 0))

    def add_odd(backs, many):
        add(backs, many, lambda back: ds_odd.at[lax.div(back, 2)], kv_odd)

    def add_even(backs, many):
        add(backs, many, lambda back: ds_even.at[lax.div(back, 2) - 1], kv_even)

    def farthest(backs, many):
        at = place.hop(backs[0])
        (ds, g_prev[...]), = gradients(many, q_t, do_s, do_t, [p_even[n_ctx // 2 - 1, :many, :]], [kv_even.at[at]], corr)
        dq_acc[:many, :] += dot(ds, kv_even[at, :, :HDIM])

    place.past(range(1, n_ctx, 2), add_odd)
    place.past(range(2, n_ctx, 2), add_even)
    g_prev[...] = jnp.zeros(g_prev.shape, F32)
    place.past(range(n_ctx, n_ctx + 1), farthest)

    for here, there in chunks(rows, n_ctx):
        dq_ref[there] = (dq_acc[here, :] * SCALE).astype(BF16)


def finish(total, last, gk_ref, gv_ref):
    terms = total[...] + last[...].astype(F32)
    gk_ref[...] = (terms[:, :HDIM] * SCALE).astype(BF16)
    gv_ref[...] = terms[:, HDIM:].astype(BF16)


def size_of(arrays):
    return sum(math.prod(array.shape) * jnp.dtype(array.dtype).itemsize for array in arrays)


def call(body, name, outs, args, scratch, flops, resident, aliases=(), away=(), leaves=(), copies=0):
    vmem = pl.BlockSpec(memory_space=pltpu.VMEM)
    anywhere = pl.BlockSpec(memory_space=pl.ANY)
    hbm = pl.BlockSpec(memory_space=pltpu.HBM)
    outs = tuple(jax.ShapeDtypeStruct(shape, dtype) for shape, dtype in outs)
    held = size_of(scratch) + 8 * 2**20
    if not resident:
        held = min(held + size_of(outs) + size_of(args), 62 * 2**20)
    in_specs, out_specs = [vmem] * len(args), [vmem] * len(outs)
    for i in away:
        in_specs[i] = hbm
    for o in leaves:
        out_specs[o] = hbm
    for i, o in aliases:
        in_specs[i] = out_specs[o] = anywhere
    return pl.pallas_call(
        body,
        out_shape=outs,
        in_specs=in_specs,
        out_specs=tuple(out_specs),
        scratch_shapes=scratch + [pltpu.SemaphoreType.DMA((copies,))] * (copies > 0),
        input_output_aliases=dict(aliases),
        compiler_params=pltpu.CompilerParams(vmem_limit_bytes=held),
        cost_estimate=pl.CostEstimate(flops=flops, bytes_accessed=2**20, transcendentals=0),
        name=name,
    )(*(pltpu.with_memory_space_constraint(arg, pltpu.HBM) if i in away else arg for i, arg in enumerate(args)))


def shards(queries, keys, values, grad_out, lengths):
    rows = keys.shape[0]
    n_dp, n_ctx = lax.axis_size("dp"), lax.axis_size("ctx")
    axes = ("dp", "ctx")
    pairs = n_ctx // 2
    ctx = lax.axis_index("ctx")
    many = HEADS * rows
    once = 2 * many * rows * HDIM
    by_row, by_lane = (many, HDIM), (HDIM, many)
    block, kv_ones = (rows, 2 * HDIM), (rows, 3 * HDIM)
    run = functools.partial(call, resident=(n_ctx + 1) * many * rows <= 6 * 2**20)
    def kernel(body, *args, **kwargs):
        return run(functools.partial(body, n_ctx), body.__name__, *args, **kwargs)

    def swap(blocks, flip):
        return lax.ppermute(blocks, axes, flip_route(n_dp, n_ctx, flip))

    later = [ctx < ctx ^ max(2 * i, 1) for i in range(pairs)]

    kv, = run(join, "join", [(block, BF16)], (keys, values), [], 1, away=(0, 1), copies=2)
    prev = lax.ppermute(kv, axes, run_route(n_dp, n_ctx))
    facts, kv_own, q_s, q_t, do_r, start, level, p_own, acc = kernel(
        prepare, [((8, HDIM), jnp.int32), (kv_ones, BF16), (by_row, BF16), (by_lane, BF16), (by_row, BF16),
                  ((rows, rows), jnp.int32), (by_row, F32), ((many, rows), BF16), ((many, 2 * HDIM), F32)],
        (lengths, queries, grad_out, kv),
        [pltpu.SMEM(lengths.shape, jnp.int32), pltpu.VMEM(queries.shape, BF16), pltpu.VMEM(queries.shape, BF16)], 2 * once,
        away=(0, 1, 2), copies=3)
    ours = kv_own[:, :2 * HDIM]
    sent = [jnp.where(after, ours, prev) for after in later]
    got = [prev] + [swap(sent[i], 2 * i) for i in range(1, pairs)]
    passed = swap(jnp.stack(sent[:1] + got[1:]), 1)
    kv_even, p_even, acc = kernel(
        attend_even, [((pairs,) + kv_ones, BF16), ((pairs, many, rows), BF16), ((many, 2 * HDIM), F32)],
        (facts, q_s, start, level, acc, *got), [], 2 * pairs * once)
    attn_out, kv_odd, ds_odd, do_s, do_t, corr, g_passed, p_own, p_even = kernel(
        forward,
        [(queries.shape, BF16), ((pairs,) + kv_ones, BF16), ((pairs, many, rows), BF16),
         (by_row, BF16), (by_lane, BF16), (by_row, F32), ((pairs,) + block, BF16), (p_own.shape, BF16), (p_even.shape, BF16)],
        (facts, q_s, q_t, do_r, start, level, acc, kv_own, kv_even, passed, p_own, p_even),
        [pltpu.VMEM(queries.shape, BF16), pltpu.VMEM((pairs, many, rows), BF16), pltpu.VMEM((many, 2 * HDIM), F32),
         pltpu.VMEM(by_row, F32), pltpu.VMEM((many, rows), BF16), pltpu.VMEM(kv_ones, BF16)],
        5 * pairs * once, aliases=((10, 7), (11, 8)), leaves=(0,), copies=2)
    partner = swap(g_passed, 1).astype(F32)
    shared = (facts, q_t, do_s, do_t, kv_even, p_even, corr)
    ds_even, g_direct = kernel(even, [((pairs - 1, many, rows), BF16), ((pairs - 1,) + block, F32)],
                               shared, [], 3 * (pairs - 1) * once)
    terms = [partner[0]] + [swap((g_direct[i - 1] + partner[i]).astype(BF16), 2 * i).astype(F32) for i in range(1, pairs)]
    grad_queries, g_own, g_prev = kernel(rest, [(queries.shape, BF16), (block, F32), (block, F32)],
                                         shared + (kv_own, p_own, kv_odd, ds_odd, ds_even),
                                         [pltpu.VMEM(by_row, F32)], (n_ctx + 7) * once)
    own_total, prev_total = g_own, g_prev
    for after, term in zip(later, terms):
        own_total = own_total + jnp.where(after, term, 0.0)
        prev_total = prev_total + jnp.where(after, 0.0, term)
    back = [(b, a) for a, b in run_route(n_dp, n_ctx)]
    last = lax.ppermute(prev_total.astype(BF16), axes, back)
    grad_keys, grad_values = run(finish, "finish", [(keys.shape, BF16), (values.shape, BF16)], (own_total, last), [], 1)
    return (attn_out, grad_queries, grad_keys, grad_values)


def solution(mesh):
    tokens = P(("dp", "ctx"), None)
    return jax.shard_map(
        shards,
        mesh=mesh,
        in_specs=(tokens, tokens, tokens, tokens, P()),
        out_specs=(tokens, tokens, tokens, tokens),
        check_vma=False,
    )
```

```python
import functools
import math

import jax
import jax.numpy as jnp
from jax import lax
from jax.experimental import pallas as pl
from jax.experimental.pallas import tpu as pltpu
from jax.sharding import PartitionSpec as P

HEADS = 8
HDIM = 128
NEG_FILL = -1e30
SCALE = float(HDIM) ** -0.5
EXP2_SCALE = SCALE * math.log2(math.e)

NT = (((1,), (1,)), ((), ()))
NN = (((1,), (0,)), ((), ()))
F32, BF16 = jnp.float32, jnp.bfloat16


def dot(a, b, dims=NN):
    return lax.dot_general(a, b, dims, preferred_element_type=F32)


def wide(column):
    return jnp.concatenate([column, column], axis=1)


def run_route(n_dp, n_ctx):
    return [(d * n_ctx + c, (d + 1) * n_ctx + c) for d in range(n_dp - 1) for c in range(n_ctx)]


def flip_route(n_dp, n_ctx, flip):
    return [(d * n_ctx + c, d * n_ctx + (c ^ flip)) for d in range(n_dp) for c in range(n_ctx)]


class Flips:
    def __init__(self, n_ctx):
        even = range(2, n_ctx, 2)
        self.near = [flip for flip in even if flip & (flip - 1) == 0]
        self.far = [flip for flip in even if flip & (flip - 1) != 0]
        self.even = self.near + self.far
        self.first = [0] + self.near
        self.passed = [1] + [flip + 1 for flip in self.near]
        self.second = self.far + self.passed
        self.last = [flip + 1 for flip in self.far]
        self.odd = self.passed + self.last


def facts_of(n_ctx, rows, index, lengths_ref):
    base = index * rows
    ends, end = [], jnp.int32(0)
    for i in range(lengths_ref.shape[0]):
        end = end + lengths_ref[i]
        ends.append(end)
    low, high = jnp.int32(0), ends[-1]
    for end in ends:
        low = jnp.where(end <= base, end, low)
    for end in reversed(ends):
        high = jnp.where(end > base, end, high)
    before = lax.div(base - low + rows - 1, rows)
    short = (high - base <= rows - rows // n_ctx).astype(jnp.int32)
    return (lax.rem(index, n_ctx), base, before, short), ends


class Place:
    def __init__(self, n_ctx, rows, facts):
        self.n_ctx, self.rows = n_ctx, rows
        self.ctx, self.base, self.before, short = facts if isinstance(facts, tuple) else (facts[i, 0] for i in range(4))
        self.short = short == 1

    def back(self, flip):
        back = lax.rem(self.ctx - (self.ctx ^ flip) + 2 * self.n_ctx, self.n_ctx)
        return jnp.where(back == 0, self.n_ctx, back)

    def needed(self, flip):
        return self.back(flip) <= self.before

    def past(self, flips, body):
        backs = [self.back(flip) for flip in flips]
        needed = [(back <= self.before).astype(jnp.int32) for back in backs]
        count = sum(needed)

        def pick(k):
            at, back, seen = jnp.int32(0), jnp.int32(0), jnp.int32(0)
            for i in range(len(flips)):
                here = (needed[i] == 1) & (seen == k)
                at, back = jnp.where(here, i, at), jnp.where(here, backs[i], back)
                seen = seen + needed[i]
            return at, back

        for short in (True, False):
            many = HEADS * (self.rows - self.rows // self.n_ctx if short else self.rows)
            fits = self.short if short else jnp.logical_not(self.short)

            if len(flips) > 1:

                @pl.when(fits)
                def _():
                    @pl.loop(0, lax.div(count, 2))
                    def _(i):
                        body(*zip(pick(2 * i), pick(2 * i + 1)), many)

            @pl.when(fits & (lax.rem(count, 2) == 1))
            def _():
                body(*zip(pick(count - 1)), many)


def chunks(rows, n_ctx):
    size = rows // n_ctx
    for c in range(n_ctx):
        for h in range(HEADS):
            yield (pl.ds((c * HEADS + h) * size, size), (pl.ds(c * size, size), pl.ds(h * HDIM, HDIM)))


def fetch(pairs, sems):
    copies = [pltpu.make_async_copy(source, target, sems.at[i]) for i, (source, target) in enumerate(pairs)]
    for copy in copies:
        copy.start()
    return copies


def join(keys, values, kv, sems):
    for copy in fetch([(keys, kv.at[:, pl.ds(0, HDIM)]), (values, kv.at[:, pl.ds(HDIM, HDIM)])], sems):
        copy.wait()


def ones_beside(values):
    return jnp.concatenate([values, jnp.ones(values.shape, BF16)], axis=1)


def side_by_side(parts, axis):
    return parts[0] if len(parts) == 1 else jnp.concatenate(parts, axis=axis)


def offsets(place, back, first, tokens, start):
    shape = (tokens, place.rows)
    key = place.base - back * place.rows + lax.broadcasted_iota(jnp.int32, shape, 1)
    query = place.base + first + lax.broadcasted_iota(jnp.int32, shape, 0)
    return jnp.where((key >= start[pl.ds(first, tokens), :]) & (key <= query), 0.0, NEG_FILL)


def levels(place, back, many, q_s, key_block, start):
    size, rows = place.rows // place.n_ctx, place.rows
    tokens = many // HEADS
    off = offsets(place, back, 0, tokens, start)
    s = dot(q_s[:many, :], key_block, NT) * EXP2_SCALE
    s = s.reshape(tokens // size, HEADS, size, rows) + off.reshape(tokens // size, 1, size, rows)
    return s.reshape(many, rows)


def fold(s):
    return jnp.maximum(s[:, :HDIM], s[:, HDIM:])


def row_max(s):
    return jnp.broadcast_to(jnp.max(s, axis=1, keepdims=True), (s.shape[0], HDIM))


def prepare(n_ctx, lengths_hbm, q_hbm, do_hbm, kv_ref, facts_ref, kv_own, q_s, q_t, do_r, start, level, p_own, acc,
            lengths_ref, q_ref, do_ref, sems):
    copies = fetch([(lengths_hbm, lengths_ref), (q_hbm, q_ref), (do_hbm, do_ref)], sems)
    rows = q_ref.shape[0]
    index = lax.axis_index("dp") * n_ctx + lax.axis_index("ctx")
    kv_own[...] = kv_ref[...]
    copies[0].wait()
    facts, ends = facts_of(n_ctx, rows, index, lengths_ref)
    place = Place(n_ctx, rows, facts)
    line = lax.broadcasted_iota(jnp.int32, facts_ref.shape, 0)
    held = jnp.zeros(facts_ref.shape, jnp.int32)
    for i, fact in enumerate(facts):
        held = jnp.where(line == i, fact, held)
    facts_ref[...] = held
    token = place.base + lax.broadcasted_iota(jnp.int32, (rows, HDIM), 0)
    begin = jnp.zeros((rows, HDIM), jnp.int32)
    for end in ends:
        begin = jnp.where(token >= end, end, begin)
    start[...] = wide(begin) if rows == 2 * HDIM else jnp.broadcast_to(begin[:, :1], (rows, rows))
    copies[1].wait()
    for here, there in chunks(rows, n_ctx):
        q_s[here, :] = q_ref[there]
    s = levels(place, 0, HEADS * rows, q_s, kv_own[:, :HDIM], start)
    top = row_max(fold(s))
    level[...] = top
    p = jnp.exp2(s - wide(top)).astype(BF16)
    p_own[...] = p
    acc[...] = dot(p, ones_beside(kv_own[:, HDIM:]))
    copies[2].wait()
    for here, there in chunks(rows, n_ctx):
        do_r[here, :] = do_ref[there]
    for h in range(HEADS):
        here = pl.ds(h * rows, rows)
        q_t[:, here] = q_s[here, :].T


def attend(place, backs, many, q_s, kvs, start, level, source, acc, probs):
    scores = [levels(place, back, many, q_s, kv[:, :HDIM], start) for back, kv in zip(backs, kvs)]
    p = [jnp.exp2(s - wide(level[:many, :])).astype(BF16) for s in scores]
    for ref, part in zip(probs, p):
        ref[:many, :] = part
    acc[:many, :] = source[:many, :] + dot(side_by_side(p, 1), side_by_side([ones_beside(kv[:, HDIM:]) for kv in kvs], 0))


def attend_first(n_ctx, facts, q_s, start, level, acc_in, *refs):
    *got, kvs, probs, acc, facts_out = refs
    facts_out[...] = facts[...]
    place = Place(n_ctx, got[0].shape[0], facts)
    for i, ref in enumerate(got):
        kvs[i] = ref[...]
    acc[...] = acc_in[...]
    place.past(Flips(n_ctx).first, lambda at, backs, many: attend(
        place, backs, many, q_s, [kvs.at[i] for i in at], start, level, acc, acc, [probs.at[i] for i in at]))


def attend_second(n_ctx, facts, q_s, start, level, acc_in, *refs):
    *got, passed, kvs, probs, acc = refs
    place = Place(n_ctx, passed.shape[1], facts)
    for i, ref in enumerate(got):
        kvs[i] = ref[...]
    for i in range(passed.shape[0]):
        kvs[len(got) + i] = passed[i]
    acc[...] = acc_in[...]
    place.past(Flips(n_ctx).second, lambda at, backs, many: attend(
        place, backs, many, q_s, [kvs.at[i] for i in at], start, level, acc, acc, [probs.at[i] for i in at]))


def settle(n_ctx, facts, q_s, do_r, start, level, acc_in, kv_own, kv_first, kv_second, kv_last, p_own_in, p_first_in, p_second_in,
           o_ref, do_s, do_t, corr, p_last, p_own, p_first, p_second, acc, top, p_new, kv_now, sems):
    rows = o_ref.shape[0]
    size = rows // n_ctx
    place = Place(n_ctx, rows, facts)
    flips = Flips(n_ctx)
    everything = HEADS * rows
    del p_own_in, p_first_in, p_second_in

    if len(flips.last) == 1:

        def add_last(at, backs, many):
            attend(place, backs, many, q_s, [kv_last.at[0]], start, level, acc_in, acc, [p_last.at[0]])
            if many < everything:
                acc[many:, :] = acc_in[many:, :]

        place.past(flips.last, add_last)

        @pl.when(jnp.logical_not(place.needed(flips.last[0])))
        def _():
            acc[...] = acc_in[...]

    else:
        acc[...] = acc_in[...]
        place.past(flips.last, lambda at, backs, many: attend(
            place, backs, many, q_s, [kv_last.at[i] for i in at], start, level, acc, acc, [p_last.at[i] for i in at]))

    @pl.when(jnp.logical_not(jnp.max(acc[:, HDIM:]) < 2.0 ** 40))
    def _():
        def block(back, step):
            @pl.loop(0, n_ctx)
            def _(c):
                here = pl.ds(c * HEADS * size, HEADS * size)
                off = offsets(place, back, c * size, size, start)
                s = dot(q_s[here, :], kv_now[:, :HDIM], NT) * EXP2_SCALE
                step(here, (s.reshape(HEADS, size, rows) + off[None]).reshape(HEADS * size, rows))

        def store(target):
            copy = pltpu.make_async_copy(p_new, target, sems.at[0])
            copy.start()
            copy.wait()

        def each(step):
            kv_now[...] = kv_own[...]
            block(0, step)
            if step is replace:
                store(p_own)
            for group, kvs, probs in ((flips.first, kv_first, p_first), (flips.second, kv_second, p_second),
                                      (flips.last, kv_last, p_last)):

                @pl.loop(0, len(group))
                def _(i):
                    flip = sum(jnp.where(i == k, group[k], 0) for k in range(len(group)))

                    @pl.when(place.needed(flip))
                    def _():
                        kv_now[...] = kvs[i]
                        block(place.back(flip), step)
                        if step is replace:
                            store(probs.at[i])

        def highest(here, s):
            top[here, :] = jnp.maximum(top[here, :], row_max(fold(s)))

        def replace(here, s):
            p = jnp.exp2(s - wide(top[here, :])).astype(BF16)
            p_new[here, :] = p
            acc[here, :] += dot(p, ones_beside(kv_now[:, HDIM:]))

        @pl.loop(0, n_ctx)
        def _(c):
            here = pl.ds(c * HEADS * size, HEADS * size)
            top[here, :] = jnp.full((HEADS * size, HDIM), NEG_FILL, F32)
            acc[here, :] = jnp.zeros((HEADS * size, 2 * HDIM), F32)

        each(highest)
        each(replace)

    for i in range(0, everything, rows):
        here = pl.ds(i, rows)
        total = acc[here, :]
        inverse = 1.0 / total[:, HDIM:]
        out = (total[:, :HDIM] * inverse).astype(BF16)
        grad = do_r[here, :].astype(F32)
        corr[here, :] = jnp.sum(grad * out.astype(F32), axis=1, keepdims=True) * inverse
        scaled = grad * inverse
        do_s[here, :] = scaled.astype(BF16)
        do_t[:, here] = scaled.T.astype(BF16)
        for part, there in chunks(rows, n_ctx):
            if i <= part.start < i + rows:
                o_ref[there] = out[part.start - i:part.start - i + size, :]


def gradients(many, q_t, do_s, do_t, ps, kvs, corr):
    d = [dot(do_s[:many, :], kv[:, HDIM:], NT) for kv in kvs]
    dv = [dot(do_t[:, :many], p) for p in ps]
    ds = [(p.astype(F32) * (each - wide(corr[:many, :]))).astype(BF16) for p, each in zip(ps, d)]
    dk = [dot(q_t[:, :many], each) for each in ds]
    return [(each, jnp.concatenate([k.T, v.T], axis=1)) for each, k, v in zip(ds, dk, dv)]


def backward(place, groups, q_t, do_s, do_t, corr, ds, out):
    done = 0
    for flips, kvs, probs, first in groups:

        def body(at, backs, many):
            ps = [probs[first + i, :many, :] for i in at]
            for i, (each, terms) in zip(at, gradients(many, q_t, do_s, do_t, ps, [kvs.at[first + i] for i in at], corr)):
                ds[done + i, :many, :] = each
                out[done + i] = terms.astype(out.dtype)

        place.past(flips, body)
        for i, flip in enumerate(flips):

            @pl.when(jnp.logical_not(place.needed(flip)))
            def _():
                out[done + i] = jnp.zeros(out.shape[1:], out.dtype)

        done += len(flips)


def odd(n_ctx, facts, q_t, do_s, do_t, corr, kv_second, kv_last, p_second, p_last, o_ref, o_hbm, ds_odd, g_passed, sems):
    copies = fetch([(o_ref, o_hbm)], sems)
    flips = Flips(n_ctx)
    backward(Place(n_ctx, o_ref.shape[0], facts),
             ((flips.passed, kv_second, p_second, len(flips.far)), (flips.last, kv_last, p_last, 0)),
             q_t, do_s, do_t, corr, ds_odd, g_passed)
    copies[0].wait()


def even(n_ctx, facts, q_t, do_s, do_t, corr, kv_first, kv_second, p_first, p_second, ds_even, g_direct):
    flips = Flips(n_ctx)
    backward(Place(n_ctx, kv_first.shape[1], facts),
             ((flips.near, kv_first, p_first, 1), (flips.far, kv_second, p_second, 0)),
             q_t, do_s, do_t, corr, ds_even, g_direct)


def rest(n_ctx, facts, q_t, do_s, do_t, corr, kv_own, kv_first, kv_second, kv_last, p_own, p_first, ds_odd, ds_even,
         dq_ref, g_own, g_prev, dq_acc, k_odd, k_even):
    rows = kv_own.shape[0]
    place = Place(n_ctx, rows, facts)
    flips = Flips(n_ctx)
    (ds, g_own[...]), = gradients(HEADS * rows, q_t, do_s, do_t, [p_own[...]], [kv_own], corr)
    dq_acc[...] = dot(ds, kv_own[:, :HDIM])
    for i in range(len(flips.odd)):
        k_odd[i] = (kv_second[len(flips.far) + i] if i < len(flips.passed) else kv_last[i - len(flips.passed)])[:, :HDIM]
    for i in range(len(flips.even)):
        k_even[i] = (kv_first[1 + i] if i < len(flips.near) else kv_second[i - len(flips.near)])[:, :HDIM]

    for group, ds, keys in ((flips.odd, ds_odd, k_odd), (flips.even, ds_even, k_even)):

        def add(at, backs, many):
            dq_acc[:many, :] += dot(side_by_side([ds[i, :many, :] for i in at], 1), side_by_side([keys[i] for i in at], 0))

        place.past(group, add)

    def farthest(at, backs, many):
        (ds, g_prev[...]), = gradients(many, q_t, do_s, do_t, [p_first[0, :many, :]], [kv_first.at[0]], corr)
        dq_acc[:many, :] += dot(ds, kv_first[0, :, :HDIM])

    g_prev[...] = jnp.zeros(g_prev.shape, F32)
    place.past([0], farthest)

    for here, there in chunks(rows, n_ctx):
        dq_ref[there] = (dq_acc[here, :] * SCALE).astype(BF16)


def finish(total, last, gk_ref, gv_ref):
    terms = total[...] + last[...].astype(F32)
    gk_ref[...] = (terms[:, :HDIM] * SCALE).astype(BF16)
    gv_ref[...] = terms[:, HDIM:].astype(BF16)


def size_of(arrays):
    return sum(math.prod(array.shape) * jnp.dtype(array.dtype).itemsize for array in arrays)


def call(body, name, outs, args, scratch, flops, resident, aliases=(), away=(), leaves=(), copies=0):
    vmem = pl.BlockSpec(memory_space=pltpu.VMEM)
    anywhere = pl.BlockSpec(memory_space=pl.ANY)
    hbm = pl.BlockSpec(memory_space=pltpu.HBM)
    outs = tuple(jax.ShapeDtypeStruct(shape, dtype) for shape, dtype in outs)
    held = size_of(scratch) + 8 * 2**20
    if not resident:
        held = min(held + size_of(outs) + size_of(args), 62 * 2**20)
    in_specs, out_specs = [vmem] * len(args), [vmem] * len(outs)
    for i in away:
        in_specs[i] = hbm
    for o in leaves:
        out_specs[o] = hbm
    for i, o in aliases:
        in_specs[i] = out_specs[o] = anywhere
    return pl.pallas_call(
        body,
        out_shape=outs,
        in_specs=in_specs,
        out_specs=tuple(out_specs),
        scratch_shapes=scratch + [pltpu.SemaphoreType.DMA((copies,))] * (copies > 0),
        input_output_aliases=dict(aliases),
        compiler_params=pltpu.CompilerParams(vmem_limit_bytes=held),
        cost_estimate=pl.CostEstimate(flops=flops, bytes_accessed=2**20, transcendentals=0),
        name=name,
    )(*(pltpu.with_memory_space_constraint(arg, pltpu.HBM) if i in away else arg for i, arg in enumerate(args)))


def shards(queries, keys, values, grad_out, lengths):
    rows = keys.shape[0]
    n_dp, n_ctx = lax.axis_size("dp"), lax.axis_size("ctx")
    axes = ("dp", "ctx")
    flips = Flips(n_ctx)
    ctx = lax.axis_index("ctx")
    many = HEADS * rows
    once = 2 * many * rows * HDIM
    by_row, by_lane = (many, HDIM), (HDIM, many)
    block, pairs = (rows, 2 * HDIM), (many, rows)
    run = functools.partial(call, resident=(n_ctx + 1) * many * rows <= 6 * 2**20)

    def kernel(body, *args, **kwargs):
        return run(functools.partial(body, n_ctx), body.__name__, *args, **kwargs)

    def several(group, shape):
        return ((len(group),) + shape, BF16)

    def swap(blocks, flip):
        return lax.ppermute(blocks, axes, flip_route(n_dp, n_ctx, flip))

    def after(flip):
        return ctx < ctx ^ flip

    kv, = run(join, "join", [(block, BF16)], (keys, values), [], 1, away=(0, 1), copies=2)
    prev = lax.ppermute(kv, axes, run_route(n_dp, n_ctx))
    facts, kv_own, q_s, q_t, do_r, start, level, p_own, acc = kernel(
        prepare, [((8, HDIM), jnp.int32), (block, BF16), (by_row, BF16), (by_lane, BF16), (by_row, BF16),
                  ((rows, rows), jnp.int32), (by_row, F32), (pairs, BF16), ((many, 2 * HDIM), F32)],
        (lengths, queries, grad_out, kv),
        [pltpu.SMEM(lengths.shape, jnp.int32), pltpu.VMEM(queries.shape, BF16), pltpu.VMEM(queries.shape, BF16)], 2 * once,
        away=(0, 1, 2), copies=3)
    got = {flip: swap(jnp.where(after(flip), kv_own, prev), flip) for flip in flips.even}
    passed = swap(jnp.stack([jnp.where(after(1), kv_own, prev)] + [got[flip] for flip in flips.near]), 1)
    kv_first, p_first, acc, facts = kernel(
        attend_first, [several(flips.first, block), several(flips.first, pairs), ((many, 2 * HDIM), F32), (facts.shape, jnp.int32)],
        (facts, q_s, start, level, acc, prev) + tuple(got[flip] for flip in flips.near), [], 2 * len(flips.first) * once)
    kv_last = swap(jnp.where(facts[0, 0] < n_ctx, jnp.stack([got[flip] for flip in flips.far]), 0), 1)
    kv_second, p_second, acc = kernel(
        attend_second, [several(flips.second, block), several(flips.second, pairs), ((many, 2 * HDIM), F32)],
        (facts, q_s, start, level, acc) + tuple(got[flip] for flip in flips.far) + (passed,), [], 2 * len(flips.second) * once)
    out, do_s, do_t, corr, p_last, p_own, p_first, p_second = kernel(
        settle,
        [(queries.shape, BF16), (by_row, BF16), (by_lane, BF16), (by_row, F32), several(flips.last, pairs), (pairs, BF16),
         (p_first.shape, BF16), (p_second.shape, BF16)],
        (facts, q_s, do_r, start, level, acc, kv_own, kv_first, kv_second, kv_last, p_own, p_first, p_second),
        [pltpu.VMEM((many, 2 * HDIM), F32), pltpu.VMEM(by_row, F32), pltpu.VMEM(pairs, BF16), pltpu.VMEM(block, BF16)],
        2 * len(flips.last) * once, aliases=((10, 5), (11, 6), (12, 7)), copies=1)
    shared = (facts, q_t, do_s, do_t, corr)
    attn_out, ds_odd, g_passed = kernel(
        odd, [(queries.shape, BF16), several(flips.odd, pairs), several(flips.odd, block)],
        shared + (kv_second, kv_last, p_second, p_last, out), [], 3 * len(flips.odd) * once, leaves=(0,), copies=1)
    partner = swap(g_passed, 1).astype(F32)
    ds_even, g_direct = kernel(
        even, [several(flips.even, pairs), ((len(flips.even),) + block, F32)],
        shared + (kv_first, kv_second, p_first, p_second), [], 3 * len(flips.even) * once)
    terms = [(1, partner[0])]
    for i, flip in enumerate(flips.even):
        terms.append((flip, swap((g_direct[i] + partner[i + 1]).astype(BF16), flip).astype(F32)))
    grad_queries, g_own, g_prev = kernel(
        rest, [(queries.shape, BF16), (block, F32), (block, F32)],
        shared + (kv_own, kv_first, kv_second, kv_last, p_own, p_first, ds_odd, ds_even),
        [pltpu.VMEM(by_row, F32), pltpu.VMEM((len(flips.odd), rows, HDIM), BF16), pltpu.VMEM((len(flips.even), rows, HDIM), BF16)],
        (n_ctx + 7) * once)
    own_total, prev_total = g_own, g_prev
    for flip, term in terms:
        own_total = own_total + jnp.where(after(flip), term, 0.0)
        prev_total = prev_total + jnp.where(after(flip), 0.0, term)
    back = [(b, a) for a, b in run_route(n_dp, n_ctx)]
    last = lax.ppermute(prev_total.astype(BF16), axes, back)
    grad_keys, grad_values = run(finish, "finish", [(keys.shape, BF16), (values.shape, BF16)], (own_total, last), [], 1)
    return (attn_out, grad_queries, grad_keys, grad_values)


def solution(mesh):
    tokens = P(("dp", "ctx"), None)
    return jax.shard_map(
        shards,
        mesh=mesh,
        in_specs=(tokens, tokens, tokens, tokens, P()),
        out_specs=(tokens, tokens, tokens, tokens),
        check_vma=False,
    )
```

```python
import functools
import math

import jax
import jax.numpy as jnp
from jax import lax
from jax.experimental import pallas as pl
from jax.experimental.pallas import tpu as pltpu
from jax.sharding import PartitionSpec as P

HEADS = 8
HDIM = 128
NEG_FILL = -1e30
SCALE = float(HDIM) ** -0.5
EXP2_SCALE = SCALE * math.log2(math.e)

NT = (((1,), (1,)), ((), ()))
NN = (((1,), (0,)), ((), ()))
F32, BF16 = jnp.float32, jnp.bfloat16


def dot(a, b, dims=NN):
    return lax.dot_general(a, b, dims, preferred_element_type=F32)


def wide(column):
    return jnp.concatenate([column, column], axis=1)


def run_route(n_dp, n_ctx):
    return [(d * n_ctx + c, (d + 1) * n_ctx + c) for d in range(n_dp - 1) for c in range(n_ctx)]


def flip_route(n_dp, n_ctx, flip):
    return [(d * n_ctx + c, d * n_ctx + (c ^ flip)) for d in range(n_dp) for c in range(n_ctx)]


def facts_of(n_ctx, rows, index, lengths_ref):
    base = index * rows
    ends, end = [], jnp.int32(0)
    for i in range(lengths_ref.shape[0]):
        end = end + lengths_ref[i]
        ends.append(end)
    low, high = jnp.int32(0), ends[-1]
    for end in ends:
        low = jnp.where(end <= base, end, low)
    for end in reversed(ends):
        high = jnp.where(end > base, end, high)
    before = lax.div(base - low + rows - 1, rows)
    short = (high - base <= rows - rows // n_ctx).astype(jnp.int32)
    return (lax.rem(index, n_ctx), base, before, short), ends


def straight_route(n_dp, n_ctx, flip):
    pairs = [(d, c, d + int(c > c ^ flip)) for d in range(n_dp) for c in range(n_ctx)]
    return [(d * n_ctx + c, run * n_ctx + (c ^ flip)) for d, c, run in pairs if run < n_dp]


class Place:
    def __init__(self, n_ctx, rows, facts):
        self.n_ctx, self.rows = n_ctx, rows
        self.ctx, self.base, self.before, short = facts if isinstance(facts, tuple) else (facts[i, 0] for i in range(4))
        self.short = short == 1

    def hop(self, back):
        return lax.div(self.ctx ^ lax.rem(self.ctx - back + 2 * self.n_ctx, self.n_ctx), 2)

    def past(self, backs, body):
        first, step = backs[0], backs.step
        count = jnp.clip(lax.div(self.before - first + step, step), 0, len(backs))
        for short in (True, False):
            many = HEADS * (self.rows - self.rows // self.n_ctx if short else self.rows)
            fits = self.short if short else jnp.logical_not(self.short)

            if len(backs) > 1:

                @pl.when(fits)
                def _():
                    @pl.loop(0, lax.div(count, 2))
                    def _(i):
                        body((first + 2 * i * step, first + (2 * i + 1) * step), many)

            @pl.when(fits & (lax.rem(count, 2) == 1))
            def _():
                body((first + (count - 1) * step,), many)

        return count


def chunks(rows, n_ctx):
    size = rows // n_ctx
    for c in range(n_ctx):
        for h in range(HEADS):
            yield (pl.ds((c * HEADS + h) * size, size), (pl.ds(c * size, size), pl.ds(h * HDIM, HDIM)))


def fetch(pairs, sems):
    copies = [pltpu.make_async_copy(source, target, sems.at[i]) for i, (source, target) in enumerate(pairs)]
    for copy in copies:
        copy.start()
    return copies


def join(keys, values, kv, sems):
    for copy in fetch([(keys, kv.at[:, pl.ds(0, HDIM)]), (values, kv.at[:, pl.ds(HDIM, HDIM)])], sems):
        copy.wait()


def ones_beside(values):
    return jnp.concatenate([values, jnp.ones(values.shape, BF16)], axis=1)


def levels(place, back, many, q_s, key_block, start):
    size, rows = place.rows // place.n_ctx, place.rows
    tokens = many // HEADS
    key = place.base - back * rows + lax.broadcasted_iota(jnp.int32, (tokens, rows), 1)
    query = place.base + lax.broadcasted_iota(jnp.int32, (tokens, rows), 0)
    off = jnp.where((key >= start[:tokens, :]) & (key <= query), 0.0, NEG_FILL)
    s = dot(q_s[:many, :], key_block, NT) * EXP2_SCALE
    s = s.reshape(tokens // size, HEADS, size, rows) + off.reshape(tokens // size, 1, size, rows)
    return s.reshape(many, rows)


def fold(s):
    return jnp.maximum(s[:, :HDIM], s[:, HDIM:])


def row_max(s):
    return jnp.broadcast_to(jnp.max(s, axis=1, keepdims=True), (s.shape[0], HDIM))


def prepare(n_ctx, lengths_hbm, q_hbm, do_hbm, kv_ref, facts_ref, kv_own, q_s, q_t, do_r, start, level, p_own, acc,
            lengths_ref, q_ref, do_ref, sems):
    copies = fetch([(lengths_hbm, lengths_ref), (q_hbm, q_ref), (do_hbm, do_ref)], sems)
    rows = q_ref.shape[0]
    index = lax.axis_index("dp") * n_ctx + lax.axis_index("ctx")
    kv_own[...] = kv_ref[...]
    copies[0].wait()
    facts, ends = facts_of(n_ctx, rows, index, lengths_ref)
    place = Place(n_ctx, rows, facts)
    line = lax.broadcasted_iota(jnp.int32, facts_ref.shape, 0)
    held = jnp.zeros(facts_ref.shape, jnp.int32)
    for i, fact in enumerate(facts):
        held = jnp.where(line == i, fact, held)
    facts_ref[...] = held
    token = place.base + lax.broadcasted_iota(jnp.int32, (rows, HDIM), 0)
    begin = jnp.zeros((rows, HDIM), jnp.int32)
    for end in ends:
        begin = jnp.where(token >= end, end, begin)
    start[...] = wide(begin) if rows == 2 * HDIM else jnp.broadcast_to(begin[:, :1], (rows, rows))
    copies[1].wait()
    for here, there in chunks(rows, n_ctx):
        q_s[here, :] = q_ref[there]
    s = levels(place, 0, HEADS * rows, q_s, kv_own[:, :HDIM], start)
    top = row_max(fold(s))
    level[...] = top
    p = jnp.exp2(s - wide(top)).astype(BF16)
    p_own[...] = p
    acc[...] = dot(p, ones_beside(kv_own[:, HDIM:]))
    copies[2].wait()
    for here, there in chunks(rows, n_ctx):
        do_r[here, :] = do_ref[there]
    for h in range(HEADS):
        here = pl.ds(h * rows, rows)
        q_t[:, here] = q_s[here, :].T


def side_by_side(parts, axis):
    return parts[0] if len(parts) == 1 else jnp.concatenate(parts, axis=axis)


def attend(place, backs, many, q_s, kvs, start, level, acc, probs):
    scores = [levels(place, back, many, q_s, kv[:, :HDIM], start) for back, kv in zip(backs, kvs)]
    p = [jnp.exp2(s - wide(level[:many, :])).astype(BF16) for s in scores]
    for ref, part in zip(probs, p):
        ref[:many, :] = part
    acc[:many, :] += dot(side_by_side(p, 1), side_by_side([ones_beside(kv[:, HDIM:]) for kv in kvs], 0))


def attend_even(n_ctx, facts, q_s, start, level, acc_in, *refs):
    *got, kv_even, p_even, acc = refs
    rows = got[0].shape[0]
    place = Place(n_ctx, rows, facts)
    for i, ref in enumerate(got):
        kv_even[i] = ref[...]
    acc[...] = acc_in[...]

    def body(backs, many):
        attend(place, backs, many, q_s, [kv_even.at[place.hop(back)] for back in backs], start, level, acc,
               [p_even.at[lax.div(back, 2) - 1] for back in backs])

    place.past(range(2, n_ctx + 1, 2), body)


def gradients(many, q_t, do_s, do_t, ps, kvs, corr):
    d = [dot(do_s[:many, :], kv[:, HDIM:], NT) for kv in kvs]
    dv = [dot(do_t[:, :many], p) for p in ps]
    ds = [(p.astype(F32) * (each - wide(corr[:many, :]))).astype(BF16) for p, each in zip(ps, d)]
    dk = [dot(q_t[:, :many], each) for each in ds]
    return [(each, jnp.concatenate([k.T, v.T], axis=1)) for each, k, v in zip(ds, dk, dv)]


def forward(n_ctx, facts, q_s, q_t, do_r, start, level, acc_in, kv_own, kv_even, kv_odd, p_own_in, p_even_in,
            o_hbm, ds_odd, do_s, do_t, corr, g_passed, p_own, p_even, o_ref, p_odd, acc, top, p_new, kv_now, sems):
    rows = o_ref.shape[0]
    size = rows // n_ctx
    place = Place(n_ctx, rows, facts)
    pairs = n_ctx // 2
    everything = HEADS * rows
    odd_backs = range(1, n_ctx, 2)
    del p_own_in, p_even_in

    def odd(backs):
        return [kv_odd.at[place.hop(back)] for back in backs]

    def attend_odd(backs, many):
        attend(place, backs, many, q_s, odd(backs), start, level, acc, [p_odd.at[lax.div(back, 2)] for back in backs])

    acc[...] = acc_in[...]
    place.past(odd_backs, attend_odd)

    @pl.when(jnp.logical_not(jnp.max(acc[:, HDIM:]) < 2.0 ** 40))
    def _():
        def each(step):
            @pl.loop(0, place.before + 1)
            def _(back):
                at = place.hop(back)

                @pl.when(back == 0)
                def _():
                    kv_now[...] = kv_own[...]

                @pl.when(lax.rem(back, 2) == 1)
                def _():
                    kv_now[...] = kv_odd[at]

                @pl.when((back > 0) & (lax.rem(back, 2) == 0))
                def _():
                    kv_now[...] = kv_even[at]

                @pl.loop(0, n_ctx)
                def _(c):
                    here = pl.ds(c * HEADS * size, HEADS * size)
                    tokens = pl.ds(c * size, size)
                    key = place.base - back * rows + lax.broadcasted_iota(jnp.int32, (size, rows), 1)
                    query = place.base + c * size + lax.broadcasted_iota(jnp.int32, (size, rows), 0)
                    off = jnp.where((key >= start[tokens, :]) & (key <= query), 0.0, NEG_FILL)
                    s = dot(q_s[here, :], kv_now[:, :HDIM], NT) * EXP2_SCALE
                    step(here, (s.reshape(HEADS, size, rows) + off[None]).reshape(HEADS * size, rows))

                if step is replace:
                    half = lax.div(back, 2)
                    for fits, target in ((back == 0, p_own), (lax.rem(back, 2) == 1, p_odd.at[half]),
                                         ((back > 0) & (lax.rem(back, 2) == 0), p_even.at[jnp.maximum(half - 1, 0)])):

                        @pl.when(fits)
                        def _():
                            copy = pltpu.make_async_copy(p_new, target, sems.at[0])
                            copy.start()
                            copy.wait()

        def highest(here, s):
            top[here, :] = jnp.maximum(top[here, :], row_max(fold(s)))

        def replace(here, s):
            p = jnp.exp2(s - wide(top[here, :])).astype(BF16)
            p_new[here, :] = p
            acc[here, :] += dot(p, ones_beside(kv_now[:, HDIM:]))

        @pl.loop(0, n_ctx)
        def _(c):
            here = pl.ds(c * HEADS * size, HEADS * size)
            top[here, :] = jnp.full((HEADS * size, HDIM), NEG_FILL, F32)
            acc[here, :] = jnp.zeros((HEADS * size, 2 * HDIM), F32)

        each(highest)
        each(replace)

    for i in range(0, everything, rows):
        here = pl.ds(i, rows)
        total = acc[here, :]
        inverse = 1.0 / total[:, HDIM:]
        out = (total[:, :HDIM] * inverse).astype(BF16)
        grad = do_r[here, :].astype(F32)
        corr[here, :] = jnp.sum(grad * out.astype(F32), axis=1, keepdims=True) * inverse
        scaled = grad * inverse
        do_s[here, :] = scaled.astype(BF16)
        do_t[:, here] = scaled.T.astype(BF16)
        for part, there in chunks(rows, n_ctx):
            if i <= part.start < i + rows:
                o_ref[there] = out[part.start - i:part.start - i + size, :]

    leaving = pltpu.make_async_copy(o_ref, o_hbm, sems.at[1])
    leaving.start()

    def backward(backs, many):
        ps = [p_odd[lax.div(back, 2), :many, :] for back in backs]
        for back, (ds, terms) in zip(backs, gradients(many, q_t, do_s, do_t, ps, odd(backs), corr)):
            ds_odd[lax.div(back, 2), :many, :] = ds
            g_passed[place.hop(back)] = terms.astype(BF16)

    done = place.past(odd_backs, backward)

    @pl.loop(done, pairs)
    def _(i):
        g_passed[place.hop(2 * i + 1)] = jnp.zeros((rows, 2 * HDIM), BF16)

    leaving.wait()


def even(n_ctx, facts, q_t, do_s, do_t, kv_even, p_even, corr, ds_even, g_direct):
    rows = kv_even.shape[1]
    place = Place(n_ctx, rows, facts)

    def backward(backs, many):
        ps = [p_even[lax.div(back, 2) - 1, :many, :] for back in backs]
        kvs = [kv_even.at[place.hop(back)] for back in backs]
        for back, (ds, terms) in zip(backs, gradients(many, q_t, do_s, do_t, ps, kvs, corr)):
            ds_even[lax.div(back, 2) - 1, :many, :] = ds
            g_direct[place.hop(back) - 1] = terms

    done = place.past(range(2, n_ctx, 2), backward)

    @pl.loop(done, n_ctx // 2 - 1)
    def _(i):
        g_direct[place.hop(2 * i + 2) - 1] = jnp.zeros((rows, 2 * HDIM), F32)


def rest(n_ctx, facts, q_t, do_s, do_t, kv_even, p_even, corr, kv_own, p_own, kv_odd, ds_odd, ds_even,
         dq_ref, g_own, g_prev, dq_acc):
    rows = kv_own.shape[0]
    place = Place(n_ctx, rows, facts)

    (ds, g_own[...]), = gradients(HEADS * rows, q_t, do_s, do_t, [p_own[...]], [kv_own], corr)
    dq_acc[...] = dot(ds, kv_own[:, :HDIM])

    def add(backs, many, ds, kv):
        dq_acc[:many, :] += dot(side_by_side([ds(back)[:many, :] for back in backs], 1),
                                side_by_side([kv[place.hop(back), :, :HDIM] for back in backs], 0))

    def add_odd(backs, many):
        add(backs, many, lambda back: ds_odd.at[lax.div(back, 2)], kv_odd)

    def add_even(backs, many):
        add(backs, many, lambda back: ds_even.at[lax.div(back, 2) - 1], kv_even)

    def farthest(backs, many):
        at = place.hop(backs[0])
        (ds, g_prev[...]), = gradients(many, q_t, do_s, do_t, [p_even[n_ctx // 2 - 1, :many, :]], [kv_even.at[at]], corr)
        dq_acc[:many, :] += dot(ds, kv_even[at, :, :HDIM])

    place.past(range(1, n_ctx, 2), add_odd)
    place.past(range(2, n_ctx, 2), add_even)
    g_prev[...] = jnp.zeros(g_prev.shape, F32)
    place.past(range(n_ctx, n_ctx + 1), farthest)

    for here, there in chunks(rows, n_ctx):
        dq_ref[there] = (dq_acc[here, :] * SCALE).astype(BF16)


def finish(total, last, gk_ref, gv_ref):
    terms = total[...] + last[...].astype(F32)
    gk_ref[...] = (terms[:, :HDIM] * SCALE).astype(BF16)
    gv_ref[...] = terms[:, HDIM:].astype(BF16)


def size_of(arrays):
    return sum(math.prod(array.shape) * jnp.dtype(array.dtype).itemsize for array in arrays)


def call(body, name, outs, args, scratch, flops, resident, aliases=(), away=(), leaves=(), copies=0):
    vmem = pl.BlockSpec(memory_space=pltpu.VMEM)
    anywhere = pl.BlockSpec(memory_space=pl.ANY)
    hbm = pl.BlockSpec(memory_space=pltpu.HBM)
    outs = tuple(jax.ShapeDtypeStruct(shape, dtype) for shape, dtype in outs)
    held = size_of(scratch) + 8 * 2**20
    if not resident:
        held = min(held + size_of(outs) + size_of(args), 62 * 2**20)
    in_specs, out_specs = [vmem] * len(args), [vmem] * len(outs)
    for i in away:
        in_specs[i] = hbm
    for o in leaves:
        out_specs[o] = hbm
    for i, o in aliases:
        in_specs[i] = out_specs[o] = anywhere
    return pl.pallas_call(
        body,
        out_shape=outs,
        in_specs=in_specs,
        out_specs=tuple(out_specs),
        scratch_shapes=scratch + [pltpu.SemaphoreType.DMA((copies,))] * (copies > 0),
        input_output_aliases=dict(aliases),
        compiler_params=pltpu.CompilerParams(vmem_limit_bytes=held),
        cost_estimate=pl.CostEstimate(flops=flops, bytes_accessed=2**20, transcendentals=0),
        name=name,
    )(*(pltpu.with_memory_space_constraint(arg, pltpu.HBM) if i in away else arg for i, arg in enumerate(args)))


def shards(queries, keys, values, grad_out, lengths):
    rows = keys.shape[0]
    n_dp, n_ctx = lax.axis_size("dp"), lax.axis_size("ctx")
    axes = ("dp", "ctx")
    pairs = n_ctx // 2
    ctx = lax.axis_index("ctx")
    many = HEADS * rows
    once = 2 * many * rows * HDIM
    by_row, by_lane = (many, HDIM), (HDIM, many)
    block = (rows, 2 * HDIM)
    run = functools.partial(call, resident=(n_ctx + 1) * many * rows <= 6 * 2**20)
    def kernel(body, *args, **kwargs):
        return run(functools.partial(body, n_ctx), body.__name__, *args, **kwargs)

    def swap(blocks, flip):
        return lax.ppermute(blocks, axes, flip_route(n_dp, n_ctx, flip))

    later = [ctx < ctx ^ max(2 * i, 1) for i in range(pairs)]

    kv, = run(join, "join", [(block, BF16)], (keys, values), [], 1, away=(0, 1), copies=2)
    near = lambda i: i & (i - 1) == 0
    prev = lax.ppermute(kv, axes, run_route(n_dp, n_ctx))
    straight = {i: lax.ppermute(kv, axes, straight_route(n_dp, n_ctx, 2 * i)) for i in range(1, pairs) if not near(i)}
    facts, kv_own, q_s, q_t, do_r, start, level, p_own, acc = kernel(
        prepare, [((8, HDIM), jnp.int32), (block, BF16), (by_row, BF16), (by_lane, BF16), (by_row, BF16),
                  ((rows, rows), jnp.int32), (by_row, F32), ((many, rows), BF16), ((many, 2 * HDIM), F32)],
        (lengths, queries, grad_out, kv),
        [pltpu.SMEM(lengths.shape, jnp.int32), pltpu.VMEM(queries.shape, BF16), pltpu.VMEM(queries.shape, BF16)], 2 * once,
        away=(0, 1, 2), copies=3)
    sent = [jnp.where(after, kv_own, prev) for after in later]
    got = [prev] + [swap(sent[i], 2 * i) if near(i) else straight[i] for i in range(1, pairs)]
    passed = swap(jnp.stack(sent[:1] + got[1:]), 1)
    kv_even, p_even, acc = kernel(
        attend_even, [((pairs,) + block, BF16), ((pairs, many, rows), BF16), ((many, 2 * HDIM), F32)],
        (facts, q_s, start, level, acc, *got), [], 2 * pairs * once)
    attn_out, ds_odd, do_s, do_t, corr, g_passed, p_own, p_even = kernel(
        forward,
        [(queries.shape, BF16), ((pairs, many, rows), BF16),
         (by_row, BF16), (by_lane, BF16), (by_row, F32), ((pairs,) + block, BF16), (p_own.shape, BF16), (p_even.shape, BF16)],
        (facts, q_s, q_t, do_r, start, level, acc, kv_own, kv_even, passed, p_own, p_even),
        [pltpu.VMEM(queries.shape, BF16), pltpu.VMEM((pairs, many, rows), BF16), pltpu.VMEM((many, 2 * HDIM), F32),
         pltpu.VMEM(by_row, F32), pltpu.VMEM((many, rows), BF16), pltpu.VMEM(block, BF16)],
        5 * pairs * once, aliases=((10, 6), (11, 7)), leaves=(0,), copies=2)
    partner = swap(g_passed, 1).astype(F32)
    shared = (facts, q_t, do_s, do_t, kv_even, p_even, corr)
    ds_even, g_direct = kernel(even, [((pairs - 1, many, rows), BF16), ((pairs - 1,) + block, F32)],
                               shared, [], 3 * (pairs - 1) * once)
    terms = [partner[0]] + [swap((g_direct[i - 1] + partner[i]).astype(BF16), 2 * i).astype(F32) for i in range(1, pairs)]
    grad_queries, g_own, g_prev = kernel(rest, [(queries.shape, BF16), (block, F32), (block, F32)],
                                         shared + (kv_own, p_own, passed, ds_odd, ds_even),
                                         [pltpu.VMEM(by_row, F32)], (n_ctx + 7) * once)
    own_total, prev_total = g_own, g_prev
    for after, term in zip(later, terms):
        own_total = own_total + jnp.where(after, term, 0.0)
        prev_total = prev_total + jnp.where(after, 0.0, term)
    back = [(b, a) for a, b in run_route(n_dp, n_ctx)]
    last = lax.ppermute(prev_total.astype(BF16), axes, back)
    grad_keys, grad_values = run(finish, "finish", [(keys.shape, BF16), (values.shape, BF16)], (own_total, last), [], 1)
    return (attn_out, grad_queries, grad_keys, grad_values)


def solution(mesh):
    tokens = P(("dp", "ctx"), None)
    return jax.shard_map(
        shards,
        mesh=mesh,
        in_specs=(tokens, tokens, tokens, tokens, P()),
        out_specs=(tokens, tokens, tokens, tokens),
        check_vma=False,
    )
```

```python
import functools
import math

import jax
import jax.numpy as jnp
from jax import lax
from jax.experimental import pallas as pl
from jax.experimental.pallas import tpu as pltpu
from jax.sharding import PartitionSpec as P

HEADS = 8
HDIM = 128
NEG_FILL = -1e30
SCALE = float(HDIM) ** -0.5
EXP2_SCALE = SCALE * math.log2(math.e)

NT = (((1,), (1,)), ((), ()))
NN = (((1,), (0,)), ((), ()))
F32, BF16 = jnp.float32, jnp.bfloat16


def dot(a, b, dims=NN):
    return lax.dot_general(a, b, dims, preferred_element_type=F32)


def wide(column):
    return jnp.concatenate([column, column], axis=1)


def run_route(n_dp, n_ctx):
    return [(d * n_ctx + c, (d + 1) * n_ctx + c) for d in range(n_dp - 1) for c in range(n_ctx)]


def flip_route(n_dp, n_ctx, flip):
    return [(d * n_ctx + c, d * n_ctx + (c ^ flip)) for d in range(n_dp) for c in range(n_ctx)]


def facts_of(n_ctx, rows, index, lengths_ref):
    base = index * rows
    ends, end = [], jnp.int32(0)
    for i in range(lengths_ref.shape[0]):
        end = end + lengths_ref[i]
        ends.append(end)
    low, high = jnp.int32(0), ends[-1]
    for end in ends:
        low = jnp.where(end <= base, end, low)
    for end in reversed(ends):
        high = jnp.where(end > base, end, high)
    before = lax.div(base - low + rows - 1, rows)
    short = (high - base <= rows - rows // n_ctx).astype(jnp.int32)
    return (lax.rem(index, n_ctx), base, before, short), ends


def straight_route(n_dp, n_ctx, flip):
    pairs = [(d, c, d + int(c > c ^ flip)) for d in range(n_dp) for c in range(n_ctx)]
    return [(d * n_ctx + c, run * n_ctx + (c ^ flip)) for d, c, run in pairs if run < n_dp]


class Place:
    def __init__(self, n_ctx, rows, facts):
        self.n_ctx, self.rows = n_ctx, rows
        self.ctx, self.base, self.before, short = facts if isinstance(facts, tuple) else (facts[i, 0] for i in range(4))
        self.short = short == 1

    def hop(self, back):
        return lax.div(self.ctx ^ lax.rem(self.ctx - back + 2 * self.n_ctx, self.n_ctx), 2)

    def past(self, backs, body):
        first, step = backs[0], backs.step
        count = jnp.clip(lax.div(self.before - first + step, step), 0, len(backs))
        for short in (True, False):
            many = HEADS * (self.rows - self.rows // self.n_ctx if short else self.rows)
            fits = self.short if short else jnp.logical_not(self.short)

            if len(backs) > 1:

                @pl.when(fits)
                def _():
                    @pl.loop(0, lax.div(count, 2))
                    def _(i):
                        body((first + 2 * i * step, first + (2 * i + 1) * step), many)

            @pl.when(fits & (lax.rem(count, 2) == 1))
            def _():
                body((first + (count - 1) * step,), many)

        return count


def chunks(rows, n_ctx):
    size = rows // n_ctx
    for c in range(n_ctx):
        for h in range(HEADS):
            yield (pl.ds((c * HEADS + h) * size, size), (pl.ds(c * size, size), pl.ds(h * HDIM, HDIM)))


def fetch(pairs, sems):
    copies = [pltpu.make_async_copy(source, target, sems.at[i]) for i, (source, target) in enumerate(pairs)]
    for copy in copies:
        copy.start()
    return copies


def join(keys, values, kv, sems):
    for copy in fetch([(keys, kv.at[:, pl.ds(0, HDIM)]), (values, kv.at[:, pl.ds(HDIM, HDIM)])], sems):
        copy.wait()


def ones_beside(values):
    return jnp.concatenate([values, jnp.ones(values.shape, BF16)], axis=1)


def levels(place, back, many, q_s, key_block, start):
    size, rows = place.rows // place.n_ctx, place.rows
    tokens = many // HEADS
    key = place.base - back * rows + lax.broadcasted_iota(jnp.int32, (tokens, rows), 1)
    query = place.base + lax.broadcasted_iota(jnp.int32, (tokens, rows), 0)
    off = jnp.where((key >= start[:tokens, :]) & (key <= query), 0.0, NEG_FILL)
    s = dot(q_s[:many, :], key_block, NT) * EXP2_SCALE
    s = s.reshape(tokens // size, HEADS, size, rows) + off.reshape(tokens // size, 1, size, rows)
    return s.reshape(many, rows)


def fold(s):
    return jnp.maximum(s[:, :HDIM], s[:, HDIM:])


def row_max(s):
    return jnp.broadcast_to(jnp.max(s, axis=1, keepdims=True), (s.shape[0], HDIM))


def prepare(n_ctx, lengths_hbm, q_hbm, do_hbm, kv_ref, facts_ref, kv_own, q_s, q_t, do_r, start, level, p_own, acc,
            lengths_ref, q_ref, do_ref, sems):
    copies = fetch([(lengths_hbm, lengths_ref), (q_hbm, q_ref), (do_hbm, do_ref)], sems)
    rows = q_ref.shape[0]
    index = lax.axis_index("dp") * n_ctx + lax.axis_index("ctx")
    kv_own[...] = kv_ref[...]
    copies[0].wait()
    facts, ends = facts_of(n_ctx, rows, index, lengths_ref)
    place = Place(n_ctx, rows, facts)
    line = lax.broadcasted_iota(jnp.int32, facts_ref.shape, 0)
    held = jnp.zeros(facts_ref.shape, jnp.int32)
    for i, fact in enumerate(facts):
        held = jnp.where(line == i, fact, held)
    facts_ref[...] = held
    token = place.base + lax.broadcasted_iota(jnp.int32, (rows, HDIM), 0)
    begin = jnp.zeros((rows, HDIM), jnp.int32)
    for end in ends:
        begin = jnp.where(token >= end, end, begin)
    start[...] = wide(begin) if rows == 2 * HDIM else jnp.broadcast_to(begin[:, :1], (rows, rows))
    copies[1].wait()
    for here, there in chunks(rows, n_ctx):
        q_s[here, :] = q_ref[there]
    s = levels(place, 0, HEADS * rows, q_s, kv_own[:, :HDIM], start)
    top = row_max(fold(s))
    level[...] = top
    p = jnp.exp2(s - wide(top)).astype(BF16)
    p_own[...] = p
    acc[...] = dot(p, ones_beside(kv_own[:, HDIM:]))
    copies[2].wait()
    for here, there in chunks(rows, n_ctx):
        do_r[here, :] = do_ref[there]
    for h in range(HEADS):
        here = pl.ds(h * rows, rows)
        q_t[:, here] = q_s[here, :].T


def side_by_side(parts, axis):
    return parts[0] if len(parts) == 1 else jnp.concatenate(parts, axis=axis)


def attend(place, backs, many, q_s, kvs, start, level, acc, probs):
    scores = [levels(place, back, many, q_s, kv[:, :HDIM], start) for back, kv in zip(backs, kvs)]
    p = [jnp.exp2(s - wide(level[:many, :])).astype(BF16) for s in scores]
    for ref, part in zip(probs, p):
        ref[:many, :] = part
    acc[:many, :] += dot(side_by_side(p, 1), side_by_side([ones_beside(kv[:, HDIM:]) for kv in kvs], 0))


def attend_even(n_ctx, facts, q_s, start, level, acc_in, *refs):
    *got, kv_even, p_even, acc = refs
    rows = got[0].shape[0]
    place = Place(n_ctx, rows, facts)
    for i, ref in enumerate(got):
        kv_even[i] = ref[...]
    acc[...] = acc_in[...]

    def body(backs, many):
        attend(place, backs, many, q_s, [kv_even.at[place.hop(back)] for back in backs], start, level, acc,
               [p_even.at[lax.div(back, 2) - 1] for back in backs])

    place.past(range(2, n_ctx + 1, 2), body)


def gradients(many, q_t, do_s, do_t, ps, kvs, corr):
    d = [dot(do_s[:many, :], kv[:, HDIM:], NT) for kv in kvs]
    dv = [dot(do_t[:, :many], p) for p in ps]
    ds = [(p.astype(F32) * (each - wide(corr[:many, :]))).astype(BF16) for p, each in zip(ps, d)]
    dk = [dot(q_t[:, :many], each) for each in ds]
    return [(each, jnp.concatenate([k.T, v.T], axis=1)) for each, k, v in zip(ds, dk, dv)]


def forward(n_ctx, facts, q_s, q_t, do_r, start, level, acc_in, kv_own, kv_even, kv_odd, p_own_in, p_even_in,
            o_hbm, k_odd, ds_odd, do_s, do_t, corr, g_passed, p_own, p_even, o_ref, p_odd, acc, top, p_new, kv_now, sems):
    rows = o_ref.shape[0]
    size = rows // n_ctx
    place = Place(n_ctx, rows, facts)
    pairs = n_ctx // 2
    everything = HEADS * rows
    odd_backs = range(1, n_ctx, 2)
    del p_own_in, p_even_in

    for i in range(pairs):
        k_odd[i] = kv_odd[i, :, :HDIM]

    def odd(backs):
        return [kv_odd.at[place.hop(back)] for back in backs]

    def attend_odd(backs, many):
        attend(place, backs, many, q_s, odd(backs), start, level, acc, [p_odd.at[lax.div(back, 2)] for back in backs])

    acc[...] = acc_in[...]
    place.past(odd_backs, attend_odd)

    @pl.when(jnp.logical_not(jnp.max(acc[:, HDIM:]) < 2.0 ** 40))
    def _():
        def each(step):
            @pl.loop(0, place.before + 1)
            def _(back):
                at = place.hop(back)

                @pl.when(back == 0)
                def _():
                    kv_now[...] = kv_own[...]

                @pl.when(lax.rem(back, 2) == 1)
                def _():
                    kv_now[...] = kv_odd[at]

                @pl.when((back > 0) & (lax.rem(back, 2) == 0))
                def _():
                    kv_now[...] = kv_even[at]

                @pl.loop(0, n_ctx)
                def _(c):
                    here = pl.ds(c * HEADS * size, HEADS * size)
                    tokens = pl.ds(c * size, size)
                    key = place.base - back * rows + lax.broadcasted_iota(jnp.int32, (size, rows), 1)
                    query = place.base + c * size + lax.broadcasted_iota(jnp.int32, (size, rows), 0)
                    off = jnp.where((key >= start[tokens, :]) & (key <= query), 0.0, NEG_FILL)
                    s = dot(q_s[here, :], kv_now[:, :HDIM], NT) * EXP2_SCALE
                    step(here, (s.reshape(HEADS, size, rows) + off[None]).reshape(HEADS * size, rows))

                if step is replace:
                    half = lax.div(back, 2)
                    for fits, target in ((back == 0, p_own), (lax.rem(back, 2) == 1, p_odd.at[half]),
                                         ((back > 0) & (lax.rem(back, 2) == 0), p_even.at[jnp.maximum(half - 1, 0)])):

                        @pl.when(fits)
                        def _():
                            copy = pltpu.make_async_copy(p_new, target, sems.at[0])
                            copy.start()
                            copy.wait()

        def highest(here, s):
            top[here, :] = jnp.maximum(top[here, :], row_max(fold(s)))

        def replace(here, s):
            p = jnp.exp2(s - wide(top[here, :])).astype(BF16)
            p_new[here, :] = p
            acc[here, :] += dot(p, ones_beside(kv_now[:, HDIM:]))

        @pl.loop(0, n_ctx)
        def _(c):
            here = pl.ds(c * HEADS * size, HEADS * size)
            top[here, :] = jnp.full((HEADS * size, HDIM), NEG_FILL, F32)
            acc[here, :] = jnp.zeros((HEADS * size, 2 * HDIM), F32)

        each(highest)
        each(replace)

    for i in range(0, everything, rows):
        here = pl.ds(i, rows)
        total = acc[here, :]
        inverse = 1.0 / total[:, HDIM:]
        out = (total[:, :HDIM] * inverse).astype(BF16)
        grad = do_r[here, :].astype(F32)
        corr[here, :] = jnp.sum(grad * out.astype(F32), axis=1, keepdims=True) * inverse
        scaled = grad * inverse
        do_s[here, :] = scaled.astype(BF16)
        do_t[:, here] = scaled.T.astype(BF16)
        for part, there in chunks(rows, n_ctx):
            if i <= part.start < i + rows:
                o_ref[there] = out[part.start - i:part.start - i + size, :]

    leaving = pltpu.make_async_copy(o_ref, o_hbm, sems.at[1])
    leaving.start()

    def backward(backs, many):
        ps = [p_odd[lax.div(back, 2), :many, :] for back in backs]
        for back, (ds, terms) in zip(backs, gradients(many, q_t, do_s, do_t, ps, odd(backs), corr)):
            ds_odd[lax.div(back, 2), :many, :] = ds
            g_passed[place.hop(back)] = terms.astype(BF16)

    done = place.past(odd_backs, backward)

    @pl.loop(done, pairs)
    def _(i):
        g_passed[place.hop(2 * i + 1)] = jnp.zeros((rows, 2 * HDIM), BF16)

    leaving.wait()


def even(n_ctx, facts, q_t, do_s, do_t, kv_even, p_even, corr, ds_even, g_direct):
    rows = kv_even.shape[1]
    place = Place(n_ctx, rows, facts)

    def backward(backs, many):
        ps = [p_even[lax.div(back, 2) - 1, :many, :] for back in backs]
        kvs = [kv_even.at[place.hop(back)] for back in backs]
        for back, (ds, terms) in zip(backs, gradients(many, q_t, do_s, do_t, ps, kvs, corr)):
            ds_even[lax.div(back, 2) - 1, :many, :] = ds
            g_direct[place.hop(back) - 1] = terms

    done = place.past(range(2, n_ctx, 2), backward)

    @pl.loop(done, n_ctx // 2 - 1)
    def _(i):
        g_direct[place.hop(2 * i + 2) - 1] = jnp.zeros((rows, 2 * HDIM), F32)


def rest(n_ctx, facts, q_t, do_s, do_t, kv_even, p_even, corr, kv_own, p_own, k_odd, ds_odd, ds_even,
         dq_ref, g_own, g_prev, dq_acc):
    rows = kv_own.shape[0]
    place = Place(n_ctx, rows, facts)

    (ds, g_own[...]), = gradients(HEADS * rows, q_t, do_s, do_t, [p_own[...]], [kv_own], corr)
    dq_acc[...] = dot(ds, kv_own[:, :HDIM])

    def add(backs, many, ds, kv):
        dq_acc[:many, :] += dot(side_by_side([ds(back)[:many, :] for back in backs], 1),
                                side_by_side([kv[place.hop(back), :, :HDIM] for back in backs], 0))

    def add_odd(backs, many):
        add(backs, many, lambda back: ds_odd.at[lax.div(back, 2)], k_odd)

    def add_even(backs, many):
        add(backs, many, lambda back: ds_even.at[lax.div(back, 2) - 1], kv_even)

    def farthest(backs, many):
        at = place.hop(backs[0])
        (ds, g_prev[...]), = gradients(many, q_t, do_s, do_t, [p_even[n_ctx // 2 - 1, :many, :]], [kv_even.at[at]], corr)
        dq_acc[:many, :] += dot(ds, kv_even[at, :, :HDIM])

    place.past(range(1, n_ctx, 2), add_odd)
    place.past(range(2, n_ctx, 2), add_even)
    g_prev[...] = jnp.zeros(g_prev.shape, F32)
    place.past(range(n_ctx, n_ctx + 1), farthest)

    for here, there in chunks(rows, n_ctx):
        dq_ref[there] = (dq_acc[here, :] * SCALE).astype(BF16)


def finish(total, last, gk_ref, gv_ref):
    terms = total[...] + last[...].astype(F32)
    gk_ref[...] = (terms[:, :HDIM] * SCALE).astype(BF16)
    gv_ref[...] = terms[:, HDIM:].astype(BF16)


def size_of(arrays):
    return sum(math.prod(array.shape) * jnp.dtype(array.dtype).itemsize for array in arrays)


def call(body, name, outs, args, scratch, flops, resident, aliases=(), away=(), leaves=(), final=(), copies=0):
    vmem = pl.BlockSpec(memory_space=pltpu.VMEM)
    anywhere = pl.BlockSpec(memory_space=pl.ANY)
    hbm = pl.BlockSpec(memory_space=pltpu.HBM)
    outs = tuple(jax.ShapeDtypeStruct(shape, dtype) if i in final or not resident else pltpu.VMEM(shape, dtype)
                 for i, (shape, dtype) in enumerate(outs))
    held = size_of(scratch) + 8 * 2**20
    if not resident:
        held = min(held + size_of(outs) + size_of(args), 62 * 2**20)
    in_specs, out_specs = [vmem] * len(args), [vmem] * len(outs)
    for i in away:
        in_specs[i] = hbm
    for o in leaves:
        out_specs[o] = hbm
    for i, o in aliases:
        in_specs[i] = out_specs[o] = anywhere
    return pl.pallas_call(
        body,
        out_shape=outs,
        in_specs=in_specs,
        out_specs=tuple(out_specs),
        scratch_shapes=scratch + [pltpu.SemaphoreType.DMA((copies,))] * (copies > 0),
        input_output_aliases=dict(aliases),
        compiler_params=pltpu.CompilerParams(vmem_limit_bytes=held),
        cost_estimate=pl.CostEstimate(flops=flops, bytes_accessed=2**20, transcendentals=0),
        name=name,
    )(*(pltpu.with_memory_space_constraint(arg, pltpu.HBM) if i in away else arg for i, arg in enumerate(args)))


def shards(queries, keys, values, grad_out, lengths):
    rows = keys.shape[0]
    n_dp, n_ctx = lax.axis_size("dp"), lax.axis_size("ctx")
    axes = ("dp", "ctx")
    pairs = n_ctx // 2
    ctx = lax.axis_index("ctx")
    many = HEADS * rows
    once = 2 * many * rows * HDIM
    by_row, by_lane = (many, HDIM), (HDIM, many)
    block = (rows, 2 * HDIM)
    run = functools.partial(call, resident=(n_ctx + 1) * many * rows <= 6 * 2**20)
    def kernel(body, *args, **kwargs):
        return run(functools.partial(body, n_ctx), body.__name__, *args, **kwargs)

    def swap(blocks, flip):
        return lax.ppermute(blocks, axes, flip_route(n_dp, n_ctx, flip))

    later = [ctx < ctx ^ max(2 * i, 1) for i in range(pairs)]

    kv, = run(join, "join", [(block, BF16)], (keys, values), [], 1, away=(0, 1), copies=2)
    near = lambda i: i & (i - 1) == 0
    prev = lax.ppermute(kv, axes, run_route(n_dp, n_ctx))
    straight = {i: lax.ppermute(kv, axes, straight_route(n_dp, n_ctx, 2 * i)) for i in range(1, pairs) if not near(i)}
    facts, kv_own, q_s, q_t, do_r, start, level, p_own, acc = kernel(
        prepare, [((8, HDIM), jnp.int32), (block, BF16), (by_row, BF16), (by_lane, BF16), (by_row, BF16),
                  ((rows, rows), jnp.int32), (by_row, F32), ((many, rows), BF16), ((many, 2 * HDIM), F32)],
        (lengths, queries, grad_out, kv),
        [pltpu.SMEM(lengths.shape, jnp.int32), pltpu.VMEM(queries.shape, BF16), pltpu.VMEM(queries.shape, BF16)], 2 * once,
        away=(0, 1, 2), copies=3)
    sent = [jnp.where(after, kv_own, prev) for after in later]
    got = [prev] + [swap(sent[i], 2 * i) if near(i) else straight[i] for i in range(1, pairs)]
    passed = swap(jnp.stack(sent[:1] + got[1:]), 1)
    kv_even, p_even, acc = kernel(
        attend_even, [((pairs,) + block, BF16), ((pairs, many, rows), BF16), ((many, 2 * HDIM), F32)],
        (facts, q_s, start, level, acc, *got), [], 2 * pairs * once)
    attn_out, k_odd, ds_odd, do_s, do_t, corr, g_passed, p_own, p_even = kernel(
        forward,
        [(queries.shape, BF16), ((pairs, rows, HDIM), BF16), ((pairs, many, rows), BF16),
         (by_row, BF16), (by_lane, BF16), (by_row, F32), ((pairs,) + block, BF16), (p_own.shape, BF16), (p_even.shape, BF16)],
        (facts, q_s, q_t, do_r, start, level, acc, kv_own, kv_even, passed, p_own, p_even),
        [pltpu.VMEM(queries.shape, BF16), pltpu.VMEM((pairs, many, rows), BF16), pltpu.VMEM((many, 2 * HDIM), F32),
         pltpu.VMEM(by_row, F32), pltpu.VMEM((many, rows), BF16), pltpu.VMEM(block, BF16)],
        5 * pairs * once, aliases=((10, 7), (11, 8)), leaves=(0,), final=(0,), copies=2)
    partner = swap(g_passed, 1).astype(F32)
    shared = (facts, q_t, do_s, do_t, kv_even, p_even, corr)
    ds_even, g_direct = kernel(even, [((pairs - 1, many, rows), BF16), ((pairs - 1,) + block, F32)],
                               shared, [], 3 * (pairs - 1) * once)
    terms = [partner[0]] + [swap((g_direct[i - 1] + partner[i]).astype(BF16), 2 * i).astype(F32) for i in range(1, pairs)]
    grad_queries, g_own, g_prev = kernel(rest, [(queries.shape, BF16), (block, F32), (block, F32)],
                                         shared + (kv_own, p_own, k_odd, ds_odd, ds_even),
                                         [pltpu.VMEM(by_row, F32)], (n_ctx + 7) * once, final=(0,))
    own_total, prev_total = g_own, g_prev
    for after, term in zip(later, terms):
        own_total = own_total + jnp.where(after, term, 0.0)
        prev_total = prev_total + jnp.where(after, 0.0, term)
    back = [(b, a) for a, b in run_route(n_dp, n_ctx)]
    last = lax.ppermute(prev_total.astype(BF16), axes, back)
    grad_keys, grad_values = run(finish, "finish", [(keys.shape, BF16), (values.shape, BF16)], (own_total, last), [], 1, final=(0, 1))
    return (attn_out, grad_queries, grad_keys, grad_values)


def solution(mesh):
    tokens = P(("dp", "ctx"), None)
    return jax.shard_map(
        shards,
        mesh=mesh,
        in_specs=(tokens, tokens, tokens, tokens, P()),
        out_specs=(tokens, tokens, tokens, tokens),
        check_vma=False,
    )
```

```python
import functools
import math

import jax
import jax.numpy as jnp
from jax import lax
from jax.experimental import pallas as pl
from jax.experimental.pallas import tpu as pltpu
from jax.sharding import PartitionSpec as P

HEADS = 8
HDIM = 128
NEG_FILL = -1e30
SCALE = float(HDIM) ** -0.5
EXP2_SCALE = SCALE * math.log2(math.e)

NT = (((1,), (1,)), ((), ()))
NN = (((1,), (0,)), ((), ()))
F32, BF16 = jnp.float32, jnp.bfloat16


def dot(a, b, dims=NN):
    return lax.dot_general(a, b, dims, preferred_element_type=F32)


def wide(column):
    return jnp.concatenate([column, column], axis=1)


def run_route(n_dp, n_ctx):
    return [(d * n_ctx + c, (d + 1) * n_ctx + c) for d in range(n_dp - 1) for c in range(n_ctx)]


def flip_route(n_dp, n_ctx, flip):
    return [(d * n_ctx + c, d * n_ctx + (c ^ flip)) for d in range(n_dp) for c in range(n_ctx)]


def facts_of(n_ctx, rows, index, lengths_ref):
    base = index * rows
    ends, end = [], jnp.int32(0)
    for i in range(lengths_ref.shape[0]):
        end = end + lengths_ref[i]
        ends.append(end)
    low, high = jnp.int32(0), ends[-1]
    for end in ends:
        low = jnp.where(end <= base, end, low)
    for end in reversed(ends):
        high = jnp.where(end > base, end, high)
    before = lax.div(base - low + rows - 1, rows)
    short = (high - base <= rows - rows // n_ctx).astype(jnp.int32)
    return (lax.rem(index, n_ctx), base, before, short), ends


def straight_route(n_dp, n_ctx, flip):
    pairs = [(d, c, d + int(c > c ^ flip)) for d in range(n_dp) for c in range(n_ctx)]
    return [(d * n_ctx + c, run * n_ctx + (c ^ flip)) for d, c, run in pairs if run < n_dp]


class Place:
    def __init__(self, n_ctx, rows, facts):
        self.n_ctx, self.rows = n_ctx, rows
        self.ctx, self.base, self.before, short = facts if isinstance(facts, tuple) else (facts[i, 0] for i in range(4))
        self.short = short == 1

    def hop(self, back):
        return lax.div(self.ctx ^ lax.rem(self.ctx - back + 2 * self.n_ctx, self.n_ctx), 2)

    def past(self, backs, body):
        first, step = backs[0], backs.step
        count = jnp.clip(lax.div(self.before - first + step, step), 0, len(backs))
        for short in (True, False):
            many = HEADS * (self.rows - self.rows // self.n_ctx if short else self.rows)
            fits = self.short if short else jnp.logical_not(self.short)

            if len(backs) > 1:

                @pl.when(fits)
                def _():
                    @pl.loop(0, lax.div(count, 2))
                    def _(i):
                        body((first + 2 * i * step, first + (2 * i + 1) * step), many)

            @pl.when(fits & (lax.rem(count, 2) == 1))
            def _():
                body((first + (count - 1) * step,), many)

        return count


def chunks(rows, n_ctx):
    size = rows // n_ctx
    for c in range(n_ctx):
        for h in range(HEADS):
            yield (pl.ds((c * HEADS + h) * size, size), (pl.ds(c * size, size), pl.ds(h * HDIM, HDIM)))


def fetch(pairs, sems):
    copies = [pltpu.make_async_copy(source, target, sems.at[i]) for i, (source, target) in enumerate(pairs)]
    for copy in copies:
        copy.start()
    return copies


def join(keys, values, kv, sems):
    for copy in fetch([(keys, kv.at[:, pl.ds(0, HDIM)]), (values, kv.at[:, pl.ds(HDIM, HDIM)])], sems):
        copy.wait()


def with_ones(kv):
    return jnp.concatenate([kv, jnp.ones((kv.shape[0], HDIM), BF16)], axis=1)


def levels(place, back, many, q_s, key_block, start):
    size, rows = place.rows // place.n_ctx, place.rows
    tokens = many // HEADS
    key = place.base - back * rows + lax.broadcasted_iota(jnp.int32, (tokens, rows), 1)
    query = place.base + lax.broadcasted_iota(jnp.int32, (tokens, rows), 0)
    off = jnp.where((key >= start[:tokens, :]) & (key <= query), 0.0, NEG_FILL)
    s = dot(q_s[:many, :], key_block, NT) * EXP2_SCALE
    s = s.reshape(tokens // size, HEADS, size, rows) + off.reshape(tokens // size, 1, size, rows)
    return s.reshape(many, rows)


def fold(s):
    return jnp.maximum(s[:, :HDIM], s[:, HDIM:])


def row_max(s):
    return jnp.broadcast_to(jnp.max(s, axis=1, keepdims=True), (s.shape[0], HDIM))


def prepare(n_ctx, lengths_hbm, q_hbm, do_hbm, kv_ref, facts_ref, kv_own, q_s, q_t, do_r, start, level, p_own, acc,
            lengths_ref, q_ref, do_ref, sems):
    copies = fetch([(lengths_hbm, lengths_ref), (q_hbm, q_ref), (do_hbm, do_ref)], sems)
    rows = q_ref.shape[0]
    index = lax.axis_index("dp") * n_ctx + lax.axis_index("ctx")
    kv_own[...] = with_ones(kv_ref[...])
    copies[0].wait()
    facts, ends = facts_of(n_ctx, rows, index, lengths_ref)
    place = Place(n_ctx, rows, facts)
    line = lax.broadcasted_iota(jnp.int32, facts_ref.shape, 0)
    held = jnp.zeros(facts_ref.shape, jnp.int32)
    for i, fact in enumerate(facts):
        held = jnp.where(line == i, fact, held)
    facts_ref[...] = held
    token = place.base + lax.broadcasted_iota(jnp.int32, (rows, HDIM), 0)
    begin = jnp.zeros((rows, HDIM), jnp.int32)
    for end in ends:
        begin = jnp.where(token >= end, end, begin)
    start[...] = wide(begin) if rows == 2 * HDIM else jnp.broadcast_to(begin[:, :1], (rows, rows))
    copies[1].wait()
    for here, there in chunks(rows, n_ctx):
        q_s[here, :] = q_ref[there]
    s = levels(place, 0, HEADS * rows, q_s, kv_own[:, :HDIM], start)
    top = row_max(fold(s))
    level[...] = top
    p = jnp.exp2(s - wide(top)).astype(BF16)
    p_own[...] = p
    acc[...] = dot(p, kv_own[:, HDIM:])
    copies[2].wait()
    for here, there in chunks(rows, n_ctx):
        do_r[here, :] = do_ref[there]
    for h in range(HEADS):
        here = pl.ds(h * rows, rows)
        q_t[:, here] = q_s[here, :].T


def side_by_side(parts, axis):
    return parts[0] if len(parts) == 1 else jnp.concatenate(parts, axis=axis)


def attend(place, backs, many, q_s, kvs, start, level, acc, probs):
    scores = [levels(place, back, many, q_s, kv[:, :HDIM], start) for back, kv in zip(backs, kvs)]
    p = [jnp.exp2(s - wide(level[:many, :])).astype(BF16) for s in scores]
    for ref, part in zip(probs, p):
        ref[:many, :] = part
    acc[:many, :] += dot(side_by_side(p, 1), side_by_side([kv[:, HDIM:] for kv in kvs], 0))


def attend_even(n_ctx, facts, q_s, start, level, acc_in, *refs):
    *got, kv_even, p_even, acc = refs
    rows = got[0].shape[0]
    place = Place(n_ctx, rows, facts)
    for i, ref in enumerate(got):
        kv_even[i] = with_ones(ref[...])
    acc[...] = acc_in[...]

    def body(backs, many):
        attend(place, backs, many, q_s, [kv_even.at[place.hop(back)] for back in backs], start, level, acc,
               [p_even.at[lax.div(back, 2) - 1] for back in backs])

    place.past(range(2, n_ctx + 1, 2), body)


def gradients(many, q_t, do_s, do_t, ps, kvs, corr):
    d = [dot(do_s[:many, :], kv[:, HDIM:2 * HDIM], NT) for kv in kvs]
    dv = [dot(do_t[:, :many], p) for p in ps]
    ds = [(p.astype(F32) * (each - wide(corr[:many, :]))).astype(BF16) for p, each in zip(ps, d)]
    dk = [dot(q_t[:, :many], each) for each in ds]
    return [(each, jnp.concatenate([k.T, v.T], axis=1)) for each, k, v in zip(ds, dk, dv)]


def forward(n_ctx, facts, q_s, q_t, do_r, start, level, acc_in, kv_own, kv_even, kv_passed, p_own_in, p_even_in,
            o_hbm, kv_odd, ds_odd, do_s, do_t, corr, g_passed, p_own, p_even, o_ref, p_odd, acc, top, p_new, kv_now, sems):
    rows = o_ref.shape[0]
    size = rows // n_ctx
    place = Place(n_ctx, rows, facts)
    pairs = n_ctx // 2
    everything = HEADS * rows
    odd_backs = range(1, n_ctx, 2)
    del p_own_in, p_even_in

    for i in range(pairs):
        kv_odd[i] = with_ones(kv_passed[i])

    def odd(backs):
        return [kv_odd.at[place.hop(back)] for back in backs]

    def attend_odd(backs, many):
        attend(place, backs, many, q_s, odd(backs), start, level, acc, [p_odd.at[lax.div(back, 2)] for back in backs])

    acc[...] = acc_in[...]
    place.past(odd_backs, attend_odd)

    @pl.when(jnp.logical_not(jnp.max(acc[:, HDIM:]) < 2.0 ** 40))
    def _():
        def each(step):
            @pl.loop(0, place.before + 1)
            def _(back):
                at = place.hop(back)

                @pl.when(back == 0)
                def _():
                    kv_now[...] = kv_own[...]

                @pl.when(lax.rem(back, 2) == 1)
                def _():
                    kv_now[...] = kv_odd[at]

                @pl.when((back > 0) & (lax.rem(back, 2) == 0))
                def _():
                    kv_now[...] = kv_even[at]

                @pl.loop(0, n_ctx)
                def _(c):
                    here = pl.ds(c * HEADS * size, HEADS * size)
                    tokens = pl.ds(c * size, size)
                    key = place.base - back * rows + lax.broadcasted_iota(jnp.int32, (size, rows), 1)
                    query = place.base + c * size + lax.broadcasted_iota(jnp.int32, (size, rows), 0)
                    off = jnp.where((key >= start[tokens, :]) & (key <= query), 0.0, NEG_FILL)
                    s = dot(q_s[here, :], kv_now[:, :HDIM], NT) * EXP2_SCALE
                    step(here, (s.reshape(HEADS, size, rows) + off[None]).reshape(HEADS * size, rows))

                if step is replace:
                    half = lax.div(back, 2)
                    for fits, target in ((back == 0, p_own), (lax.rem(back, 2) == 1, p_odd.at[half]),
                                         ((back > 0) & (lax.rem(back, 2) == 0), p_even.at[jnp.maximum(half - 1, 0)])):

                        @pl.when(fits)
                        def _():
                            copy = pltpu.make_async_copy(p_new, target, sems.at[0])
                            copy.start()
                            copy.wait()

        def highest(here, s):
            top[here, :] = jnp.maximum(top[here, :], row_max(fold(s)))

        def replace(here, s):
            p = jnp.exp2(s - wide(top[here, :])).astype(BF16)
            p_new[here, :] = p
            acc[here, :] += dot(p, kv_now[:, HDIM:])

        @pl.loop(0, n_ctx)
        def _(c):
            here = pl.ds(c * HEADS * size, HEADS * size)
            top[here, :] = jnp.full((HEADS * size, HDIM), NEG_FILL, F32)
            acc[here, :] = jnp.zeros((HEADS * size, 2 * HDIM), F32)

        each(highest)
        each(replace)

    for i in range(0, everything, rows):
        here = pl.ds(i, rows)
        total = acc[here, :]
        inverse = 1.0 / total[:, HDIM:]
        out = (total[:, :HDIM] * inverse).astype(BF16)
        grad = do_r[here, :].astype(F32)
        corr[here, :] = jnp.sum(grad * out.astype(F32), axis=1, keepdims=True) * inverse
        scaled = grad * inverse
        do_s[here, :] = scaled.astype(BF16)
        do_t[:, here] = scaled.T.astype(BF16)
        for part, there in chunks(rows, n_ctx):
            if i <= part.start < i + rows:
                o_ref[there] = out[part.start - i:part.start - i + size, :]

    leaving = pltpu.make_async_copy(o_ref, o_hbm, sems.at[1])
    leaving.start()

    def backward(backs, many):
        ps = [p_odd[lax.div(back, 2), :many, :] for back in backs]
        for back, (ds, terms) in zip(backs, gradients(many, q_t, do_s, do_t, ps, odd(backs), corr)):
            ds_odd[lax.div(back, 2), :many, :] = ds
            g_passed[place.hop(back)] = terms.astype(BF16)

    done = place.past(odd_backs, backward)

    @pl.loop(done, pairs)
    def _(i):
        g_passed[place.hop(2 * i + 1)] = jnp.zeros((rows, 2 * HDIM), BF16)

    leaving.wait()


def even(n_ctx, facts, q_t, do_s, do_t, kv_even, p_even, corr, ds_even, g_direct):
    rows = kv_even.shape[1]
    place = Place(n_ctx, rows, facts)

    def backward(backs, many):
        ps = [p_even[lax.div(back, 2) - 1, :many, :] for back in backs]
        kvs = [kv_even.at[place.hop(back)] for back in backs]
        for back, (ds, terms) in zip(backs, gradients(many, q_t, do_s, do_t, ps, kvs, corr)):
            ds_even[lax.div(back, 2) - 1, :many, :] = ds
            g_direct[place.hop(back) - 1] = terms

    done = place.past(range(2, n_ctx, 2), backward)

    @pl.loop(done, n_ctx // 2 - 1)
    def _(i):
        g_direct[place.hop(2 * i + 2) - 1] = jnp.zeros((rows, 2 * HDIM), F32)


def rest(n_ctx, facts, q_t, do_s, do_t, kv_even, p_even, corr, kv_own, p_own, kv_odd, ds_odd, ds_even,
         dq_ref, g_own, g_prev, dq_acc):
    rows = kv_own.shape[0]
    place = Place(n_ctx, rows, facts)

    (ds, g_own[...]), = gradients(HEADS * rows, q_t, do_s, do_t, [p_own[...]], [kv_own], corr)
    dq_acc[...] = dot(ds, kv_own[:, :HDIM])

    def add(backs, many, ds, kv):
        dq_acc[:many, :] += dot(side_by_side([ds(back)[:many, :] for back in backs], 1),
                                side_by_side([kv[place.hop(back), :, :HDIM] for back in backs], 0))

    def add_odd(backs, many):
        add(backs, many, lambda back: ds_odd.at[lax.div(back, 2)], kv_odd)

    def add_even(backs, many):
        add(backs, many, lambda back: ds_even.at[lax.div(back, 2) - 1], kv_even)

    def farthest(backs, many):
        at = place.hop(backs[0])
        (ds, g_prev[...]), = gradients(many, q_t, do_s, do_t, [p_even[n_ctx // 2 - 1, :many, :]], [kv_even.at[at]], corr)
        dq_acc[:many, :] += dot(ds, kv_even[at, :, :HDIM])

    place.past(range(1, n_ctx, 2), add_odd)
    place.past(range(2, n_ctx, 2), add_even)
    g_prev[...] = jnp.zeros(g_prev.shape, F32)
    place.past(range(n_ctx, n_ctx + 1), farthest)

    for here, there in chunks(rows, n_ctx):
        dq_ref[there] = (dq_acc[here, :] * SCALE).astype(BF16)


def finish(total, last, gk_ref, gv_ref):
    terms = total[...] + last[...].astype(F32)
    gk_ref[...] = (terms[:, :HDIM] * SCALE).astype(BF16)
    gv_ref[...] = terms[:, HDIM:].astype(BF16)


def size_of(arrays):
    return sum(math.prod(array.shape) * jnp.dtype(array.dtype).itemsize for array in arrays)


def call(body, name, outs, args, scratch, flops, resident, aliases=(), away=(), leaves=(), copies=0):
    vmem = pl.BlockSpec(memory_space=pltpu.VMEM)
    anywhere = pl.BlockSpec(memory_space=pl.ANY)
    hbm = pl.BlockSpec(memory_space=pltpu.HBM)
    outs = tuple(jax.ShapeDtypeStruct(shape, dtype) for shape, dtype in outs)
    held = size_of(scratch) + 8 * 2**20
    if not resident:
        held = min(held + size_of(outs) + size_of(args), 62 * 2**20)
    in_specs, out_specs = [vmem] * len(args), [vmem] * len(outs)
    for i in away:
        in_specs[i] = hbm
    for o in leaves:
        out_specs[o] = hbm
    for i, o in aliases:
        in_specs[i] = out_specs[o] = anywhere
    return pl.pallas_call(
        body,
        out_shape=outs,
        in_specs=in_specs,
        out_specs=tuple(out_specs),
        scratch_shapes=scratch + [pltpu.SemaphoreType.DMA((copies,))] * (copies > 0),
        input_output_aliases=dict(aliases),
        compiler_params=pltpu.CompilerParams(vmem_limit_bytes=held),
        cost_estimate=pl.CostEstimate(flops=flops, bytes_accessed=2**20, transcendentals=0),
        name=name,
    )(*(pltpu.with_memory_space_constraint(arg, pltpu.HBM) if i in away else arg for i, arg in enumerate(args)))


def shards(queries, keys, values, grad_out, lengths):
    rows = keys.shape[0]
    n_dp, n_ctx = lax.axis_size("dp"), lax.axis_size("ctx")
    axes = ("dp", "ctx")
    pairs = n_ctx // 2
    ctx = lax.axis_index("ctx")
    many = HEADS * rows
    once = 2 * many * rows * HDIM
    by_row, by_lane = (many, HDIM), (HDIM, many)
    block, kv_ones = (rows, 2 * HDIM), (rows, 3 * HDIM)
    run = functools.partial(call, resident=(n_ctx + 1) * many * rows <= 6 * 2**20)
    def kernel(body, *args, **kwargs):
        return run(functools.partial(body, n_ctx), body.__name__, *args, **kwargs)

    def swap(blocks, flip):
        return lax.ppermute(blocks, axes, flip_route(n_dp, n_ctx, flip))

    later = [ctx < ctx ^ max(2 * i, 1) for i in range(pairs)]

    kv, = run(join, "join", [(block, BF16)], (keys, values), [], 1, away=(0, 1), copies=2)
    near = lambda i: i & (i - 1) == 0
    prev = lax.ppermute(kv, axes, run_route(n_dp, n_ctx))
    straight = {i: lax.ppermute(kv, axes, straight_route(n_dp, n_ctx, 2 * i)) for i in range(1, pairs) if not near(i)}
    facts, kv_own, q_s, q_t, do_r, start, level, p_own, acc = kernel(
        prepare, [((8, HDIM), jnp.int32), (kv_ones, BF16), (by_row, BF16), (by_lane, BF16), (by_row, BF16),
                  ((rows, rows), jnp.int32), (by_row, F32), ((many, rows), BF16), ((many, 2 * HDIM), F32)],
        (lengths, queries, grad_out, kv),
        [pltpu.SMEM(lengths.shape, jnp.int32), pltpu.VMEM(queries.shape, BF16), pltpu.VMEM(queries.shape, BF16)], 2 * once,
        away=(0, 1, 2), copies=3)
    ours = kv_own[:, :2 * HDIM]
    sent = [jnp.where(after, ours, prev) for after in later]
    got = [prev] + [swap(sent[i], 2 * i) if near(i) else straight[i] for i in range(1, pairs)]
    passed = swap(jnp.stack(sent[:1] + got[1:]), 1)
    kv_even, p_even, acc = kernel(
        attend_even, [((pairs,) + kv_ones, BF16), ((pairs, many, rows), BF16), ((many, 2 * HDIM), F32)],
        (facts, q_s, start, level, acc, *got), [], 2 * pairs * once)
    attn_out, kv_odd, ds_odd, do_s, do_t, corr, g_passed, p_own, p_even = kernel(
        forward,
        [(queries.shape, BF16), ((pairs,) + kv_ones, BF16), ((pairs, many, rows), BF16),
         (by_row, BF16), (by_lane, BF16), (by_row, F32), ((pairs,) + block, BF16), (p_own.shape, BF16), (p_even.shape, BF16)],
        (facts, q_s, q_t, do_r, start, level, acc, kv_own, kv_even, passed, p_own, p_even),
        [pltpu.VMEM(queries.shape, BF16), pltpu.VMEM((pairs, many, rows), BF16), pltpu.VMEM((many, 2 * HDIM), F32),
         pltpu.VMEM(by_row, F32), pltpu.VMEM((many, rows), BF16), pltpu.VMEM(kv_ones, BF16)],
        5 * pairs * once, aliases=((10, 7), (11, 8)), leaves=(0,), copies=2)
    partner = swap(g_passed, 1).astype(F32)
    shared = (facts, q_t, do_s, do_t, kv_even, p_even, corr)
    ds_even, g_direct = kernel(even, [((pairs - 1, many, rows), BF16), ((pairs - 1,) + block, F32)],
                               shared, [], 3 * (pairs - 1) * once)
    terms = [partner[0]] + [swap((g_direct[i - 1] + partner[i]).astype(BF16), 2 * i).astype(F32) for i in range(1, pairs)]
    grad_queries, g_own, g_prev = kernel(rest, [(queries.shape, BF16), (block, F32), (block, F32)],
                                         shared + (kv_own, p_own, kv_odd, ds_odd, ds_even),
                                         [pltpu.VMEM(by_row, F32)], (n_ctx + 7) * once)
    own_total, prev_total = g_own, g_prev
    for after, term in zip(later, terms):
        own_total = own_total + jnp.where(after, term, 0.0)
        prev_total = prev_total + jnp.where(after, 0.0, term)
    back = [(b, a) for a, b in run_route(n_dp, n_ctx)]
    last = lax.ppermute(prev_total.astype(BF16), axes, back)
    grad_keys, grad_values = run(finish, "finish", [(keys.shape, BF16), (values.shape, BF16)], (own_total, last), [], 1)
    return (attn_out, grad_queries, grad_keys, grad_values)


def solution(mesh):
    tokens = P(("dp", "ctx"), None)
    return jax.shard_map(
        shards,
        mesh=mesh,
        in_specs=(tokens, tokens, tokens, tokens, P()),
        out_specs=(tokens, tokens, tokens, tokens),
        check_vma=False,
    )
```

```python
import functools
import math

import jax
import jax.numpy as jnp
from jax import lax
from jax.experimental import pallas as pl
from jax.experimental.pallas import tpu as pltpu
from jax.sharding import PartitionSpec as P

HEADS = 8
HDIM = 128
NEG_FILL = -1e30
SCALE = float(HDIM) ** -0.5
EXP2_SCALE = SCALE * math.log2(math.e)

NT = (((1,), (1,)), ((), ()))
NN = (((1,), (0,)), ((), ()))
F32, BF16 = jnp.float32, jnp.bfloat16


def dot(a, b, dims=NN):
    return lax.dot_general(a, b, dims, preferred_element_type=F32)


def wide(column):
    return jnp.concatenate([column, column], axis=1)


def run_route(n_dp, n_ctx):
    return [(d * n_ctx + c, (d + 1) * n_ctx + c) for d in range(n_dp - 1) for c in range(n_ctx)]


def flip_route(n_dp, n_ctx, flip):
    return [(d * n_ctx + c, d * n_ctx + (c ^ flip)) for d in range(n_dp) for c in range(n_ctx)]


def facts_of(n_ctx, rows, index, lengths_ref):
    base = index * rows
    ends, end = [], jnp.int32(0)
    for i in range(lengths_ref.shape[0]):
        end = end + lengths_ref[i]
        ends.append(end)
    low, high = jnp.int32(0), ends[-1]
    for end in ends:
        low = jnp.where(end <= base, end, low)
    for end in reversed(ends):
        high = jnp.where(end > base, end, high)
    before = lax.div(base - low + rows - 1, rows)
    short = (high - base <= rows - rows // n_ctx).astype(jnp.int32)
    return (lax.rem(index, n_ctx), base, before, short), ends


def straight_route(n_dp, n_ctx, flip):
    pairs = [(d, c, d + int(c > c ^ flip)) for d in range(n_dp) for c in range(n_ctx)]
    return [(d * n_ctx + c, run * n_ctx + (c ^ flip)) for d, c, run in pairs if run < n_dp]


class Place:
    def __init__(self, n_ctx, rows, facts):
        self.n_ctx, self.rows = n_ctx, rows
        self.ctx, self.base, self.before, short = facts if isinstance(facts, tuple) else (facts[i, 0] for i in range(4))
        self.short = short == 1

    def hop(self, back):
        return lax.div(self.ctx ^ lax.rem(self.ctx - back + 2 * self.n_ctx, self.n_ctx), 2)

    def past(self, backs, body):
        first, step = backs[0], backs.step
        count = jnp.clip(lax.div(self.before - first + step, step), 0, len(backs))
        for short in (True, False):
            many = HEADS * (self.rows - self.rows // self.n_ctx if short else self.rows)
            fits = self.short if short else jnp.logical_not(self.short)

            if len(backs) > 1:

                @pl.when(fits)
                def _():
                    @pl.loop(0, lax.div(count, 2))
                    def _(i):
                        body((first + 2 * i * step, first + (2 * i + 1) * step), many)

            @pl.when(fits & (lax.rem(count, 2) == 1))
            def _():
                body((first + (count - 1) * step,), many)

        return count


def chunks(rows, n_ctx):
    size = rows // n_ctx
    for c in range(n_ctx):
        for h in range(HEADS):
            yield (pl.ds((c * HEADS + h) * size, size), (pl.ds(c * size, size), pl.ds(h * HDIM, HDIM)))


def fetch(pairs, sems):
    copies = [pltpu.make_async_copy(source, target, sems.at[i]) for i, (source, target) in enumerate(pairs)]
    for copy in copies:
        copy.start()
    return copies


def join(keys, values, *refs):
    *joined, sems = refs
    for copy in fetch([(source, kv.at[:, pl.ds(lane, HDIM)]) for kv in joined for source, lane in ((keys, 0), (values, HDIM))], sems):
        copy.wait()


def ones_beside(values):
    return jnp.concatenate([values, jnp.ones(values.shape, BF16)], axis=1)


def levels(place, back, many, q_s, key_block, start):
    size, rows = place.rows // place.n_ctx, place.rows
    tokens = many // HEADS
    key = place.base - back * rows + lax.broadcasted_iota(jnp.int32, (tokens, rows), 1)
    query = place.base + lax.broadcasted_iota(jnp.int32, (tokens, rows), 0)
    off = jnp.where((key >= start[:tokens, :]) & (key <= query), 0.0, NEG_FILL)
    s = dot(q_s[:many, :], key_block, NT) * EXP2_SCALE
    s = s.reshape(tokens // size, HEADS, size, rows) + off.reshape(tokens // size, 1, size, rows)
    return s.reshape(many, rows)


def fold(s):
    return jnp.maximum(s[:, :HDIM], s[:, HDIM:])


def row_max(s):
    return jnp.broadcast_to(jnp.max(s, axis=1, keepdims=True), (s.shape[0], HDIM))


def prepare(n_ctx, lengths_hbm, q_hbm, do_hbm, kv_ref, facts_ref, kv_own, q_s, q_t, do_r, start, level, p_own, acc,
            lengths_ref, q_ref, do_ref, sems):
    copies = fetch([(lengths_hbm, lengths_ref), (q_hbm, q_ref), (do_hbm, do_ref)], sems)
    rows = q_ref.shape[0]
    index = lax.axis_index("dp") * n_ctx + lax.axis_index("ctx")
    kv_own[...] = kv_ref[...]
    copies[0].wait()
    facts, ends = facts_of(n_ctx, rows, index, lengths_ref)
    place = Place(n_ctx, rows, facts)
    line = lax.broadcasted_iota(jnp.int32, facts_ref.shape, 0)
    held = jnp.zeros(facts_ref.shape, jnp.int32)
    for i, fact in enumerate(facts):
        held = jnp.where(line == i, fact, held)
    facts_ref[...] = held
    token = place.base + lax.broadcasted_iota(jnp.int32, (rows, HDIM), 0)
    begin = jnp.zeros((rows, HDIM), jnp.int32)
    for end in ends:
        begin = jnp.where(token >= end, end, begin)
    start[...] = wide(begin) if rows == 2 * HDIM else jnp.broadcast_to(begin[:, :1], (rows, rows))
    copies[1].wait()
    for here, there in chunks(rows, n_ctx):
        q_s[here, :] = q_ref[there]
    s = levels(place, 0, HEADS * rows, q_s, kv_own[:, :HDIM], start)
    top = row_max(fold(s))
    level[...] = top
    p = jnp.exp2(s - wide(top)).astype(BF16)
    p_own[...] = p
    acc[...] = dot(p, ones_beside(kv_own[:, HDIM:]))
    copies[2].wait()
    for here, there in chunks(rows, n_ctx):
        do_r[here, :] = do_ref[there]
    for h in range(HEADS):
        here = pl.ds(h * rows, rows)
        q_t[:, here] = q_s[here, :].T


def side_by_side(parts, axis):
    return parts[0] if len(parts) == 1 else jnp.concatenate(parts, axis=axis)


def attend(place, backs, many, q_s, kvs, start, level, acc, probs):
    scores = [levels(place, back, many, q_s, kv[:, :HDIM], start) for back, kv in zip(backs, kvs)]
    p = [jnp.exp2(s - wide(level[:many, :])).astype(BF16) for s in scores]
    for ref, part in zip(probs, p):
        ref[:many, :] = part
    acc[:many, :] += dot(side_by_side(p, 1), side_by_side([ones_beside(kv[:, HDIM:]) for kv in kvs], 0))


def attend_even(n_ctx, facts, q_s, start, level, acc_in, *refs):
    *got, kv_even, p_even, acc = refs
    rows = got[0].shape[0]
    place = Place(n_ctx, rows, facts)
    for i, ref in enumerate(got):
        kv_even[i] = ref[...]
    acc[...] = acc_in[...]

    def body(backs, many):
        attend(place, backs, many, q_s, [kv_even.at[place.hop(back)] for back in backs], start, level, acc,
               [p_even.at[lax.div(back, 2) - 1] for back in backs])

    place.past(range(2, n_ctx + 1, 2), body)


def gradients(many, q_t, do_s, do_t, ps, kvs, corr):
    d = [dot(do_s[:many, :], kv[:, HDIM:], NT) for kv in kvs]
    dv = [dot(do_t[:, :many], p) for p in ps]
    ds = [(p.astype(F32) * (each - wide(corr[:many, :]))).astype(BF16) for p, each in zip(ps, d)]
    dk = [dot(q_t[:, :many], each) for each in ds]
    return [(each, jnp.concatenate([k.T, v.T], axis=1)) for each, k, v in zip(ds, dk, dv)]


def forward(n_ctx, facts, q_s, q_t, do_r, start, level, acc_in, kv_own, kv_even, kv_odd, p_own_in, p_even_in,
            o_hbm, k_odd, ds_odd, do_s, do_t, corr, g_passed, p_own, p_even, o_ref, p_odd, acc, top, p_new, kv_now, sems):
    rows = o_ref.shape[0]
    size = rows // n_ctx
    place = Place(n_ctx, rows, facts)
    pairs = n_ctx // 2
    everything = HEADS * rows
    odd_backs = range(1, n_ctx, 2)
    del p_own_in, p_even_in

    for i in range(pairs):
        k_odd[i] = kv_odd[i, :, :HDIM]

    def odd(backs):
        return [kv_odd.at[place.hop(back)] for back in backs]

    def attend_odd(backs, many):
        attend(place, backs, many, q_s, odd(backs), start, level, acc, [p_odd.at[lax.div(back, 2)] for back in backs])

    acc[...] = acc_in[...]
    place.past(odd_backs, attend_odd)

    @pl.when(jnp.logical_not(jnp.max(acc[:, HDIM:]) < 2.0 ** 40))
    def _():
        def each(step):
            @pl.loop(0, place.before + 1)
            def _(back):
                at = place.hop(back)

                @pl.when(back == 0)
                def _():
                    kv_now[...] = kv_own[...]

                @pl.when(lax.rem(back, 2) == 1)
                def _():
                    kv_now[...] = kv_odd[at]

                @pl.when((back > 0) & (lax.rem(back, 2) == 0))
                def _():
                    kv_now[...] = kv_even[at]

                @pl.loop(0, n_ctx)
                def _(c):
                    here = pl.ds(c * HEADS * size, HEADS * size)
                    tokens = pl.ds(c * size, size)
                    key = place.base - back * rows + lax.broadcasted_iota(jnp.int32, (size, rows), 1)
                    query = place.base + c * size + lax.broadcasted_iota(jnp.int32, (size, rows), 0)
                    off = jnp.where((key >= start[tokens, :]) & (key <= query), 0.0, NEG_FILL)
                    s = dot(q_s[here, :], kv_now[:, :HDIM], NT) * EXP2_SCALE
                    step(here, (s.reshape(HEADS, size, rows) + off[None]).reshape(HEADS * size, rows))

                if step is replace:
                    half = lax.div(back, 2)
                    for fits, target in ((back == 0, p_own), (lax.rem(back, 2) == 1, p_odd.at[half]),
                                         ((back > 0) & (lax.rem(back, 2) == 0), p_even.at[jnp.maximum(half - 1, 0)])):

                        @pl.when(fits)
                        def _():
                            copy = pltpu.make_async_copy(p_new, target, sems.at[0])
                            copy.start()
                            copy.wait()

        def highest(here, s):
            top[here, :] = jnp.maximum(top[here, :], row_max(fold(s)))

        def replace(here, s):
            p = jnp.exp2(s - wide(top[here, :])).astype(BF16)
            p_new[here, :] = p
            acc[here, :] += dot(p, ones_beside(kv_now[:, HDIM:]))

        @pl.loop(0, n_ctx)
        def _(c):
            here = pl.ds(c * HEADS * size, HEADS * size)
            top[here, :] = jnp.full((HEADS * size, HDIM), NEG_FILL, F32)
            acc[here, :] = jnp.zeros((HEADS * size, 2 * HDIM), F32)

        each(highest)
        each(replace)

    for i in range(0, everything, rows):
        here = pl.ds(i, rows)
        total = acc[here, :]
        inverse = 1.0 / total[:, HDIM:]
        out = (total[:, :HDIM] * inverse).astype(BF16)
        grad = do_r[here, :].astype(F32)
        corr[here, :] = jnp.sum(grad * out.astype(F32), axis=1, keepdims=True) * inverse
        scaled = grad * inverse
        do_s[here, :] = scaled.astype(BF16)
        do_t[:, here] = scaled.T.astype(BF16)
        for part, there in chunks(rows, n_ctx):
            if i <= part.start < i + rows:
                o_ref[there] = out[part.start - i:part.start - i + size, :]

    leaving = pltpu.make_async_copy(o_ref, o_hbm, sems.at[1])
    leaving.start()

    def backward(backs, many):
        ps = [p_odd[lax.div(back, 2), :many, :] for back in backs]
        for back, (ds, terms) in zip(backs, gradients(many, q_t, do_s, do_t, ps, odd(backs), corr)):
            ds_odd[lax.div(back, 2), :many, :] = ds
            g_passed[place.hop(back)] = terms.astype(BF16)

    done = place.past(odd_backs, backward)

    @pl.loop(done, pairs)
    def _(i):
        g_passed[place.hop(2 * i + 1)] = jnp.zeros((rows, 2 * HDIM), BF16)

    leaving.wait()


def even(n_ctx, facts, q_t, do_s, do_t, kv_even, p_even, corr, ds_even, g_direct):
    rows = kv_even.shape[1]
    place = Place(n_ctx, rows, facts)

    def backward(backs, many):
        ps = [p_even[lax.div(back, 2) - 1, :many, :] for back in backs]
        kvs = [kv_even.at[place.hop(back)] for back in backs]
        for back, (ds, terms) in zip(backs, gradients(many, q_t, do_s, do_t, ps, kvs, corr)):
            ds_even[lax.div(back, 2) - 1, :many, :] = ds
            g_direct[place.hop(back) - 1] = terms

    done = place.past(range(2, n_ctx, 2), backward)

    @pl.loop(done, n_ctx // 2 - 1)
    def _(i):
        g_direct[place.hop(2 * i + 2) - 1] = jnp.zeros((rows, 2 * HDIM), F32)


def rest(n_ctx, facts, q_t, do_s, do_t, kv_even, p_even, corr, kv_own, p_own, k_odd, ds_odd, ds_even,
         dq_ref, g_own, g_prev, dq_acc):
    rows = kv_own.shape[0]
    place = Place(n_ctx, rows, facts)

    (ds, g_own[...]), = gradients(HEADS * rows, q_t, do_s, do_t, [p_own[...]], [kv_own], corr)
    dq_acc[...] = dot(ds, kv_own[:, :HDIM])

    def add(backs, many, ds, kv):
        dq_acc[:many, :] += dot(side_by_side([ds(back)[:many, :] for back in backs], 1),
                                side_by_side([kv[place.hop(back), :, :HDIM] for back in backs], 0))

    def add_odd(backs, many):
        add(backs, many, lambda back: ds_odd.at[lax.div(back, 2)], k_odd)

    def add_even(backs, many):
        add(backs, many, lambda back: ds_even.at[lax.div(back, 2) - 1], kv_even)

    def farthest(backs, many):
        at = place.hop(backs[0])
        (ds, g_prev[...]), = gradients(many, q_t, do_s, do_t, [p_even[n_ctx // 2 - 1, :many, :]], [kv_even.at[at]], corr)
        dq_acc[:many, :] += dot(ds, kv_even[at, :, :HDIM])

    place.past(range(1, n_ctx, 2), add_odd)
    place.past(range(2, n_ctx, 2), add_even)
    g_prev[...] = jnp.zeros(g_prev.shape, F32)
    place.past(range(n_ctx, n_ctx + 1), farthest)

    for here, there in chunks(rows, n_ctx):
        dq_ref[there] = (dq_acc[here, :] * SCALE).astype(BF16)


def finish(total, last, gk_ref, gv_ref):
    terms = total[...] + last[...].astype(F32)
    gk_ref[...] = (terms[:, :HDIM] * SCALE).astype(BF16)
    gv_ref[...] = terms[:, HDIM:].astype(BF16)


def size_of(arrays):
    return sum(math.prod(array.shape) * jnp.dtype(array.dtype).itemsize for array in arrays)


def call(body, name, outs, args, scratch, flops, resident, aliases=(), away=(), leaves=(), copies=0):
    vmem = pl.BlockSpec(memory_space=pltpu.VMEM)
    anywhere = pl.BlockSpec(memory_space=pl.ANY)
    hbm = pl.BlockSpec(memory_space=pltpu.HBM)
    outs = tuple(jax.ShapeDtypeStruct(shape, dtype) for shape, dtype in outs)
    held = size_of(scratch) + 8 * 2**20
    if not resident:
        held = min(held + size_of(outs) + size_of(args), 62 * 2**20)
    in_specs, out_specs = [vmem] * len(args), [vmem] * len(outs)
    for i in away:
        in_specs[i] = hbm
    for o in leaves:
        out_specs[o] = hbm
    for i, o in aliases:
        in_specs[i] = out_specs[o] = anywhere
    return pl.pallas_call(
        body,
        out_shape=outs,
        in_specs=in_specs,
        out_specs=tuple(out_specs),
        scratch_shapes=scratch + [pltpu.SemaphoreType.DMA((copies,))] * (copies > 0),
        input_output_aliases=dict(aliases),
        compiler_params=pltpu.CompilerParams(vmem_limit_bytes=held),
        cost_estimate=pl.CostEstimate(flops=flops, bytes_accessed=2**20, transcendentals=0),
        name=name,
    )(*(pltpu.with_memory_space_constraint(arg, pltpu.HBM) if i in away else arg for i, arg in enumerate(args)))


def shards(queries, keys, values, grad_out, lengths):
    rows = keys.shape[0]
    n_dp, n_ctx = lax.axis_size("dp"), lax.axis_size("ctx")
    axes = ("dp", "ctx")
    pairs = n_ctx // 2
    ctx = lax.axis_index("ctx")
    many = HEADS * rows
    once = 2 * many * rows * HDIM
    by_row, by_lane = (many, HDIM), (HDIM, many)
    block = (rows, 2 * HDIM)
    run = functools.partial(call, resident=(n_ctx + 1) * many * rows <= 6 * 2**20)
    def kernel(body, *args, **kwargs):
        return run(functools.partial(body, n_ctx), body.__name__, *args, **kwargs)

    def swap(blocks, flip):
        return lax.ppermute(blocks, axes, flip_route(n_dp, n_ctx, flip))

    later = [ctx < ctx ^ max(2 * i, 1) for i in range(pairs)]

    kv, kv_again = run(join, "join", [(block, BF16)] * 2, (keys, values), [], 1, away=(0, 1), copies=4)
    near = lambda i: i & (i - 1) == 0
    prev = lax.ppermute(kv, axes, run_route(n_dp, n_ctx))
    straight = {i: lax.ppermute(kv_again, axes, straight_route(n_dp, n_ctx, 2 * i)) for i in range(1, pairs) if not near(i)}
    facts, kv_own, q_s, q_t, do_r, start, level, p_own, acc = kernel(
        prepare, [((8, HDIM), jnp.int32), (block, BF16), (by_row, BF16), (by_lane, BF16), (by_row, BF16),
                  ((rows, rows), jnp.int32), (by_row, F32), ((many, rows), BF16), ((many, 2 * HDIM), F32)],
        (lengths, queries, grad_out, kv),
        [pltpu.SMEM(lengths.shape, jnp.int32), pltpu.VMEM(queries.shape, BF16), pltpu.VMEM(queries.shape, BF16)], 2 * once,
        away=(0, 1, 2), copies=3)
    sent = [jnp.where(after, kv_own, prev) for after in later]
    got = [prev] + [swap(sent[i], 2 * i) if near(i) else straight[i] for i in range(1, pairs)]
    passed = swap(jnp.stack(sent[:1] + got[1:]), 1)
    kv_even, p_even, acc = kernel(
        attend_even, [((pairs,) + block, BF16), ((pairs, many, rows), BF16), ((many, 2 * HDIM), F32)],
        (facts, q_s, start, level, acc, *got), [], 2 * pairs * once)
    attn_out, k_odd, ds_odd, do_s, do_t, corr, g_passed, p_own, p_even = kernel(
        forward,
        [(queries.shape, BF16), ((pairs, rows, HDIM), BF16), ((pairs, many, rows), BF16),
         (by_row, BF16), (by_lane, BF16), (by_row, F32), ((pairs,) + block, BF16), (p_own.shape, BF16), (p_even.shape, BF16)],
        (facts, q_s, q_t, do_r, start, level, acc, kv_own, kv_even, passed, p_own, p_even),
        [pltpu.VMEM(queries.shape, BF16), pltpu.VMEM((pairs, many, rows), BF16), pltpu.VMEM((many, 2 * HDIM), F32),
         pltpu.VMEM(by_row, F32), pltpu.VMEM((many, rows), BF16), pltpu.VMEM(block, BF16)],
        5 * pairs * once, aliases=((10, 7), (11, 8)), leaves=(0,), copies=2)
    partner = swap(g_passed, 1).astype(F32)
    shared = (facts, q_t, do_s, do_t, kv_even, p_even, corr)
    ds_even, g_direct = kernel(even, [((pairs - 1, many, rows), BF16), ((pairs - 1,) + block, F32)],
                               shared, [], 3 * (pairs - 1) * once)
    terms = [partner[0]] + [swap((g_direct[i - 1] + partner[i]).astype(BF16), 2 * i).astype(F32) for i in range(1, pairs)]
    grad_queries, g_own, g_prev = kernel(rest, [(queries.shape, BF16), (block, F32), (block, F32)],
                                         shared + (kv_own, p_own, k_odd, ds_odd, ds_even),
                                         [pltpu.VMEM(by_row, F32)], (n_ctx + 7) * once)
    own_total, prev_total = g_own, g_prev
    for after, term in zip(later, terms):
        own_total = own_total + jnp.where(after, term, 0.0)
        prev_total = prev_total + jnp.where(after, 0.0, term)
    back = [(b, a) for a, b in run_route(n_dp, n_ctx)]
    last = lax.ppermute(prev_total.astype(BF16), axes, back)
    grad_keys, grad_values = run(finish, "finish", [(keys.shape, BF16), (values.shape, BF16)], (own_total, last), [], 1)
    return (attn_out, grad_queries, grad_keys, grad_values)


def solution(mesh):
    tokens = P(("dp", "ctx"), None)
    return jax.shard_map(
        shards,
        mesh=mesh,
        in_specs=(tokens, tokens, tokens, tokens, P()),
        out_specs=(tokens, tokens, tokens, tokens),
        check_vma=False,
    )
```

```python
import functools
import math

import jax
import jax.numpy as jnp
from jax import lax
from jax.experimental import pallas as pl
from jax.experimental.pallas import tpu as pltpu
from jax.sharding import PartitionSpec as P

HEADS = 8
HDIM = 128
NEG_FILL = -1e30
SCALE = float(HDIM) ** -0.5
EXP2_SCALE = SCALE * math.log2(math.e)

NT = (((1,), (1,)), ((), ()))
NN = (((1,), (0,)), ((), ()))
F32, BF16 = jnp.float32, jnp.bfloat16


def dot(a, b, dims=NN):
    return lax.dot_general(a, b, dims, preferred_element_type=F32)


def wide(column):
    return jnp.concatenate([column, column], axis=1)


def run_route(n_dp, n_ctx):
    return [(d * n_ctx + c, (d + 1) * n_ctx + c) for d in range(n_dp - 1) for c in range(n_ctx)]


def flip_route(n_dp, n_ctx, flip):
    return [(d * n_ctx + c, d * n_ctx + (c ^ flip)) for d in range(n_dp) for c in range(n_ctx)]


def facts_of(n_ctx, rows, index, lengths_ref):
    base = index * rows
    ends, end = [], jnp.int32(0)
    for i in range(lengths_ref.shape[0]):
        end = end + lengths_ref[i]
        ends.append(end)
    low, high = jnp.int32(0), ends[-1]
    for end in ends:
        low = jnp.where(end <= base, end, low)
    for end in reversed(ends):
        high = jnp.where(end > base, end, high)
    before = lax.div(base - low + rows - 1, rows)
    short = (high - base <= rows - rows // n_ctx).astype(jnp.int32)
    return (lax.rem(index, n_ctx), base, before, short), ends


def straight_route(n_dp, n_ctx, flip):
    pairs = [(d, c, d + int(c > c ^ flip)) for d in range(n_dp) for c in range(n_ctx)]
    return [(d * n_ctx + c, run * n_ctx + (c ^ flip)) for d, c, run in pairs if run < n_dp]


class Place:
    def __init__(self, n_ctx, rows, facts):
        self.n_ctx, self.rows = n_ctx, rows
        self.ctx, self.base, self.before, short = facts if isinstance(facts, tuple) else (facts[i, 0] for i in range(4))
        self.short = short == 1

    def hop(self, back):
        return lax.div(self.ctx ^ lax.rem(self.ctx - back + 2 * self.n_ctx, self.n_ctx), 2)

    def past(self, backs, body):
        first, step = backs[0], backs.step
        count = jnp.clip(lax.div(self.before - first + step, step), 0, len(backs))
        for short in (True, False):
            many = HEADS * (self.rows - self.rows // self.n_ctx if short else self.rows)
            fits = self.short if short else jnp.logical_not(self.short)

            if len(backs) > 1:

                @pl.when(fits)
                def _():
                    @pl.loop(0, lax.div(count, 2))
                    def _(i):
                        body((first + 2 * i * step, first + (2 * i + 1) * step), many)

            @pl.when(fits & (lax.rem(count, 2) == 1))
            def _():
                body((first + (count - 1) * step,), many)

        return count


def chunks(rows, n_ctx):
    size = rows // n_ctx
    for c in range(n_ctx):
        for h in range(HEADS):
            yield (pl.ds((c * HEADS + h) * size, size), (pl.ds(c * size, size), pl.ds(h * HDIM, HDIM)))


def fetch(pairs, sems):
    copies = [pltpu.make_async_copy(source, target, sems.at[i]) for i, (source, target) in enumerate(pairs)]
    for copy in copies:
        copy.start()
    return copies


def join(keys, values, kv, sems):
    for copy in fetch([(keys, kv.at[:, pl.ds(0, HDIM)]), (values, kv.at[:, pl.ds(HDIM, HDIM)])], sems):
        copy.wait()


def ones_beside(values):
    return jnp.concatenate([values, jnp.ones(values.shape, BF16)], axis=1)


def levels(place, back, many, q_s, key_block, start):
    size, rows = place.rows // place.n_ctx, place.rows
    tokens = many // HEADS
    key = place.base - back * rows + lax.broadcasted_iota(jnp.int32, (tokens, rows), 1)
    query = place.base + lax.broadcasted_iota(jnp.int32, (tokens, rows), 0)
    off = jnp.where((key >= start[:tokens, :]) & (key <= query), 0.0, NEG_FILL)
    s = dot(q_s[:many, :], key_block, NT) * EXP2_SCALE
    s = s.reshape(tokens // size, HEADS, size, rows) + off.reshape(tokens // size, 1, size, rows)
    return s.reshape(many, rows)


def fold(s):
    return jnp.maximum(s[:, :HDIM], s[:, HDIM:])


def row_max(s):
    return jnp.broadcast_to(jnp.max(s, axis=1, keepdims=True), (s.shape[0], HDIM))


def prepare(n_ctx, lengths_hbm, q_hbm, do_hbm, kv_ref, facts_ref, kv_own, q_s, q_t, do_r, start, level, p_own, acc,
            lengths_ref, q_ref, do_ref, sems):
    copies = fetch([(lengths_hbm, lengths_ref), (q_hbm, q_ref), (do_hbm, do_ref)], sems)
    rows = q_ref.shape[0]
    index = lax.axis_index("dp") * n_ctx + lax.axis_index("ctx")
    kv_own[...] = kv_ref[...]
    copies[0].wait()
    facts, ends = facts_of(n_ctx, rows, index, lengths_ref)
    place = Place(n_ctx, rows, facts)
    line = lax.broadcasted_iota(jnp.int32, facts_ref.shape, 0)
    held = jnp.zeros(facts_ref.shape, jnp.int32)
    for i, fact in enumerate(facts):
        held = jnp.where(line == i, fact, held)
    facts_ref[...] = held
    token = place.base + lax.broadcasted_iota(jnp.int32, (rows, HDIM), 0)
    begin = jnp.zeros((rows, HDIM), jnp.int32)
    for end in ends:
        begin = jnp.where(token >= end, end, begin)
    start[...] = wide(begin) if rows == 2 * HDIM else jnp.broadcast_to(begin[:, :1], (rows, rows))
    copies[1].wait()
    for here, there in chunks(rows, n_ctx):
        q_s[here, :] = q_ref[there]
    s = levels(place, 0, HEADS * rows, q_s, kv_own[:, :HDIM], start)
    top = row_max(fold(s))
    level[...] = top
    p = jnp.exp2(s - wide(top)).astype(BF16)
    p_own[...] = p
    acc[...] = dot(p, ones_beside(kv_own[:, HDIM:]))
    copies[2].wait()
    for here, there in chunks(rows, n_ctx):
        do_r[here, :] = do_ref[there]
    for h in range(HEADS):
        here = pl.ds(h * rows, rows)
        q_t[:, here] = q_s[here, :].T


def side_by_side(parts, axis):
    return parts[0] if len(parts) == 1 else jnp.concatenate(parts, axis=axis)


def attend(place, backs, many, q_s, kvs, start, level, acc, probs):
    scores = [levels(place, back, many, q_s, kv[:, :HDIM], start) for back, kv in zip(backs, kvs)]
    p = [jnp.exp2(s - wide(level[:many, :])).astype(BF16) for s in scores]
    for ref, part in zip(probs, p):
        ref[:many, :] = part
    acc[:many, :] += dot(side_by_side(p, 1), side_by_side([ones_beside(kv[:, HDIM:]) for kv in kvs], 0))


def attend_even(n_ctx, facts, q_s, start, level, acc_in, *refs):
    *got, kv_even, p_even, acc = refs
    rows = got[0].shape[0]
    place = Place(n_ctx, rows, facts)
    for i, ref in enumerate(got):
        kv_even[i] = ref[...]
    acc[...] = acc_in[...]

    def body(backs, many):
        attend(place, backs, many, q_s, [kv_even.at[place.hop(back)] for back in backs], start, level, acc,
               [p_even.at[lax.div(back, 2) - 1] for back in backs])

    place.past(range(2, n_ctx + 1, 2), body)


def gradients(many, q_t, do_s, do_t, ps, kvs, corr):
    d = [dot(do_s[:many, :], kv[:, HDIM:], NT) for kv in kvs]
    dv = [dot(do_t[:, :many], p) for p in ps]
    ds = [(p.astype(F32) * (each - wide(corr[:many, :]))).astype(BF16) for p, each in zip(ps, d)]
    dk = [dot(q_t[:, :many], each) for each in ds]
    return [(each, jnp.concatenate([k.T, v.T], axis=1)) for each, k, v in zip(ds, dk, dv)]


def forward(n_ctx, facts, q_s, q_t, do_r, start, level, acc_in, kv_own, kv_even, kv_odd, p_own_in, p_even_in,
            o_hbm, k_odd, ds_odd, do_s, do_t, corr, g_passed, p_own, p_even, o_ref, p_odd, acc, p_new, kv_now, sems):
    rows = o_ref.shape[0]
    size = rows // n_ctx
    place = Place(n_ctx, rows, facts)
    pairs = n_ctx // 2
    everything = HEADS * rows
    odd_backs = range(1, n_ctx, 2)
    del p_own_in, p_even_in

    for i in range(pairs):
        k_odd[i] = kv_odd[i, :, :HDIM]

    def odd(backs):
        return [kv_odd.at[place.hop(back)] for back in backs]

    def attend_odd(backs, many):
        attend(place, backs, many, q_s, odd(backs), start, level, acc, [p_odd.at[lax.div(back, 2)] for back in backs])

    acc[...] = acc_in[...]
    place.past(odd_backs, attend_odd)

    @pl.when(jnp.logical_not(jnp.max(acc[:, HDIM:]) < 2.0 ** 40))
    def _():
        def each(step):
            @pl.loop(0, place.before + 1)
            def _(back):
                at = place.hop(back)

                @pl.when(back == 0)
                def _():
                    kv_now[...] = kv_own[...]

                @pl.when(lax.rem(back, 2) == 1)
                def _():
                    kv_now[...] = kv_odd[at]

                @pl.when((back > 0) & (lax.rem(back, 2) == 0))
                def _():
                    kv_now[...] = kv_even[at]

                half = lax.div(back, 2)
                targets = ((back == 0, p_own), (lax.rem(back, 2) == 1, p_odd.at[half]),
                           ((back > 0) & (lax.rem(back, 2) == 0), p_even.at[jnp.maximum(half - 1, 0)]))

                @pl.loop(0, n_ctx)
                def _(c):
                    here = pl.ds(c * HEADS * size, HEADS * size)
                    tokens = pl.ds(c * size, size)
                    key = place.base - back * rows + lax.broadcasted_iota(jnp.int32, (size, rows), 1)
                    query = place.base + c * size + lax.broadcasted_iota(jnp.int32, (size, rows), 0)
                    off = jnp.where((key >= start[tokens, :]) & (key <= query), 0.0, NEG_FILL)
                    s = dot(q_s[here, :], kv_now[:, :HDIM], NT) * EXP2_SCALE
                    step(here, (s.reshape(HEADS, size, rows) + off[None]).reshape(HEADS * size, rows))

                    if step is replace:
                        for fits, target in targets:

                            @pl.when(fits)
                            def _():
                                copy = pltpu.make_async_copy(p_new, target.at[here], sems.at[0])
                                copy.start()
                                copy.wait()

        def highest(here, s):
            corr[here, :] = jnp.maximum(corr[here, :], row_max(fold(s)))

        def replace(here, s):
            p = jnp.exp2(s - wide(corr[here, :])).astype(BF16)
            p_new[...] = p
            acc[here, :] += dot(p, ones_beside(kv_now[:, HDIM:]))

        @pl.loop(0, n_ctx)
        def _(c):
            here = pl.ds(c * HEADS * size, HEADS * size)
            corr[here, :] = jnp.full((HEADS * size, HDIM), NEG_FILL, F32)
            acc[here, :] = jnp.zeros((HEADS * size, 2 * HDIM), F32)

        each(highest)
        each(replace)

    for i in range(0, everything, rows):
        here = pl.ds(i, rows)
        total = acc[here, :]
        inverse = 1.0 / total[:, HDIM:]
        out = (total[:, :HDIM] * inverse).astype(BF16)
        grad = do_r[here, :].astype(F32)
        corr[here, :] = jnp.sum(grad * out.astype(F32), axis=1, keepdims=True) * inverse
        scaled = grad * inverse
        do_s[here, :] = scaled.astype(BF16)
        do_t[:, here] = scaled.T.astype(BF16)
        for part, there in chunks(rows, n_ctx):
            if i <= part.start < i + rows:
                o_ref[there] = out[part.start - i:part.start - i + size, :]

    leaving = pltpu.make_async_copy(o_ref, o_hbm, sems.at[1])
    leaving.start()

    def backward(backs, many):
        ps = [p_odd[lax.div(back, 2), :many, :] for back in backs]
        for back, (ds, terms) in zip(backs, gradients(many, q_t, do_s, do_t, ps, odd(backs), corr)):
            ds_odd[lax.div(back, 2), :many, :] = ds
            g_passed[place.hop(back)] = terms.astype(BF16)

    done = place.past(odd_backs, backward)

    @pl.loop(done, pairs)
    def _(i):
        g_passed[place.hop(2 * i + 1)] = jnp.zeros((rows, 2 * HDIM), BF16)

    leaving.wait()


def even(n_ctx, facts, q_t, do_s, do_t, kv_even, p_even, corr, ds_even, g_direct):
    rows = kv_even.shape[1]
    place = Place(n_ctx, rows, facts)

    def backward(backs, many):
        ps = [p_even[lax.div(back, 2) - 1, :many, :] for back in backs]
        kvs = [kv_even.at[place.hop(back)] for back in backs]
        for back, (ds, terms) in zip(backs, gradients(many, q_t, do_s, do_t, ps, kvs, corr)):
            ds_even[lax.div(back, 2) - 1, :many, :] = ds
            g_direct[place.hop(back) - 1] = terms

    done = place.past(range(2, n_ctx, 2), backward)

    @pl.loop(done, n_ctx // 2 - 1)
    def _(i):
        g_direct[place.hop(2 * i + 2) - 1] = jnp.zeros((rows, 2 * HDIM), F32)


def rest(n_ctx, facts, q_t, do_s, do_t, kv_even, p_even, corr, kv_own, p_own, k_odd, ds_odd, ds_even,
         dq_ref, g_own, g_prev, dq_acc):
    rows = kv_own.shape[0]
    place = Place(n_ctx, rows, facts)

    (ds, g_own[...]), = gradients(HEADS * rows, q_t, do_s, do_t, [p_own[...]], [kv_own], corr)
    dq_acc[...] = dot(ds, kv_own[:, :HDIM])

    def add(backs, many, ds, kv):
        dq_acc[:many, :] += dot(side_by_side([ds(back)[:many, :] for back in backs], 1),
                                side_by_side([kv[place.hop(back), :, :HDIM] for back in backs], 0))

    def add_odd(backs, many):
        add(backs, many, lambda back: ds_odd.at[lax.div(back, 2)], k_odd)

    def add_even(backs, many):
        add(backs, many, lambda back: ds_even.at[lax.div(back, 2) - 1], kv_even)

    def farthest(backs, many):
        at = place.hop(backs[0])
        (ds, g_prev[...]), = gradients(many, q_t, do_s, do_t, [p_even[n_ctx // 2 - 1, :many, :]], [kv_even.at[at]], corr)
        dq_acc[:many, :] += dot(ds, kv_even[at, :, :HDIM])

    place.past(range(1, n_ctx, 2), add_odd)
    place.past(range(2, n_ctx, 2), add_even)
    g_prev[...] = jnp.zeros(g_prev.shape, F32)
    place.past(range(n_ctx, n_ctx + 1), farthest)

    for here, there in chunks(rows, n_ctx):
        dq_ref[there] = (dq_acc[here, :] * SCALE).astype(BF16)


def finish(total, last, gk_ref, gv_ref):
    terms = total[...] + last[...].astype(F32)
    gk_ref[...] = (terms[:, :HDIM] * SCALE).astype(BF16)
    gv_ref[...] = terms[:, HDIM:].astype(BF16)


def size_of(arrays):
    return sum(math.prod(array.shape) * jnp.dtype(array.dtype).itemsize for array in arrays)


def call(body, name, outs, args, scratch, flops, resident, aliases=(), away=(), leaves=(), copies=0):
    vmem = pl.BlockSpec(memory_space=pltpu.VMEM)
    anywhere = pl.BlockSpec(memory_space=pl.ANY)
    hbm = pl.BlockSpec(memory_space=pltpu.HBM)
    outs = tuple(jax.ShapeDtypeStruct(shape, dtype) for shape, dtype in outs)
    held = size_of(scratch) + 8 * 2**20
    if not resident:
        held = min(held + size_of(outs) + size_of(args), 62 * 2**20)
    in_specs, out_specs = [vmem] * len(args), [vmem] * len(outs)
    for i in away:
        in_specs[i] = hbm
    for o in leaves:
        out_specs[o] = hbm
    for i, o in aliases:
        in_specs[i] = out_specs[o] = anywhere
    return pl.pallas_call(
        body,
        out_shape=outs,
        in_specs=in_specs,
        out_specs=tuple(out_specs),
        scratch_shapes=scratch + [pltpu.SemaphoreType.DMA((copies,))] * (copies > 0),
        input_output_aliases=dict(aliases),
        compiler_params=pltpu.CompilerParams(vmem_limit_bytes=held),
        cost_estimate=pl.CostEstimate(flops=flops, bytes_accessed=2**20, transcendentals=0),
        name=name,
    )(*(pltpu.with_memory_space_constraint(arg, pltpu.HBM) if i in away else arg for i, arg in enumerate(args)))


def shards(queries, keys, values, grad_out, lengths):
    rows = keys.shape[0]
    n_dp, n_ctx = lax.axis_size("dp"), lax.axis_size("ctx")
    axes = ("dp", "ctx")
    pairs = n_ctx // 2
    ctx = lax.axis_index("ctx")
    many = HEADS * rows
    once = 2 * many * rows * HDIM
    by_row, by_lane = (many, HDIM), (HDIM, many)
    block = (rows, 2 * HDIM)
    run = functools.partial(call, resident=(n_ctx + 1) * many * rows <= 6 * 2**20)
    def kernel(body, *args, **kwargs):
        return run(functools.partial(body, n_ctx), body.__name__, *args, **kwargs)

    def swap(blocks, flip):
        return lax.ppermute(blocks, axes, flip_route(n_dp, n_ctx, flip))

    later = [ctx < ctx ^ max(2 * i, 1) for i in range(pairs)]

    kv, = run(join, "join", [(block, BF16)], (keys, values), [], 1, away=(0, 1), copies=2)
    near = lambda i: i & (i - 1) == 0
    prev = lax.ppermute(kv, axes, run_route(n_dp, n_ctx))
    straight = {i: lax.ppermute(kv, axes, straight_route(n_dp, n_ctx, 2 * i)) for i in range(1, pairs) if not near(i)}
    facts, kv_own, q_s, q_t, do_r, start, level, p_own, acc = kernel(
        prepare, [((8, HDIM), jnp.int32), (block, BF16), (by_row, BF16), (by_lane, BF16), (by_row, BF16),
                  ((rows, rows), jnp.int32), (by_row, F32), ((many, rows), BF16), ((many, 2 * HDIM), F32)],
        (lengths, queries, grad_out, kv),
        [pltpu.SMEM(lengths.shape, jnp.int32), pltpu.VMEM(queries.shape, BF16), pltpu.VMEM(queries.shape, BF16)], 2 * once,
        away=(0, 1, 2), copies=3)
    sent = [jnp.where(after, kv_own, prev) for after in later]
    got = [prev] + [swap(sent[i], 2 * i) if near(i) else straight[i] for i in range(1, pairs)]
    passed = swap(jnp.stack(sent[:1] + got[1:]), 1)
    kv_even, p_even, acc = kernel(
        attend_even, [((pairs,) + block, BF16), ((pairs, many, rows), BF16), ((many, 2 * HDIM), F32)],
        (facts, q_s, start, level, acc, *got), [], 2 * pairs * once)
    attn_out, k_odd, ds_odd, do_s, do_t, corr, g_passed, p_own, p_even = kernel(
        forward,
        [(queries.shape, BF16), ((pairs, rows, HDIM), BF16), ((pairs, many, rows), BF16),
         (by_row, BF16), (by_lane, BF16), (by_row, F32), ((pairs,) + block, BF16), (p_own.shape, BF16), (p_even.shape, BF16)],
        (facts, q_s, q_t, do_r, start, level, acc, kv_own, kv_even, passed, p_own, p_even),
        [pltpu.VMEM(queries.shape, BF16), pltpu.VMEM((pairs, many, rows), BF16), pltpu.VMEM((many, 2 * HDIM), F32),
         pltpu.VMEM((many // n_ctx, rows), BF16), pltpu.VMEM(block, BF16)],
        5 * pairs * once, aliases=((10, 7), (11, 8)), leaves=(0,), copies=2)
    partner = swap(g_passed, 1).astype(F32)
    shared = (facts, q_t, do_s, do_t, kv_even, p_even, corr)
    ds_even, g_direct = kernel(even, [((pairs - 1, many, rows), BF16), ((pairs - 1,) + block, F32)],
                               shared, [], 3 * (pairs - 1) * once)
    back = lambda route: [(b, a) for a, b in route]
    terms = [partner[0]]
    for i in range(1, pairs):
        summed = (g_direct[i - 1] + partner[i]).astype(BF16)
        terms.append(swap(summed, 2 * i) if near(i) else lax.ppermute(summed, axes, back(straight_route(n_dp, n_ctx, 2 * i))))
    grad_queries, g_own, g_prev = kernel(rest, [(queries.shape, BF16), (block, F32), (block, F32)],
                                         shared + (kv_own, p_own, k_odd, ds_odd, ds_even),
                                         [pltpu.VMEM(by_row, F32)], (n_ctx + 7) * once)
    own_total, prev_total = g_own, g_prev
    for i, term in enumerate(terms):
        term = term.astype(F32)
        own_total = own_total + (jnp.where(later[i], term, 0.0) if near(i) else term)
        if near(i):
            prev_total = prev_total + jnp.where(later[i], 0.0, term)
    last = lax.ppermute(prev_total.astype(BF16), axes, back(run_route(n_dp, n_ctx)))
    grad_keys, grad_values = run(finish, "finish", [(keys.shape, BF16), (values.shape, BF16)], (own_total, last), [], 1)
    return (attn_out, grad_queries, grad_keys, grad_values)


def solution(mesh):
    tokens = P(("dp", "ctx"), None)
    return jax.shard_map(
        shards,
        mesh=mesh,
        in_specs=(tokens, tokens, tokens, tokens, P()),
        out_specs=(tokens, tokens, tokens, tokens),
        check_vma=False,
    )
```

```python
import functools
import math

import jax
import jax.numpy as jnp
from jax import lax
from jax.experimental import pallas as pl
from jax.experimental.pallas import tpu as pltpu
from jax.sharding import PartitionSpec as P

HEADS = 8
HDIM = 128
NEG_FILL = -1e30
SCALE = float(HDIM) ** -0.5
EXP2_SCALE = SCALE * math.log2(math.e)

NT = (((1,), (1,)), ((), ()))
NN = (((1,), (0,)), ((), ()))
F32, BF16 = jnp.float32, jnp.bfloat16


def dot(a, b, dims=NN):
    return lax.dot_general(a, b, dims, preferred_element_type=F32)


def wide(column):
    return jnp.concatenate([column, column], axis=1)


def run_route(n_dp, n_ctx):
    return [(d * n_ctx + c, (d + 1) * n_ctx + c) for d in range(n_dp - 1) for c in range(n_ctx)]


def flip_route(n_dp, n_ctx, flip):
    return [(d * n_ctx + c, d * n_ctx + (c ^ flip)) for d in range(n_dp) for c in range(n_ctx)]


def facts_of(n_ctx, rows, index, lengths_ref):
    base = index * rows
    ends, end = [], jnp.int32(0)
    for i in range(lengths_ref.shape[0]):
        end = end + lengths_ref[i]
        ends.append(end)
    low, high = jnp.int32(0), ends[-1]
    for end in ends:
        low = jnp.where(end <= base, end, low)
    for end in reversed(ends):
        high = jnp.where(end > base, end, high)
    before = lax.div(base - low + rows - 1, rows)
    short = (high - base <= rows - rows // n_ctx).astype(jnp.int32)
    return (lax.rem(index, n_ctx), base, before, short), ends


class Place:
    def __init__(self, n_ctx, rows, facts):
        self.n_ctx, self.rows = n_ctx, rows
        self.ctx, self.base, self.before, short = facts if isinstance(facts, tuple) else (facts[i, 0] for i in range(4))
        self.short = short == 1

    def hop(self, back):
        return lax.div(self.ctx ^ lax.rem(self.ctx - back + 2 * self.n_ctx, self.n_ctx), 2)

    def past(self, backs, body):
        first, step = backs[0], backs.step
        count = jnp.clip(lax.div(self.before - first + step, step), 0, len(backs))
        for short in (True, False):
            many = HEADS * (self.rows - self.rows // self.n_ctx if short else self.rows)
            fits = self.short if short else jnp.logical_not(self.short)

            if len(backs) > 1:

                @pl.when(fits)
                def _():
                    @pl.loop(0, lax.div(count, 2))
                    def _(i):
                        body((first + 2 * i * step, first + (2 * i + 1) * step), many)

            @pl.when(fits & (lax.rem(count, 2) == 1))
            def _():
                body((first + (count - 1) * step,), many)

        return count


def chunks(rows, n_ctx):
    size = rows // n_ctx
    for c in range(n_ctx):
        for h in range(HEADS):
            yield (pl.ds((c * HEADS + h) * size, size), (pl.ds(c * size, size), pl.ds(h * HDIM, HDIM)))


def fetch(pairs, sems):
    copies = [pltpu.make_async_copy(source, target, sems.at[i]) for i, (source, target) in enumerate(pairs)]
    for copy in copies:
        copy.start()
    return copies


def join(keys, values, kv, sems):
    for copy in fetch([(keys, kv.at[:, pl.ds(0, HDIM)]), (values, kv.at[:, pl.ds(HDIM, HDIM)])], sems):
        copy.wait()


def ones_beside(values):
    return jnp.concatenate([values, jnp.ones(values.shape, BF16)], axis=1)


def levels(place, back, many, q_s, key_block, start):
    size, rows = place.rows // place.n_ctx, place.rows
    tokens = many // HEADS
    key = place.base - back * rows + lax.broadcasted_iota(jnp.int32, (tokens, rows), 1)
    query = place.base + lax.broadcasted_iota(jnp.int32, (tokens, rows), 0)
    off = jnp.where((key >= start[:tokens, :]) & (key <= query), 0.0, NEG_FILL)
    s = dot(q_s[:many, :], key_block, NT) * EXP2_SCALE
    s = s.reshape(tokens // size, HEADS, size, rows) + off.reshape(tokens // size, 1, size, rows)
    return s.reshape(many, rows)


def fold(s):
    return jnp.maximum(s[:, :HDIM], s[:, HDIM:])


def row_max(s):
    return jnp.broadcast_to(jnp.max(s, axis=1, keepdims=True), (s.shape[0], HDIM))


def prepare(n_ctx, lengths_hbm, q_hbm, do_hbm, kv_ref, facts_ref, kv_own, q_s, q_t, do_r, start, level, p_own, acc,
            lengths_ref, q_ref, do_ref, sems):
    copies = fetch([(lengths_hbm, lengths_ref), (q_hbm, q_ref), (do_hbm, do_ref)], sems)
    rows = q_ref.shape[0]
    index = lax.axis_index("dp") * n_ctx + lax.axis_index("ctx")
    kv_own[...] = kv_ref[...]
    copies[0].wait()
    facts, ends = facts_of(n_ctx, rows, index, lengths_ref)
    place = Place(n_ctx, rows, facts)
    line = lax.broadcasted_iota(jnp.int32, facts_ref.shape, 0)
    held = jnp.zeros(facts_ref.shape, jnp.int32)
    for i, fact in enumerate(facts):
        held = jnp.where(line == i, fact, held)
    facts_ref[...] = held
    token = place.base + lax.broadcasted_iota(jnp.int32, (rows, HDIM), 0)
    begin = jnp.zeros((rows, HDIM), jnp.int32)
    for end in ends:
        begin = jnp.where(token >= end, end, begin)
    start[...] = wide(begin) if rows == 2 * HDIM else jnp.broadcast_to(begin[:, :1], (rows, rows))
    copies[1].wait()
    for here, there in chunks(rows, n_ctx):
        q_s[here, :] = q_ref[there]
    s = levels(place, 0, HEADS * rows, q_s, kv_own[:, :HDIM], start)
    top = row_max(fold(s))
    level[...] = top
    p = jnp.exp2(s - wide(top)).astype(BF16)
    p_own[...] = p
    acc[...] = dot(p, ones_beside(kv_own[:, HDIM:]))
    copies[2].wait()
    for here, there in chunks(rows, n_ctx):
        do_r[here, :] = do_ref[there]
    for h in range(HEADS):
        here = pl.ds(h * rows, rows)
        q_t[:, here] = q_s[here, :].T


def side_by_side(parts, axis):
    return parts[0] if len(parts) == 1 else jnp.concatenate(parts, axis=axis)


def attend(place, backs, many, q_s, kvs, start, level, acc, probs):
    scores = [levels(place, back, many, q_s, kv[:, :HDIM], start) for back, kv in zip(backs, kvs)]
    p = [jnp.exp2(s - wide(level[:many, :])).astype(BF16) for s in scores]
    for ref, part in zip(probs, p):
        ref[:many, :] = part
    acc[:many, :] += dot(side_by_side(p, 1), side_by_side([ones_beside(kv[:, HDIM:]) for kv in kvs], 0))


def attend_even(n_ctx, facts, q_s, start, level, acc_in, *refs):
    *got, kv_even, p_even, acc = refs
    rows = got[0].shape[0]
    place = Place(n_ctx, rows, facts)
    for i, ref in enumerate(got):
        kv_even[i] = ref[...]
    acc[...] = acc_in[...]

    def body(backs, many):
        attend(place, backs, many, q_s, [kv_even.at[place.hop(back)] for back in backs], start, level, acc,
               [p_even.at[lax.div(back, 2) - 1] for back in backs])

    place.past(range(2, n_ctx + 1, 2), body)


def gradients(many, q_t, do_s, do_t, ps, kvs, corr):
    d = [dot(do_s[:many, :], kv[:, HDIM:], NT) for kv in kvs]
    dv = [dot(do_t[:, :many], p) for p in ps]
    ds = [(p.astype(F32) * (each - wide(corr[:many, :]))).astype(BF16) for p, each in zip(ps, d)]
    dk = [dot(q_t[:, :many], each) for each in ds]
    return [(each, jnp.concatenate([k.T, v.T], axis=1)) for each, k, v in zip(ds, dk, dv)]


def forward(n_ctx, facts, q_s, q_t, do_r, start, level, acc_in, kv_own, kv_even, kv_odd, p_own_in, p_even_in,
            o_hbm, k_odd, ds_odd, do_s, do_t, corr, g_passed, p_own, p_even, o_ref, p_odd, acc, p_new, kv_now, sems):
    rows = o_ref.shape[0]
    size = rows // n_ctx
    place = Place(n_ctx, rows, facts)
    pairs = n_ctx // 2
    everything = HEADS * rows
    odd_backs = range(1, n_ctx, 2)
    del p_own_in, p_even_in

    for i in range(pairs):
        k_odd[i] = kv_odd[i, :, :HDIM]

    def odd(backs):
        return [kv_odd.at[place.hop(back)] for back in backs]

    def attend_odd(backs, many):
        attend(place, backs, many, q_s, odd(backs), start, level, acc, [p_odd.at[lax.div(back, 2)] for back in backs])

    acc[...] = acc_in[...]
    place.past(odd_backs, attend_odd)

    @pl.when(jnp.logical_not(jnp.max(acc[:, HDIM:]) < 2.0 ** 40))
    def _():
        def each(step):
            @pl.loop(0, place.before + 1)
            def _(back):
                at = place.hop(back)

                @pl.when(back == 0)
                def _():
                    kv_now[...] = kv_own[...]

                @pl.when(lax.rem(back, 2) == 1)
                def _():
                    kv_now[...] = kv_odd[at]

                @pl.when((back > 0) & (lax.rem(back, 2) == 0))
                def _():
                    kv_now[...] = kv_even[at]

                half = lax.div(back, 2)
                targets = ((back == 0, p_own), (lax.rem(back, 2) == 1, p_odd.at[half]),
                           ((back > 0) & (lax.rem(back, 2) == 0), p_even.at[jnp.maximum(half - 1, 0)]))

                @pl.loop(0, n_ctx)
                def _(c):
                    here = pl.ds(c * HEADS * size, HEADS * size)
                    tokens = pl.ds(c * size, size)
                    key = place.base - back * rows + lax.broadcasted_iota(jnp.int32, (size, rows), 1)
                    query = place.base + c * size + lax.broadcasted_iota(jnp.int32, (size, rows), 0)
                    off = jnp.where((key >= start[tokens, :]) & (key <= query), 0.0, NEG_FILL)
                    s = dot(q_s[here, :], kv_now[:, :HDIM], NT) * EXP2_SCALE
                    step(here, (s.reshape(HEADS, size, rows) + off[None]).reshape(HEADS * size, rows))

                    if step is replace:
                        for fits, target in targets:

                            @pl.when(fits)
                            def _():
                                copy = pltpu.make_async_copy(p_new, target.at[here], sems.at[0])
                                copy.start()
                                copy.wait()

        def highest(here, s):
            corr[here, :] = jnp.maximum(corr[here, :], row_max(fold(s)))

        def replace(here, s):
            p = jnp.exp2(s - wide(corr[here, :])).astype(BF16)
            p_new[...] = p
            acc[here, :] += dot(p, ones_beside(kv_now[:, HDIM:]))

        @pl.loop(0, n_ctx)
        def _(c):
            here = pl.ds(c * HEADS * size, HEADS * size)
            corr[here, :] = jnp.full((HEADS * size, HDIM), NEG_FILL, F32)
            acc[here, :] = jnp.zeros((HEADS * size, 2 * HDIM), F32)

        each(highest)
        each(replace)

    for i in range(0, everything, rows):
        here = pl.ds(i, rows)
        total = acc[here, :]
        inverse = 1.0 / total[:, HDIM:]
        out = (total[:, :HDIM] * inverse).astype(BF16)
        grad = do_r[here, :].astype(F32)
        corr[here, :] = jnp.sum(grad * out.astype(F32), axis=1, keepdims=True) * inverse
        scaled = grad * inverse
        do_s[here, :] = scaled.astype(BF16)
        do_t[:, here] = scaled.T.astype(BF16)
        for part, there in chunks(rows, n_ctx):
            if i <= part.start < i + rows:
                o_ref[there] = out[part.start - i:part.start - i + size, :]

    leaving = pltpu.make_async_copy(o_ref, o_hbm, sems.at[1])
    leaving.start()

    def backward(backs, many):
        ps = [p_odd[lax.div(back, 2), :many, :] for back in backs]
        for back, (ds, terms) in zip(backs, gradients(many, q_t, do_s, do_t, ps, odd(backs), corr)):
            ds_odd[lax.div(back, 2), :many, :] = ds
            g_passed[place.hop(back)] = terms.astype(BF16)

    done = place.past(odd_backs, backward)

    @pl.loop(done, pairs)
    def _(i):
        g_passed[place.hop(2 * i + 1)] = jnp.zeros((rows, 2 * HDIM), BF16)

    leaving.wait()


def even(n_ctx, facts, q_t, do_s, do_t, kv_even, p_even, corr, ds_even, g_direct):
    rows = kv_even.shape[1]
    place = Place(n_ctx, rows, facts)

    def backward(backs, many):
        ps = [p_even[lax.div(back, 2) - 1, :many, :] for back in backs]
        kvs = [kv_even.at[place.hop(back)] for back in backs]
        for back, (ds, terms) in zip(backs, gradients(many, q_t, do_s, do_t, ps, kvs, corr)):
            ds_even[lax.div(back, 2) - 1, :many, :] = ds
            g_direct[place.hop(back) - 1] = terms

    done = place.past(range(2, n_ctx, 2), backward)

    @pl.loop(done, n_ctx // 2 - 1)
    def _(i):
        g_direct[place.hop(2 * i + 2) - 1] = jnp.zeros((rows, 2 * HDIM), F32)


def rest(n_ctx, facts, q_t, do_s, do_t, kv_even, p_even, corr, kv_own, p_own, k_odd, ds_odd, ds_even,
         dq_ref, g_own, g_prev, dq_acc):
    rows = kv_own.shape[0]
    place = Place(n_ctx, rows, facts)

    (ds, g_own[...]), = gradients(HEADS * rows, q_t, do_s, do_t, [p_own[...]], [kv_own], corr)
    dq_acc[...] = dot(ds, kv_own[:, :HDIM])

    def add(backs, many, ds, kv):
        dq_acc[:many, :] += dot(side_by_side([ds(back)[:many, :] for back in backs], 1),
                                side_by_side([kv[place.hop(back), :, :HDIM] for back in backs], 0))

    def add_odd(backs, many):
        add(backs, many, lambda back: ds_odd.at[lax.div(back, 2)], k_odd)

    def add_even(backs, many):
        add(backs, many, lambda back: ds_even.at[lax.div(back, 2) - 1], kv_even)

    def farthest(backs, many):
        at = place.hop(backs[0])
        (ds, g_prev[...]), = gradients(many, q_t, do_s, do_t, [p_even[n_ctx // 2 - 1, :many, :]], [kv_even.at[at]], corr)
        dq_acc[:many, :] += dot(ds, kv_even[at, :, :HDIM])

    place.past(range(1, n_ctx, 2), add_odd)
    place.past(range(2, n_ctx, 2), add_even)
    g_prev[...] = jnp.zeros(g_prev.shape, F32)
    place.past(range(n_ctx, n_ctx + 1), farthest)

    for here, there in chunks(rows, n_ctx):
        dq_ref[there] = (dq_acc[here, :] * SCALE).astype(BF16)


def finish(total, last, gk_ref, gv_ref):
    terms = total[...] + last[...].astype(F32)
    gk_ref[...] = (terms[:, :HDIM] * SCALE).astype(BF16)
    gv_ref[...] = terms[:, HDIM:].astype(BF16)


def size_of(arrays):
    return sum(math.prod(array.shape) * jnp.dtype(array.dtype).itemsize for array in arrays)


def call(body, name, outs, args, scratch, flops, resident, aliases=(), away=(), leaves=(), copies=0):
    vmem = pl.BlockSpec(memory_space=pltpu.VMEM)
    anywhere = pl.BlockSpec(memory_space=pl.ANY)
    hbm = pl.BlockSpec(memory_space=pltpu.HBM)
    outs = tuple(jax.ShapeDtypeStruct(shape, dtype) for shape, dtype in outs)
    held = size_of(scratch) + 8 * 2**20
    if not resident:
        held = min(held + size_of(outs) + size_of(args), 62 * 2**20)
    in_specs, out_specs = [vmem] * len(args), [vmem] * len(outs)
    for i in away:
        in_specs[i] = hbm
    for o in leaves:
        out_specs[o] = hbm
    for i, o in aliases:
        in_specs[i] = out_specs[o] = anywhere
    return pl.pallas_call(
        body,
        out_shape=outs,
        in_specs=in_specs,
        out_specs=tuple(out_specs),
        scratch_shapes=scratch + [pltpu.SemaphoreType.DMA((copies,))] * (copies > 0),
        input_output_aliases=dict(aliases),
        compiler_params=pltpu.CompilerParams(vmem_limit_bytes=held),
        cost_estimate=pl.CostEstimate(flops=flops, bytes_accessed=2**20, transcendentals=0),
        name=name,
    )(*(pltpu.with_memory_space_constraint(arg, pltpu.HBM) if i in away else arg for i, arg in enumerate(args)))


def shards(queries, keys, values, grad_out, lengths):
    rows = keys.shape[0]
    n_dp, n_ctx = lax.axis_size("dp"), lax.axis_size("ctx")
    axes = ("dp", "ctx")
    pairs = n_ctx // 2
    ctx = lax.axis_index("ctx")
    many = HEADS * rows
    once = 2 * many * rows * HDIM
    by_row, by_lane = (many, HDIM), (HDIM, many)
    block = (rows, 2 * HDIM)
    run = functools.partial(call, resident=(n_ctx + 1) * many * rows <= 6 * 2**20)
    def kernel(body, *args, **kwargs):
        return run(functools.partial(body, n_ctx), body.__name__, *args, **kwargs)

    def swap(blocks, flip):
        return lax.ppermute(blocks, axes, flip_route(n_dp, n_ctx, flip))

    later = [ctx < ctx ^ max(2 * i, 1) for i in range(pairs)]

    kv, = run(join, "join", [(block, BF16)], (keys, values), [], 1, away=(0, 1), copies=2)
    prev = lax.ppermute(kv, axes, run_route(n_dp, n_ctx))
    facts, kv_own, q_s, q_t, do_r, start, level, p_own, acc = kernel(
        prepare, [((8, HDIM), jnp.int32), (block, BF16), (by_row, BF16), (by_lane, BF16), (by_row, BF16),
                  ((rows, rows), jnp.int32), (by_row, F32), ((many, rows), BF16), ((many, 2 * HDIM), F32)],
        (lengths, queries, grad_out, kv),
        [pltpu.SMEM(lengths.shape, jnp.int32), pltpu.VMEM(queries.shape, BF16), pltpu.VMEM(queries.shape, BF16)], 2 * once,
        away=(0, 1, 2), copies=3)
    sent = [jnp.where(after, kv_own, prev) for after in later]
    got = [prev] + [swap(sent[i], 2 * i) for i in range(1, pairs)]
    passed = swap(jnp.stack(sent[:1] + got[1:]), 1)
    kv_even, p_even, acc = kernel(
        attend_even, [((pairs,) + block, BF16), ((pairs, many, rows), BF16), ((many, 2 * HDIM), F32)],
        (facts, q_s, start, level, acc, *got), [], 2 * pairs * once)
    attn_out, k_odd, ds_odd, do_s, do_t, corr, g_passed, p_own, p_even = kernel(
        forward,
        [(queries.shape, BF16), ((pairs, rows, HDIM), BF16), ((pairs, many, rows), BF16),
         (by_row, BF16), (by_lane, BF16), (by_row, F32), ((pairs,) + block, BF16), (p_own.shape, BF16), (p_even.shape, BF16)],
        (facts, q_s, q_t, do_r, start, level, acc, kv_own, kv_even, passed, p_own, p_even),
        [pltpu.VMEM(queries.shape, BF16), pltpu.VMEM((pairs, many, rows), BF16), pltpu.VMEM((many, 2 * HDIM), F32),
         pltpu.VMEM((many // n_ctx, rows), BF16), pltpu.VMEM(block, BF16)],
        5 * pairs * once, aliases=((10, 7), (11, 8)), leaves=(0,), copies=2)
    partner = swap(g_passed, 1).astype(F32)
    shared = (facts, q_t, do_s, do_t, kv_even, p_even, corr)
    ds_even, g_direct = kernel(even, [((pairs - 1, many, rows), BF16), ((pairs - 1,) + block, F32)],
                               shared, [], 3 * (pairs - 1) * once)
    terms = [partner[0]] + [swap((g_direct[i - 1] + partner[i]).astype(BF16), 2 * i).astype(F32) for i in range(1, pairs)]
    grad_queries, g_own, g_prev = kernel(rest, [(queries.shape, BF16), (block, F32), (block, F32)],
                                         shared + (kv_own, p_own, k_odd, ds_odd, ds_even),
                                         [pltpu.VMEM(by_row, F32)], (n_ctx + 7) * once)
    own_total, prev_total = g_own, g_prev
    for after, term in zip(later, terms):
        own_total = own_total + jnp.where(after, term, 0.0)
        prev_total = prev_total + jnp.where(after, 0.0, term)
    back = [(b, a) for a, b in run_route(n_dp, n_ctx)]
    last = lax.ppermute(prev_total.astype(BF16), axes, back)
    grad_keys, grad_values = run(finish, "finish", [(keys.shape, BF16), (values.shape, BF16)], (own_total, last), [], 1)
    return (attn_out, grad_queries, grad_keys, grad_values)


def solution(mesh):
    tokens = P(("dp", "ctx"), None)
    return jax.shard_map(
        shards,
        mesh=mesh,
        in_specs=(tokens, tokens, tokens, tokens, P()),
        out_specs=(tokens, tokens, tokens, tokens),
        check_vma=False,
    )
```

```python
import functools
import math

import jax
import jax.numpy as jnp
from jax import lax
from jax.experimental import pallas as pl
from jax.experimental.pallas import tpu as pltpu
from jax.sharding import PartitionSpec as P

HEADS = 8
HDIM = 128
NEG_FILL = -1e30
SCALE = float(HDIM) ** -0.5
EXP2_SCALE = SCALE * math.log2(math.e)

NT = (((1,), (1,)), ((), ()))
NN = (((1,), (0,)), ((), ()))
F32, BF16 = jnp.float32, jnp.bfloat16


def dot(a, b, dims=NN):
    return lax.dot_general(a, b, dims, preferred_element_type=F32)


def wide(column):
    return jnp.concatenate([column, column], axis=1)


def run_route(n_dp, n_ctx):
    return [(d * n_ctx + c, (d + 1) * n_ctx + c) for d in range(n_dp - 1) for c in range(n_ctx)]


def flip_route(n_dp, n_ctx, flip):
    return [(d * n_ctx + c, d * n_ctx + (c ^ flip)) for d in range(n_dp) for c in range(n_ctx)]


def facts_of(n_ctx, rows, index, lengths_ref):
    base = index * rows
    ends, end = [], jnp.int32(0)
    for i in range(lengths_ref.shape[0]):
        end = end + lengths_ref[i]
        ends.append(end)
    low, high = jnp.int32(0), ends[-1]
    for end in ends:
        low = jnp.where(end <= base, end, low)
    for end in reversed(ends):
        high = jnp.where(end > base, end, high)
    before = lax.div(base - low + rows - 1, rows)
    short = (high - base <= rows - rows // n_ctx).astype(jnp.int32)
    return (lax.rem(index, n_ctx), base, before, short), ends


class Place:
    def __init__(self, n_ctx, rows, facts):
        self.n_ctx, self.rows = n_ctx, rows
        self.ctx, self.base, self.before, short = facts if isinstance(facts, tuple) else (facts[i, 0] for i in range(4))
        self.short = short == 1

    def hop(self, back):
        return lax.div(self.ctx ^ lax.rem(self.ctx - back + 2 * self.n_ctx, self.n_ctx), 2)

    def those(self, flips, body):
        backs = [lax.rem(self.ctx - (self.ctx ^ flip) + self.n_ctx, self.n_ctx) for flip in flips]
        needed = [(back <= self.before).astype(jnp.int32) for back in backs]
        count = sum(needed)

        def pick(k):
            at, back, seen = jnp.int32(0), jnp.int32(0), jnp.int32(0)
            for i in range(len(flips)):
                here = (needed[i] == 1) & (seen == k)
                at, back = jnp.where(here, i, at), jnp.where(here, backs[i], back)
                seen = seen + needed[i]
            return at, back

        for short in (True, False):
            many = HEADS * (self.rows - self.rows // self.n_ctx if short else self.rows)
            fits = self.short if short else jnp.logical_not(self.short)

            if len(flips) > 1:

                @pl.when(fits)
                def _():
                    @pl.loop(0, lax.div(count, 2))
                    def _(i):
                        body(*zip(pick(2 * i), pick(2 * i + 1)), many)

            @pl.when(fits & (lax.rem(count, 2) == 1))
            def _():
                body(*zip(pick(count - 1)), many)

        return needed

    def past(self, backs, body):
        first, step = backs[0], backs.step
        count = jnp.clip(lax.div(self.before - first + step, step), 0, len(backs))
        for short in (True, False):
            many = HEADS * (self.rows - self.rows // self.n_ctx if short else self.rows)
            fits = self.short if short else jnp.logical_not(self.short)

            if len(backs) > 1:

                @pl.when(fits)
                def _():
                    @pl.loop(0, lax.div(count, 2))
                    def _(i):
                        body((first + 2 * i * step, first + (2 * i + 1) * step), many)

            @pl.when(fits & (lax.rem(count, 2) == 1))
            def _():
                body((first + (count - 1) * step,), many)

        return count


def chunks(rows, n_ctx):
    size = rows // n_ctx
    for c in range(n_ctx):
        for h in range(HEADS):
            yield (pl.ds((c * HEADS + h) * size, size), (pl.ds(c * size, size), pl.ds(h * HDIM, HDIM)))


def fetch(pairs, sems):
    copies = [pltpu.make_async_copy(source, target, sems.at[i]) for i, (source, target) in enumerate(pairs)]
    for copy in copies:
        copy.start()
    return copies


def join(keys, values, kv, sems):
    for copy in fetch([(keys, kv.at[:, pl.ds(0, HDIM)]), (values, kv.at[:, pl.ds(HDIM, HDIM)])], sems):
        copy.wait()


def ones_beside(values):
    return jnp.concatenate([values, jnp.ones(values.shape, BF16)], axis=1)


def levels(place, back, many, q_s, key_block, start):
    size, rows = place.rows // place.n_ctx, place.rows
    tokens = many // HEADS
    key = place.base - back * rows + lax.broadcasted_iota(jnp.int32, (tokens, rows), 1)
    query = place.base + lax.broadcasted_iota(jnp.int32, (tokens, rows), 0)
    off = jnp.where((key >= start[:tokens, :]) & (key <= query), 0.0, NEG_FILL)
    s = dot(q_s[:many, :], key_block, NT) * EXP2_SCALE
    s = s.reshape(tokens // size, HEADS, size, rows) + off.reshape(tokens // size, 1, size, rows)
    return s.reshape(many, rows)


def fold(s):
    return jnp.maximum(s[:, :HDIM], s[:, HDIM:])


def row_max(s):
    return jnp.broadcast_to(jnp.max(s, axis=1, keepdims=True), (s.shape[0], HDIM))


def prepare(n_ctx, lengths_hbm, q_hbm, do_hbm, kv_ref, facts_ref, kv_own, q_s, q_t, do_r, start, level, p_own, acc,
            lengths_ref, q_ref, do_ref, sems):
    copies = fetch([(lengths_hbm, lengths_ref), (q_hbm, q_ref), (do_hbm, do_ref)], sems)
    rows = q_ref.shape[0]
    index = lax.axis_index("dp") * n_ctx + lax.axis_index("ctx")
    kv_own[...] = kv_ref[...]
    copies[0].wait()
    facts, ends = facts_of(n_ctx, rows, index, lengths_ref)
    place = Place(n_ctx, rows, facts)
    line = lax.broadcasted_iota(jnp.int32, facts_ref.shape, 0)
    held = jnp.zeros(facts_ref.shape, jnp.int32)
    for i, fact in enumerate(facts):
        held = jnp.where(line == i, fact, held)
    facts_ref[...] = held
    token = place.base + lax.broadcasted_iota(jnp.int32, (rows, HDIM), 0)
    begin = jnp.zeros((rows, HDIM), jnp.int32)
    for end in ends:
        begin = jnp.where(token >= end, end, begin)
    start[...] = wide(begin) if rows == 2 * HDIM else jnp.broadcast_to(begin[:, :1], (rows, rows))
    copies[1].wait()
    for here, there in chunks(rows, n_ctx):
        q_s[here, :] = q_ref[there]
    s = levels(place, 0, HEADS * rows, q_s, kv_own[:, :HDIM], start)
    top = row_max(fold(s))
    level[...] = top
    p = jnp.exp2(s - wide(top)).astype(BF16)
    p_own[...] = p
    acc[...] = dot(p, ones_beside(kv_own[:, HDIM:]))
    copies[2].wait()
    for here, there in chunks(rows, n_ctx):
        do_r[here, :] = do_ref[there]
    for h in range(HEADS):
        here = pl.ds(h * rows, rows)
        q_t[:, here] = q_s[here, :].T


def side_by_side(parts, axis):
    return parts[0] if len(parts) == 1 else jnp.concatenate(parts, axis=axis)


def attend(place, backs, many, q_s, kvs, start, level, acc, probs):
    scores = [levels(place, back, many, q_s, kv[:, :HDIM], start) for back, kv in zip(backs, kvs)]
    p = [jnp.exp2(s - wide(level[:many, :])).astype(BF16) for s in scores]
    for ref, part in zip(probs, p):
        ref[:many, :] = part
    acc[:many, :] += dot(side_by_side(p, 1), side_by_side([ones_beside(kv[:, HDIM:]) for kv in kvs], 0))


def attend_even(n_ctx, facts, q_s, start, level, acc_in, *refs):
    *got, kv_even, p_even, acc = refs
    rows = got[0].shape[0]
    place = Place(n_ctx, rows, facts)
    for i, ref in enumerate(got):
        kv_even[i] = ref[...]
    acc[...] = acc_in[...]

    def body(backs, many):
        attend(place, backs, many, q_s, [kv_even.at[place.hop(back)] for back in backs], start, level, acc,
               [p_even.at[lax.div(back, 2) - 1] for back in backs])

    place.past(range(2, n_ctx + 1, 2), body)


def gradients(many, q_t, do_s, do_t, ps, kvs, corr):
    d = [dot(do_s[:many, :], kv[:, HDIM:], NT) for kv in kvs]
    dv = [dot(do_t[:, :many], p) for p in ps]
    ds = [(p.astype(F32) * (each - wide(corr[:many, :]))).astype(BF16) for p, each in zip(ps, d)]
    dk = [dot(q_t[:, :many], each) for each in ds]
    return [(each, jnp.concatenate([k.T, v.T], axis=1)) for each, k, v in zip(ds, dk, dv)]


def forward(n_ctx, facts, q_s, q_t, do_r, start, level, acc_in, kv_own, kv_even, kv_odd, p_own_in, p_even_in,
            o_hbm, k_odd, ds_odd, do_s, do_t, corr, g_passed, p_own, p_even, o_ref, p_odd, acc, p_new, kv_now, sems):
    rows = o_ref.shape[0]
    size = rows // n_ctx
    place = Place(n_ctx, rows, facts)
    pairs = n_ctx // 2
    everything = HEADS * rows
    odd_backs = range(1, n_ctx, 2)
    del p_own_in, p_even_in

    for i in range(pairs):
        k_odd[i] = kv_odd[i, :, :HDIM]

    def odd(backs):
        return [kv_odd.at[place.hop(back)] for back in backs]

    def attend_odd(backs, many):
        attend(place, backs, many, q_s, odd(backs), start, level, acc, [p_odd.at[lax.div(back, 2)] for back in backs])

    acc[...] = acc_in[...]
    place.past(odd_backs, attend_odd)

    @pl.when(jnp.logical_not(jnp.max(acc[:, HDIM:]) < 2.0 ** 40))
    def _():
        def each(step):
            @pl.loop(0, place.before + 1)
            def _(back):
                at = place.hop(back)

                @pl.when(back == 0)
                def _():
                    kv_now[...] = kv_own[...]

                @pl.when(lax.rem(back, 2) == 1)
                def _():
                    kv_now[...] = kv_odd[at]

                @pl.when((back > 0) & (lax.rem(back, 2) == 0))
                def _():
                    kv_now[...] = kv_even[at]

                half = lax.div(back, 2)
                targets = ((back == 0, p_own), (lax.rem(back, 2) == 1, p_odd.at[half]),
                           ((back > 0) & (lax.rem(back, 2) == 0), p_even.at[jnp.maximum(half - 1, 0)]))

                @pl.loop(0, n_ctx)
                def _(c):
                    here = pl.ds(c * HEADS * size, HEADS * size)
                    tokens = pl.ds(c * size, size)
                    key = place.base - back * rows + lax.broadcasted_iota(jnp.int32, (size, rows), 1)
                    query = place.base + c * size + lax.broadcasted_iota(jnp.int32, (size, rows), 0)
                    off = jnp.where((key >= start[tokens, :]) & (key <= query), 0.0, NEG_FILL)
                    s = dot(q_s[here, :], kv_now[:, :HDIM], NT) * EXP2_SCALE
                    step(here, (s.reshape(HEADS, size, rows) + off[None]).reshape(HEADS * size, rows))

                    if step is replace:
                        for fits, target in targets:

                            @pl.when(fits)
                            def _():
                                copy = pltpu.make_async_copy(p_new, target.at[here], sems.at[0])
                                copy.start()
                                copy.wait()

        def highest(here, s):
            corr[here, :] = jnp.maximum(corr[here, :], row_max(fold(s)))

        def replace(here, s):
            p = jnp.exp2(s - wide(corr[here, :])).astype(BF16)
            p_new[...] = p
            acc[here, :] += dot(p, ones_beside(kv_now[:, HDIM:]))

        @pl.loop(0, n_ctx)
        def _(c):
            here = pl.ds(c * HEADS * size, HEADS * size)
            corr[here, :] = jnp.full((HEADS * size, HDIM), NEG_FILL, F32)
            acc[here, :] = jnp.zeros((HEADS * size, 2 * HDIM), F32)

        each(highest)
        each(replace)

    for i in range(0, everything, rows):
        here = pl.ds(i, rows)
        total = acc[here, :]
        inverse = 1.0 / total[:, HDIM:]
        out = (total[:, :HDIM] * inverse).astype(BF16)
        grad = do_r[here, :].astype(F32)
        corr[here, :] = jnp.sum(grad * out.astype(F32), axis=1, keepdims=True) * inverse
        scaled = grad * inverse
        do_s[here, :] = scaled.astype(BF16)
        do_t[:, here] = scaled.T.astype(BF16)
        for part, there in chunks(rows, n_ctx):
            if i <= part.start < i + rows:
                o_ref[there] = out[part.start - i:part.start - i + size, :]

    leaving = pltpu.make_async_copy(o_ref, o_hbm, sems.at[1])
    leaving.start()

    def backward(backs, many):
        ps = [p_odd[lax.div(back, 2), :many, :] for back in backs]
        for back, (ds, terms) in zip(backs, gradients(many, q_t, do_s, do_t, ps, odd(backs), corr)):
            ds_odd[lax.div(back, 2), :many, :] = ds
            g_passed[place.hop(back)] = terms.astype(BF16)

    done = place.past(odd_backs, backward)

    @pl.loop(done, pairs)
    def _(i):
        g_passed[place.hop(2 * i + 1)] = jnp.zeros((rows, 2 * HDIM), BF16)

    leaving.wait()


def even(n_ctx, flips, facts, q_t, do_s, do_t, kv_even, p_even, corr, *refs):
    *_, ds_even, g_even, facts_out = refs
    rows = kv_even.shape[1]
    place = Place(n_ctx, rows, facts)
    facts_out[...] = facts[...]

    def backward(at, backs, many):
        ps = [p_even[lax.div(back, 2) - 1, :many, :] for back in backs]
        kvs = [kv_even.at[place.hop(back)] for back in backs]
        for i, (ds, terms) in zip(at, gradients(many, q_t, do_s, do_t, ps, kvs, corr)):
            ds_even[i, :many, :] = ds
            g_even[i] = terms

    for i, needed in enumerate(place.those(flips, backward)):

        @pl.when(needed == 0)
        def _():
            g_even[i] = jnp.zeros((rows, 2 * HDIM), F32)


def ends(n_ctx, facts, q_t, do_s, do_t, kv_even, p_even, corr, kv_own, p_own, g_own, g_prev, ds_own, ds_prev):
    place = Place(n_ctx, kv_own.shape[0], facts)
    (ds_own[...], g_own[...]), = gradients(p_own.shape[0], q_t, do_s, do_t, [p_own[...]], [kv_own], corr)

    def farthest(backs, many):
        at = place.hop(backs[0])
        (ds_prev[:many, :], g_prev[...]), = gradients(many, q_t, do_s, do_t, [p_even[n_ctx // 2 - 1, :many, :]], [kv_even.at[at]], corr)

    g_prev[...] = jnp.zeros(g_prev.shape, F32)
    place.past(range(n_ctx, n_ctx + 1), farthest)


def query_gradients(n_ctx, groups, facts, kv_own, kv_even, k_odd, ds_own, ds_prev, ds_odd, *refs):
    *ds_even, _, dq_ref, dq_acc = refs
    place = Place(n_ctx, kv_own.shape[0], facts)
    dq_acc[...] = dot(ds_own[...], kv_own[:, :HDIM])

    def add(backs, many, ds, kv):
        dq_acc[:many, :] += dot(side_by_side([each[:many, :] for each in ds], 1),
                                side_by_side([kv[place.hop(back), :, :HDIM] for back in backs], 0))

    place.past(range(1, n_ctx, 2), lambda backs, many: add(backs, many, [ds_odd.at[lax.div(back, 2)] for back in backs], k_odd))
    for flips, ds in zip(groups, ds_even):
        place.those(flips, lambda at, backs, many: add(backs, many, [ds.at[i] for i in at], kv_even))
    place.past(range(n_ctx, n_ctx + 1), lambda backs, many: add(backs, many, [ds_prev], kv_even))
    for here, there in chunks(kv_own.shape[0], n_ctx):
        dq_ref[there] = (dq_acc[here, :] * SCALE).astype(BF16)


def finish(total, last, gk_ref, gv_ref):
    terms = total[...] + last[...].astype(F32)
    gk_ref[...] = (terms[:, :HDIM] * SCALE).astype(BF16)
    gv_ref[...] = terms[:, HDIM:].astype(BF16)


def size_of(arrays):
    return sum(math.prod(array.shape) * jnp.dtype(array.dtype).itemsize for array in arrays)


def call(body, name, outs, args, scratch, flops, resident, aliases=(), away=(), leaves=(), copies=0):
    vmem = pl.BlockSpec(memory_space=pltpu.VMEM)
    anywhere = pl.BlockSpec(memory_space=pl.ANY)
    hbm = pl.BlockSpec(memory_space=pltpu.HBM)
    outs = tuple(jax.ShapeDtypeStruct(shape, dtype) for shape, dtype in outs)
    held = size_of(scratch) + 8 * 2**20
    if not resident:
        held = min(held + size_of(outs) + size_of(args), 62 * 2**20)
    in_specs, out_specs = [vmem] * len(args), [vmem] * len(outs)
    for i in away:
        in_specs[i] = hbm
    for o in leaves:
        out_specs[o] = hbm
    for i, o in aliases:
        in_specs[i] = out_specs[o] = anywhere
    return pl.pallas_call(
        body,
        out_shape=outs,
        in_specs=in_specs,
        out_specs=tuple(out_specs),
        scratch_shapes=scratch + [pltpu.SemaphoreType.DMA((copies,))] * (copies > 0),
        input_output_aliases=dict(aliases),
        compiler_params=pltpu.CompilerParams(vmem_limit_bytes=held),
        cost_estimate=pl.CostEstimate(flops=flops, bytes_accessed=2**20, transcendentals=0),
        name=name,
    )(*(pltpu.with_memory_space_constraint(arg, pltpu.HBM) if i in away else arg for i, arg in enumerate(args)))


def shards(queries, keys, values, grad_out, lengths):
    rows = keys.shape[0]
    n_dp, n_ctx = lax.axis_size("dp"), lax.axis_size("ctx")
    axes = ("dp", "ctx")
    pairs = n_ctx // 2
    ctx = lax.axis_index("ctx")
    many = HEADS * rows
    once = 2 * many * rows * HDIM
    by_row, by_lane = (many, HDIM), (HDIM, many)
    block = (rows, 2 * HDIM)
    run = functools.partial(call, resident=(n_ctx + 1) * many * rows <= 6 * 2**20)
    def kernel(body, *args, **kwargs):
        return run(functools.partial(body, n_ctx), body.__name__, *args, **kwargs)

    def swap(blocks, flip):
        return lax.ppermute(blocks, axes, flip_route(n_dp, n_ctx, flip))

    later = [ctx < ctx ^ max(2 * i, 1) for i in range(pairs)]

    kv, = run(join, "join", [(block, BF16)], (keys, values), [], 1, away=(0, 1), copies=2)
    prev = lax.ppermute(kv, axes, run_route(n_dp, n_ctx))
    facts, kv_own, q_s, q_t, do_r, start, level, p_own, acc = kernel(
        prepare, [((8, HDIM), jnp.int32), (block, BF16), (by_row, BF16), (by_lane, BF16), (by_row, BF16),
                  ((rows, rows), jnp.int32), (by_row, F32), ((many, rows), BF16), ((many, 2 * HDIM), F32)],
        (lengths, queries, grad_out, kv),
        [pltpu.SMEM(lengths.shape, jnp.int32), pltpu.VMEM(queries.shape, BF16), pltpu.VMEM(queries.shape, BF16)], 2 * once,
        away=(0, 1, 2), copies=3)
    sent = [jnp.where(after, kv_own, prev) for after in later]
    got = [prev] + [swap(sent[i], 2 * i) for i in range(1, pairs)]
    passed = swap(jnp.stack(sent[:1] + got[1:]), 1)
    kv_even, p_even, acc = kernel(
        attend_even, [((pairs,) + block, BF16), ((pairs, many, rows), BF16), ((many, 2 * HDIM), F32)],
        (facts, q_s, start, level, acc, *got), [], 2 * pairs * once)
    attn_out, k_odd, ds_odd, do_s, do_t, corr, g_passed, p_own, p_even = kernel(
        forward,
        [(queries.shape, BF16), ((pairs, rows, HDIM), BF16), ((pairs, many, rows), BF16),
         (by_row, BF16), (by_lane, BF16), (by_row, F32), ((pairs,) + block, BF16), (p_own.shape, BF16), (p_even.shape, BF16)],
        (facts, q_s, q_t, do_r, start, level, acc, kv_own, kv_even, passed, p_own, p_even),
        [pltpu.VMEM(queries.shape, BF16), pltpu.VMEM((pairs, many, rows), BF16), pltpu.VMEM((many, 2 * HDIM), F32),
         pltpu.VMEM((many // n_ctx, rows), BF16), pltpu.VMEM(block, BF16)],
        5 * pairs * once, aliases=((10, 7), (11, 8)), leaves=(0,), copies=2)
    partner = swap(g_passed, 1).astype(F32)
    shared = (q_t, do_s, do_t, kv_even, p_even, corr)
    near = [2 * i for i in range(1, pairs) if i & (i - 1) == 0]
    far = [2 * i for i in range(1, pairs) if i & (i - 1) != 0]

    def evens(flips, facts, *extra):
        return run(functools.partial(even, n_ctx, flips), "even",
                   [((len(flips), many, rows), BF16), ((len(flips),) + block, F32), (facts.shape, jnp.int32)],
                   (facts,) + shared + extra, [], 3 * len(flips) * once)

    ds_far, g_far, facts = evens(far, facts)
    terms = [(0, partner[0])]
    summed = [(g_far[i] + partner[flip // 2]).astype(BF16) for i, flip in enumerate(far)]
    for flip, terms_far in zip(far, summed):
        terms.append((flip, swap(terms_far, flip).astype(F32)))
    ds_near, g_near, facts = evens(near, facts, *summed)
    for i, flip in enumerate(near):
        terms.append((flip, swap((g_near[i] + partner[flip // 2]).astype(BF16), flip).astype(F32)))
    g_own, g_prev, ds_own, ds_prev = kernel(
        ends, [(block, F32), (block, F32), ((many, rows), BF16), ((many, rows), BF16)],
        (facts,) + shared + (kv_own, p_own), [], 6 * once)
    own_total, prev_total = g_own, g_prev
    for flip, term in terms:
        after = later[flip // 2]
        own_total = own_total + jnp.where(after, term, 0.0)
        prev_total = prev_total + jnp.where(after, 0.0, term)
    back = [(b, a) for a, b in run_route(n_dp, n_ctx)]
    last = lax.ppermute(prev_total.astype(BF16), axes, back)
    grad_queries, = run(functools.partial(query_gradients, n_ctx, (near, far)), "query_gradients", [(queries.shape, BF16)],
                        (facts, kv_own, kv_even, k_odd, ds_own, ds_prev, ds_odd, ds_near, ds_far, own_total),
                        [pltpu.VMEM(by_row, F32)], (n_ctx + 1) * once)
    grad_keys, grad_values = run(finish, "finish", [(keys.shape, BF16), (values.shape, BF16)], (own_total, last), [], 1)
    return (attn_out, grad_queries, grad_keys, grad_values)


def solution(mesh):
    tokens = P(("dp", "ctx"), None)
    return jax.shard_map(
        shards,
        mesh=mesh,
        in_specs=(tokens, tokens, tokens, tokens, P()),
        out_specs=(tokens, tokens, tokens, tokens),
        check_vma=False,
    )
```
